32 devices in a mesh: fsdp: 4 (over z), ctx: 4 (over x, core), tp: 2 (over y).
Axes of the slice: x: 2, y: 2, z: 4, core: 2. Of those that a mesh axis runs over, the one named last changes fastest.
Arguments:
- tokens: bfloat16 [8192, 1024], P(('fsdp', 'ctx', 'tp')), may hold values from -6 to 6
- cotangent: bfloat16 [8192, 1024], P(('fsdp', 'ctx', 'tp')), may hold values from -6 to 6
- lengths: int32 [4, 12], P('fsdp'), may hold values from 1 to 455, as said below
- dealing: int32 [4, 12], P('fsdp'), may hold values from 0 to 11, as said below
- norm_in: bfloat16 [1024], P('fsdp'), may hold values from 0.5 to 1.5
- w_query: bfloat16 [1024, 512], P('fsdp', 'tp'), may hold values from -0.1875 to 0.1875
- w_keyval: bfloat16 [1024, 2, 128], P('fsdp', 'tp'), may hold values from -0.1875 to 0.1875
- w_attn_out: bfloat16 [512, 1024], P('tp', 'fsdp'), may hold values from -1 to 1
- w_zx: bfloat16 [1024, 2, 1536], P('fsdp', None, 'tp'), may hold values from -0.1875 to 0.1875
- w_bc: bfloat16 [1024, 256], P('fsdp'), may hold values from -0.1875 to 0.1875
- w_step: bfloat16 [1024, 24], P('fsdp', 'tp'), may hold values from -0.1875 to 0.1875
- head_params: float32 [3, 24], P(None, 'tp'), may hold values from -7 to 2.8, as said below
- taps_x: bfloat16 [5, 24, 64], P(None, 'tp', 'fsdp'), may hold values from -0.5 to 0.5
- taps_bc: bfloat16 [5, 256], P(None, 'fsdp'), may hold values from -0.5 to 0.5
- gain_mamba: bfloat16 [24, 64], P('tp', 'fsdp'), may hold values from 0.5 to 1.5
- w_mamba_out: bfloat16 [1536, 1024], P('tp', 'fsdp'), may hold values from -0.15625 to 0.15625
- norm_mid: bfloat16 [1024], P('fsdp'), may hold values from 0.5 to 1.5
- w_gate_up: bfloat16 [1024, 2, 2048], P('fsdp', None, 'tp'), may hold values from -0.1875 to 0.1875
- w_down: bfloat16 [2048, 1024], P('tp', 'fsdp'), may hold values from -0.125 to 0.125
Outputs:
- mixed: bfloat16 [8192, 1024], P(('fsdp', 'ctx', 'tp'))
- grad_tokens: bfloat16 [8192, 1024], P(('fsdp', 'ctx', 'tp'))
- grad_norm_in: float32 [1024], P('fsdp')
- grad_query: float32 [1024, 512], P('fsdp', 'tp')
- grad_keyval: float32 [1024, 2, 128], P('fsdp', 'tp')
- grad_attn_out: float32 [512, 1024], P('tp', 'fsdp')
- grad_zx: float32 [1024, 2, 1536], P('fsdp', None, 'tp')
- grad_bc: float32 [1024, 256], P('fsdp')
- grad_step: float32 [1024, 24], P('fsdp', 'tp')
- grad_heads: float32 [3, 24], P(None, 'tp')
- grad_taps_x: float32 [5, 24, 64], P(None, 'tp', 'fsdp')
- grad_taps_bc: float32 [5, 256], P(None, 'fsdp')
- grad_gain: float32 [24, 64], P('tp', 'fsdp')
- grad_mamba_out: float32 [1536, 1024], P('tp', 'fsdp')
- grad_norm_mid: float32 [1024], P('fsdp')
- grad_gate_up: float32 [1024, 2, 2048], P('fsdp', None, 'tp')
- grad_down: float32 [2048, 1024], P('tp', 'fsdp')
The draws below stay inside these ranges and needn't reach their ends.
Inputs may be any that keep to these rules, and one draw needn't show every extreme that they name: Each group's lengths sum to 2048; the largest is exactly 455 in every draw. `dealing`: each row is a permutation of the group's sequences; laid end to end in the dealt order, each run of 3 sequences holds exactly 512 tokens. `head_params`: row 0 holds step biases, row 1 logarithms of decay rates, row 2 skip factors.
All inputs are finite; a program needn't handle non-finite values.
Results may differ from the reference program's by a relative error of at most 0.02.
Values may be sent and summed in bfloat16 or wider, within the bound.
No kernel may reach another device: no remote copies, remote signals or barrier semaphores. Data moves between devices by JAX's collectives and lax.ppermute only.
A program may use at most 192 MiB of HBM per device.

```python
import jax
import jax.numpy as jnp
from jax import lax

D = 1024
HQ = 8
KVH = 2
HD = 64
MH = 24
NS = 128
KC = 4
FF = 2048
BLK = 128
SEQ_RANK = 3
TOK_RANK = 512
G_TOK = 2048
TOKENS = 8192
SEQ_G = 12
LONGEST = 455
DI = 1536
N_FSDP = 4
N_CTX = 4


def plan_sequences(key):
    base = jax.random.fold_in(key, 17)
    key_long, key_split, key_pick, key_order, key_given = jax.random.split(base, 5)
    spare = TOK_RANK - LONGEST
    firsts = jax.random.randint(key_long, (N_FSDP, N_CTX), spare, LONGEST + 1)
    chosen = jax.random.randint(key_pick, (N_FSDP, 1), 0, N_CTX)
    firsts = jnp.where(jnp.arange(N_CTX)[None, :] == chosen, LONGEST, firsts)
    remains = TOK_RANK - firsts
    seconds = jax.random.randint(key_split, (N_FSDP, N_CTX), 1, remains)
    thirds = remains - seconds
    pieces = jnp.stack([firsts, seconds, thirds], axis=2)
    orders = jax.random.randint(key_order, (N_FSDP, N_CTX, SEQ_RANK), 0, 1 << 20) * SEQ_RANK + jnp.arange(SEQ_RANK)[None, None, :]
    within = jnp.argsort(orders, axis=2)
    dealt = jnp.take_along_axis(pieces, within, axis=2).reshape(N_FSDP, SEQ_G)
    given_scores = jax.random.randint(key_given, (N_FSDP, SEQ_G), 0, 1 << 20) * SEQ_G + jnp.arange(SEQ_G)[None, :]
    given_to_dealt = jnp.argsort(given_scores, axis=1)
    lengths = jnp.take_along_axis(dealt, given_to_dealt, axis=1)
    dealing = jnp.argsort(given_to_dealt, axis=1)
    return (lengths.astype(jnp.int32), dealing.astype(jnp.int32))


def draw_lengths(key, part):
    return plan_sequences(key)[0]


def draw_dealing(key, part):
    return plan_sequences(key)[1]


def draw_head_params(key, part):
    key_bias, key_rate, key_skip = jax.random.split(jax.random.fold_in(key, 29), 3)
    biases = jax.random.uniform(key_bias, (1, MH), jnp.float32, -6.0, -2.0)
    rates = jax.random.uniform(key_rate, (1, MH), jnp.float32, 0.0, 2.8)
    skips = jax.random.uniform(key_skip, (1, MH), jnp.float32, 0.5, 1.5)
    return jnp.concatenate([biases, rates, skips], axis=0)


def block_levels(key, dims, cuts, low, top_value):
    factor_of = 1.0
    for dim, blocks in cuts:
        heights = jax.random.uniform(jax.random.fold_in(jax.random.fold_in(key, 6), dim), (blocks,), jnp.float32, low / len(cuts), top_value / len(cuts))
        factor_of = factor_of * jnp.repeat(jnp.exp(heights), dims[dim] // blocks).reshape((-1,) + (1,) * (len(dims) - 1 - dim))
    return factor_of


def normal_values(stream_key, shape, deviation, bound, shards=(), kind=jnp.bfloat16):
    values = jax.random.normal(stream_key, shape, jnp.float32) * deviation
    if len(shards) > 0:
        values = block_levels(stream_key, shape, shards, -0.22, 0.18) * values
    return jnp.clip(values, min=-bound, max=bound).astype(kind)


def setup_inputs(seed: int = 0) -> dict:
    key_of = jax.random.split(jax.random.key(seed), 20)
    return {
        "tokens": normal_values(key_of[0], (TOKENS, D), 1.0, 6.0, ((0, 32),)),
        "cotangent": normal_values(key_of[1], (TOKENS, D), 1.0, 6.0, ((0, 32),)),
        "lengths": draw_lengths(jax.random.fold_in(key_of[19], 71), 0),
        "dealing": draw_dealing(jax.random.fold_in(key_of[19], 71), 0),
        "norm_in": jnp.clip(1.0 + 0.1 * jax.random.normal(key_of[4], (D,), jnp.float32), 0.5, 1.5).astype(jnp.bfloat16),
        "w_query": normal_values(key_of[5], (D, HQ * HD), D ** -0.5, 0.1875, ((0, 4), (1, 2))),
        "w_keyval": normal_values(key_of[6], (D, KVH, 2 * HD), D ** -0.5, 0.1875, ((0, 4), (1, 2))),
        "w_attn_out": normal_values(key_of[7], (HQ * HD, D), (HQ * HD // 16) ** -0.5, 1.0, ((0, 2), (1, 4))),
        "w_zx": normal_values(key_of[8], (D, 2, DI), D ** -0.5, 0.1875, ((0, 4), (2, 2))),
        "w_bc": normal_values(key_of[9], (D, 2 * NS), D ** -0.5, 0.1875, ((0, 4),)),
        "w_step": normal_values(key_of[10], (D, MH), D ** -0.5, 0.1875, ((0, 4), (1, 2))),
        "head_params": draw_head_params(jax.random.fold_in(key_of[19], 71), 0),
        "taps_x": jnp.clip(jax.random.uniform(key_of[12], (KC + 1, MH, HD), jnp.float32, -0.5, 0.5) * block_levels(key_of[12], (KC + 1, MH, HD), ((1, 2), (2, 4)), -0.4, 0.0), -0.5, 0.5).astype(jnp.bfloat16),
        "taps_bc": jnp.clip(jax.random.uniform(key_of[13], (KC + 1, 2 * NS), jnp.float32, -0.5, 0.5) * block_levels(key_of[13], (KC + 1, 2 * NS), ((1, 4),), -0.4, 0.0), -0.5, 0.5).astype(jnp.bfloat16),
        "gain_mamba": jnp.clip(1.0 + 0.1 * jax.random.normal(key_of[14], (MH, HD), jnp.float32), 0.5, 1.5).astype(jnp.bfloat16),
        "w_mamba_out": normal_values(key_of[15], (DI, D), DI ** -0.5, 0.15625, ((0, 2), (1, 4))),
        "norm_mid": jnp.clip(1.0 + 0.1 * jax.random.normal(key_of[16], (D,), jnp.float32), 0.5, 1.5).astype(jnp.bfloat16),
        "w_gate_up": normal_values(key_of[17], (D, 2, FF), D ** -0.5, 0.1875, ((0, 4), (2, 2))),
        "w_down": normal_values(key_of[18], (FF, D), FF ** -0.5, 0.125, ((0, 2), (1, 4))),
    }


EPSILON = 1e-05
ROPE_BASE = 100000000000.0
PRECISE = lax.Precision.HIGHEST

@jax.custom_vjp
def low(v):
    return lax.optimization_barrier(v.astype(jnp.bfloat16)).astype(jnp.float32)

@jax.custom_vjp
def low_back(v):
    return v

def low_keep(v):
    return (low(v), None)

def low_pass(kept, grad):
    return (grad,)

def back_keep(v):
    return (v, None)

def back_low(kept, grad):
    return (low(grad),)
low.defvjp(low_keep, low_pass)
low_back.defvjp(back_keep, back_low)

def low_both(value):
    return low_back(low(value))

def product(left, right):
    return jnp.dot(left, right, precision=PRECISE)

def dealt_rows(lengths, dealing, first_row, row_count):
    seq_count = lengths.shape[0]
    numbers = jnp.arange(seq_count, dtype=jnp.int32)
    given_start = jnp.cumsum(lengths, dtype=jnp.int32) - lengths
    chosen = (dealing[:, None] == numbers[None, :]).astype(jnp.int32)
    dealt_len = lax.optimization_barrier(jnp.sum(chosen * lengths[None, :], axis=1, dtype=jnp.int32))
    dealt_from = lax.optimization_barrier(jnp.sum(chosen * given_start[None, :], axis=1, dtype=jnp.int32))
    dealt_start = jnp.cumsum(dealt_len, dtype=jnp.int32) - dealt_len
    spots = first_row + jnp.arange(row_count, dtype=jnp.int32)
    inside = ((spots[:, None] >= dealt_start[None, :]) & (spots[:, None] < (dealt_start + dealt_len)[None, :])).astype(jnp.int32)
    segment = lax.optimization_barrier(jnp.sum(inside * numbers[None, :], axis=1, dtype=jnp.int32))
    begins = lax.optimization_barrier(jnp.sum(inside * dealt_start[None, :], axis=1, dtype=jnp.int32))
    anchor = lax.optimization_barrier(jnp.sum(inside * dealt_from[None, :], axis=1, dtype=jnp.int32))
    position = spots - begins
    return (anchor + position, segment, position)

def rotary(vectors, position):
    half_width = vectors.shape[-1] // 2
    freqs = ROPE_BASE ** (-jnp.arange(half_width, dtype=jnp.float32) / half_width)
    angles = position.astype(jnp.float32)[:, None] * freqs[None, :]
    cosine = jnp.cos(angles)[:, None, :]
    sine_part = jnp.sin(angles)[:, None, :]
    front = vectors[..., :half_width]
    behind = vectors[..., half_width:]
    return jnp.concatenate([front * cosine - behind * sine_part, behind * cosine + front * sine_part], axis=-1)

def attend_block(query_part, key_rows, value_rows, query_seg, query_spot, segment, spots):
    head_width = query_part.shape[-1]
    scores = jnp.einsum('igsd,jgd->gsij', query_part, key_rows, precision=PRECISE) * head_width ** (-0.5)
    scores = low_back(scores)
    allowed = (query_seg[:, None] == segment[None, :]) & (query_spot[:, None] >= spots[None, :])
    scores = jnp.where(allowed[None, None], scores, -1e+30)
    peak = lax.optimization_barrier(jnp.max(scores, axis=-1, keepdims=True))
    weights = jnp.exp(scores - peak)
    probs = low(weights / lax.optimization_barrier(jnp.sum(weights, axis=-1, keepdims=True)))
    return jnp.einsum('gsij,jgd->igsd', probs, value_rows, precision=PRECISE)

def attend(queries, key_rows, value_rows, segment):
    row_total, head_count, head_width = queries.shape
    kv_count = key_rows.shape[1]
    grouped = queries.reshape(row_total, kv_count, head_count // kv_count, head_width)
    spots = jnp.arange(row_total, dtype=jnp.int32)
    block_rows = row_total // 2
    outputs = []
    for block_index in range(2):
        lower = block_index * block_rows
        outputs.append(jax.checkpoint(attend_block)(grouped[lower:lower + block_rows], key_rows, value_rows, segment[lower:lower + block_rows], spots[lower:lower + block_rows], segment, spots))
    return jnp.concatenate(outputs, axis=0).reshape(row_total, head_count, head_width)

def attention_core(query_raw, keyval_raw, segment, position):
    row_total = query_raw.shape[0]
    queries = low(rotary(query_raw.reshape(row_total, -1, HD), position))
    pairs = keyval_raw.reshape(row_total, -1, 2 * HD)
    key_rows = low(rotary(pairs[..., :HD], position))
    value_rows = low(pairs[..., HD:])
    return attend(queries, key_rows, value_rows, segment).reshape(row_total, -1)

def convolve(signal, taps, position):
    row_total = signal.shape[0]
    width_k = taps.shape[0] - 1
    result = taps[width_k][None, :] + taps[width_k - 1][None, :] * signal
    for lag_index in range(1, width_k):
        moved = jnp.concatenate([jnp.zeros((lag_index, signal.shape[1]), signal.dtype), signal[:row_total - lag_index]], axis=0)
        usable = (position >= lag_index).astype(signal.dtype)[:, None]
        result = result + taps[width_k - 1 - lag_index][None, :] * moved * usable
    return result

def state_space(inputs, b_rows, c_rows, steps, rates, segment):
    row_total, head_count, head_width = inputs.shape
    state_width = b_rows.shape[1]
    block_count = row_total // BLK

    def split_blocks(array):
        return array.reshape((block_count, BLK) + array.shape[1:])

    def advance(carry, pieces):
        states, last_seg = carry
        x_part, b_part, c_part, step_part, seg_part = pieces
        decays = jnp.cumsum(step_part * rates[None, :], axis=0)
        spots = jnp.arange(BLK)
        allowed = (seg_part[:, None] == seg_part[None, :]) & (spots[:, None] >= spots[None, :])
        spread = jnp.where(allowed[:, :, None], decays[:, None, :] - decays[None, :, :], 0.0)
        mixing = jnp.where(allowed[:, :, None], jnp.exp(spread), 0.0)
        inner = product(c_part, b_part.T)
        coupling = mixing * inner[:, :, None] * step_part[None, :, :]
        local_out = jnp.einsum('ijh,jhp->ihp', coupling, x_part, precision=PRECISE)
        carried = (seg_part == last_seg).astype(jnp.float32)[:, None] * jnp.exp(decays)
        recall = jnp.einsum('in,hpn->ihp', c_part, states, precision=PRECISE) * carried[:, :, None]
        tail_seg = seg_part[BLK - 1]
        keeps = (seg_part == tail_seg).astype(jnp.float32)[:, None] * jnp.exp(decays[BLK - 1][None, :] - decays) * step_part
        fresh = jnp.einsum('jhp,jn->hpn', keeps[:, :, None] * x_part, b_part, precision=PRECISE)
        linger = (tail_seg == last_seg).astype(jnp.float32) * jnp.exp(decays[BLK - 1])
        return ((states * linger[:, None, None] + fresh, tail_seg), local_out + recall)
    start = (jnp.zeros((head_count, head_width, state_width), jnp.float32), jnp.int32(-1))
    pieces = (split_blocks(inputs), split_blocks(b_rows), split_blocks(c_rows), split_blocks(steps), split_blocks(segment))
    final_carry, outputs = lax.scan(jax.checkpoint(advance), start, pieces)
    return outputs.reshape(row_total, head_count, head_width)

def mamba_mix(gate_in, x_in, bc_in, step_in, taps_x, taps_bc, head_params, gain_mamba, segment, position):
    row_total = x_in.shape[0]
    head_count = head_params.shape[1]
    conv_x = low(jax.nn.silu(convolve(x_in, taps_x.reshape(taps_x.shape[0], -1), position)))
    conv_bc = low(jax.nn.silu(convolve(bc_in, taps_bc, position)))
    state_width = conv_bc.shape[1] // 2
    steps = jax.nn.softplus(step_in + head_params[0][None, :])
    rates = -jnp.exp(head_params[1])
    heads_in = conv_x.reshape(row_total, head_count, -1)
    mixed = state_space(heads_in, conv_bc[:, :state_width], conv_bc[:, state_width:], steps, rates, segment)
    mixed = mixed + head_params[2][None, :, None] * heads_in
    gated = mixed.reshape(row_total, -1) * jax.nn.silu(gate_in)
    normed = gated * lax.rsqrt(lax.optimization_barrier(jnp.mean(gated * gated, axis=-1, keepdims=True)) + EPSILON)
    return normed * gain_mamba.reshape(1, -1)

def layer_pack(x_rows, segment, position, params):
    norm_in, w_query, w_keyval, w_attn_out, w_zx, w_bc, w_step, head_params, taps_x, taps_bc, gain_mamba, w_mamba_out, norm_mid, w_gate_up, w_down = params
    row_total = x_rows.shape[0]
    unit_in = x_rows * lax.rsqrt(lax.optimization_barrier(jnp.mean(x_rows * x_rows, axis=1, keepdims=True)) + EPSILON)
    normed_in = low(unit_in * norm_in[None, :])
    query_raw = low_back(product(normed_in, w_query))
    keyval_raw = low_back(product(normed_in, w_keyval.reshape(D, -1)))
    attn_rows = low_both(attention_core(query_raw, keyval_raw, segment, position))
    zx_raw = low_back(product(normed_in, w_zx.reshape(D, -1))).reshape(row_total, 2, -1)
    bc_raw = product(normed_in, w_bc)
    step_raw = low_back(product(normed_in, w_step))
    mamba_rows = low_both(mamba_mix(zx_raw[:, 0], zx_raw[:, 1], bc_raw, step_raw, taps_x, taps_bc, head_params, gain_mamba, segment, position))
    mixer = low_back(product(attn_rows, w_attn_out) + product(mamba_rows, w_mamba_out))
    hidden = x_rows + mixer
    unit_mid = hidden * lax.rsqrt(lax.optimization_barrier(jnp.mean(hidden * hidden, axis=1, keepdims=True)) + EPSILON)
    normed_mid = low(unit_mid * norm_mid[None, :])
    gate_up = low_back(product(normed_mid, w_gate_up.reshape(D, -1))).reshape(row_total, 2, -1)
    activated = low(jax.nn.silu(gate_up[:, 0]) * gate_up[:, 1])
    return hidden + low_back(product(activated, w_down))

def pack_rows(group_lengths, group_dealing):

    def one_rank(rank_index):
        return dealt_rows(group_lengths, group_dealing, rank_index * TOK_RANK, TOK_RANK)
    return jax.vmap(one_rank)(jnp.arange(N_CTX, dtype=jnp.int32))

def reference(tokens, cotangent, lengths, dealing, norm_in, w_query, w_keyval, w_attn_out, w_zx, w_bc, w_step, head_params, taps_x, taps_bc, gain_mamba, w_mamba_out, norm_mid, w_gate_up, w_down):
    sources, segments, positions = jax.vmap(pack_rows)(lengths, dealing)
    sources = sources + (jnp.arange(N_FSDP, dtype=jnp.int32) * G_TOK)[:, None, None]
    sources = sources.reshape(-1, TOK_RANK)
    segments = segments.reshape(-1, TOK_RANK)
    positions = positions.reshape(-1, TOK_RANK)
    params = tuple((weight_arg.astype(jnp.float32) for weight_arg in (norm_in, w_query, w_keyval, w_attn_out, w_zx, w_bc, w_step, head_params, taps_x, taps_bc, gain_mamba, w_mamba_out, norm_mid, w_gate_up, w_down)))

    def forward(token_rows, weight_set):
        packed = jnp.take(token_rows, sources, axis=0)

        def run_pack(carry, items):
            return (carry, layer_pack(items[0], items[1], items[2], weight_set))
        final_carry, results = lax.scan(jax.checkpoint(run_pack), None, (packed, segments, positions))
        return jnp.zeros_like(token_rows).at[sources.reshape(-1)].set(results.reshape(-1, D))
    result, pullback = jax.vjp(forward, tokens.astype(jnp.float32), params)
    grad_x, grads = pullback(cotangent.astype(jnp.float32))
    return (result.astype(jnp.bfloat16), grad_x.astype(jnp.bfloat16), grads[0], grads[1], grads[2], grads[3], grads[4], grads[5], grads[6], grads[7], grads[8], grads[9], grads[10], grads[11], grads[12], grads[13], grads[14])
```

```python
import jax
import jax.numpy as jnp
from jax import lax
from jax.experimental import pallas as pl
from jax.experimental.pallas import tpu as pltpu
from jax.sharding import PartitionSpec as P

HD = 64
BLK = 128
LANES = 128
EPSILON = 1e-05
ROPE_BASE = 100000000000.0
PRECISE = lax.Precision.HIGHEST
F32 = jnp.float32
BF = jnp.bfloat16
FAR = -1e30


def dot_nn(a, b, precision=None):
    return lax.dot_general(
        a, b, (((1,), (0,)), ((), ())), precision=precision, preferred_element_type=F32
    )


def dot_nt(a, b, precision=None):
    return lax.dot_general(
        a, b, (((1,), (1,)), ((), ())), precision=precision, preferred_element_type=F32
    )


def dot_tn(a, b, precision=None):
    return lax.dot_general(
        a, b, (((0,), (0,)), ((), ())), precision=precision, preferred_element_type=F32
    )


def iota(shape, dim):
    return lax.broadcasted_iota(jnp.int32, shape, dim)


def swap_halves(v):
    lanes = v.shape[1]
    low = (iota(v.shape, 1) & (HD - 1)) < HD // 2
    return jnp.where(low, pltpu.roll(v, lanes - HD // 2, 1), pltpu.roll(v, HD // 2, 1))


def split_pair(v):
    first = iota(v.shape, 1) < HD
    zero = jnp.zeros_like(v)
    return jnp.concatenate([jnp.where(first, v, zero), jnp.where(first, zero, v)], axis=0)


def keys_values(kv, cos, sin):
    first = iota(kv.shape, 1) < HD
    roped = kv * cos + swap_halves(kv) * sin
    keys = jnp.where(first, roped, 0.0)
    values = jnp.where(first, 0.0, kv)
    key_pair = (keys.astype(BF), pltpu.roll(keys, HD, 1).astype(BF))
    value_pair = (pltpu.roll(values, HD, 1).astype(BF), values.astype(BF))
    return key_pair, value_pair


def attention_probs(query, key, allowed):
    scores = dot_nt(query, key) * HD ** (-0.5)
    scores = jnp.where(allowed, scores, FAR)
    weights = jnp.exp(scores - jnp.max(scores, axis=1, keepdims=True))
    return weights / jnp.sum(weights, axis=1, keepdims=True)


def allowed_rows(segc, segr, lower, count):
    keys = lower + count
    same = segc[lower:keys, :] == segr[:, :keys]
    return same & (iota((count, keys), 0) + lower >= iota((count, keys), 1))


def attention_fwd_kernel(q_ref, kv_ref, cos_ref, sin_ref, segc_ref, segr_ref, out_ref):
    rows, width = q_ref.shape
    cos, sin = cos_ref[...], sin_ref[...]
    key_pair, value_pair = keys_values(kv_ref[...], cos, sin)
    segc, segr = segc_ref[...], segr_ref[...]
    for pair in range(width // LANES):
        cols = slice(pair * LANES, (pair + 1) * LANES)
        raw = q_ref[:, cols]
        query = (raw * cos + swap_halves(raw) * sin).astype(BF)
        for lower in range(0, rows, BLK):
            keys = lower + BLK
            allowed = allowed_rows(segc, segr, lower, BLK)
            total = None
            for side in range(2):
                probs = attention_probs(query[lower:keys], key_pair[side][:keys], allowed)
                part = dot_nn(probs.astype(BF), value_pair[side][:keys])
                total = part if total is None else total + part
            out_ref[lower:keys, cols] = total.astype(BF)


def attention_bwd_kernel(
    q_ref, kv_ref, cos_ref, sin_ref, segc_ref, segr_ref, do_ref, out_ref, dk_ref, dv_ref
):
    rows, width = q_ref.shape
    cos, sin = cos_ref[...], sin_ref[...]
    key_pair, value_pair = keys_values(kv_ref[...], cos, sin)
    segc, segr = segc_ref[...], segr_ref[...]
    dk_ref[...] = jnp.zeros_like(dk_ref)
    dv_ref[...] = jnp.zeros_like(dv_ref)
    for pair in range(width // LANES):
        cols = slice(pair * LANES, (pair + 1) * LANES)
        raw = q_ref[:, cols]
        query = (raw * cos + swap_halves(raw) * sin).astype(BF)
        for lower in range(0, rows, BLK):
            keys = lower + BLK
            allowed = allowed_rows(segc, segr, lower, BLK)
            query_part = query[lower:keys]
            grad = do_ref[lower:keys, cols]
            d_query = None
            probs_all, scores_all = [], []
            for side in range(2):
                probs = attention_probs(query_part, key_pair[side][:keys], allowed)
                d_probs = dot_nt(grad, value_pair[side][:keys])
                inner = jnp.sum(d_probs * probs, axis=1, keepdims=True)
                d_scores = (probs * (d_probs - inner)).astype(BF)
                part = dot_nn(d_scores, key_pair[side][:keys])
                d_query = part if d_query is None else d_query + part
                probs_all.append(probs.astype(BF))
                scores_all.append(d_scores)
            dv_ref[:keys, :] += dot_tn(jnp.concatenate(probs_all, axis=0), split_pair(grad))
            dk_ref[:keys, :] += dot_tn(jnp.concatenate(scores_all, axis=0), split_pair(query_part))
            d_query = d_query * HD ** (-0.5)
            cos_part, sin_part = cos[lower:keys], sin[lower:keys]
            out_ref[lower:keys, cols] = (
                d_query * cos_part - swap_halves(d_query) * sin_part
            ).astype(BF)
    first = iota(dk_ref.shape, 1) < HD
    d_key = dk_ref[...]
    d_key = (d_key + pltpu.roll(d_key, HD, 1)) * HD ** (-0.5)
    d_key = d_key * cos - swap_halves(d_key) * sin
    d_value = dv_ref[...]
    d_value = d_value + pltpu.roll(d_value, HD, 1)
    out_ref[:, width:] = jnp.where(first, d_key, d_value).astype(BF)


def conv_rows(signal, taps_ref, position):
    total = taps_ref[4:5, :] + taps_ref[3:4, :] * signal
    for lag in range(1, 4):
        moved = jnp.where(position >= lag, pltpu.roll(signal, lag, 0), 0.0)
        total = total + taps_ref[3 - lag : 4 - lag, :] * moved
    return total


def conv_back(signal, d_pre, taps_ref, grad_ref, position):
    rows = signal.shape[0]
    grad_ref[...] = jnp.zeros_like(grad_ref)
    grad_ref[4:5, :] = jnp.sum(d_pre, axis=0, keepdims=True)
    grad_ref[3:4, :] = jnp.sum(d_pre * signal, axis=0, keepdims=True)
    total = taps_ref[3:4, :] * d_pre
    for lag in range(1, 4):
        kept = jnp.where(position >= lag, d_pre, 0.0)
        grad_ref[3 - lag : 4 - lag, :] = jnp.sum(
            kept * pltpu.roll(signal, lag, 0), axis=0, keepdims=True
        )
        total = total + taps_ref[3 - lag : 4 - lag, :] * pltpu.roll(kept, rows - lag, 0)
    return total


def softplus(v):
    return jnp.maximum(v, 0.0) + jnp.log1p(jnp.exp(-jnp.abs(v)))


def spread_matrix(width):
    shape = (LANES, width)
    return (iota(shape, 0) == (iota(shape, 1) >> 6)).astype(F32)


def scan_setup(step_ref, heads_ref):
    steps = softplus(step_ref[...] + heads_ref[0:1, :])
    rates = -jnp.exp(heads_ref[1:2, :])
    return steps, rates


def block_decays(steps, rates, segc, lower):
    upper = lower + BLK
    shape = (BLK, BLK)
    lower_ones = (iota(shape, 0) >= iota(shape, 1)).astype(F32)
    decays = dot_nn(lower_ones, steps[lower:upper] * rates, PRECISE)
    seg_part = segc[lower:upper]
    if lower == 0:
        arrive = None
    else:
        carried = seg_part == segc[lower - 1 : lower]
        arrive = jnp.where(carried, jnp.exp(decays), 0.0)
    kept = seg_part == segc[upper - 1 : upper]
    leave = jnp.where(kept, jnp.exp(decays[BLK - 1 : BLK] - decays), 0.0)
    return decays, arrive, leave, lower_ones


def block_mixing(decays, decays_t, head, allowed):
    gap = decays[:, head : head + 1] - decays_t[head : head + 1, :]
    return jnp.exp(jnp.where(allowed, gap, FAR))


def scan_fwd_kernel(
    x_ref, bc_ref, step_ref, tapx_ref, tapbc_ref, heads_ref, skip_ref, segc_ref, segr_ref,
    pos_ref, out_ref, states_ref,
):
    rows, width = x_ref.shape
    position = pos_ref[...]
    segc, segr = segc_ref[...], segr_ref[...]
    conv_x = jax.nn.silu(conv_rows(x_ref[...], tapx_ref, position)).astype(BF)
    conv_bc = jax.nn.silu(conv_rows(bc_ref[...], tapbc_ref, position)).astype(BF)
    steps, rates = scan_setup(step_ref, heads_ref)
    spread = spread_matrix(width)
    scaled = conv_x.astype(F32) * dot_nn(steps, spread, PRECISE)
    state = None
    for lower in range(0, rows, BLK):
        upper = lower + BLK
        b_part = conv_bc[lower:upper, :LANES]
        c_part = conv_bc[lower:upper, LANES:]
        decays, arrive, leave, lower_ones = block_decays(steps, rates, segc, lower)
        decays_t = decays.T
        allowed = (segc[lower:upper] == segr[:, lower:upper]) & (lower_ones > 0.0)
        inner = dot_nt(c_part, b_part)
        scaled_part = scaled[lower:upper]
        scaled_low = scaled_part.astype(BF)
        fresh = dot_tn(b_part, (scaled_part * dot_nn(leave, spread, PRECISE)).astype(BF))
        if state is None:
            recall = None
            states_ref[lower // BLK] = jnp.zeros(fresh.shape, F32)
            state = fresh
        else:
            arrive_wide = dot_nn(arrive, spread, PRECISE)
            recall = dot_nn(c_part, state.astype(BF)) * arrive_wide
            states_ref[lower // BLK] = state
            state = state * arrive_wide[BLK - 1 : BLK] + fresh
        for pair in range(width // LANES):
            cols = slice(pair * LANES, (pair + 1) * LANES)
            mixes = [
                (block_mixing(decays, decays_t, 2 * pair + side, allowed) * inner).astype(BF)
                for side in range(2)
            ]
            local = dot_nn(jnp.concatenate(mixes, axis=1), split_pair(scaled_low[:, cols]))
            if recall is not None:
                local = local + recall[:, cols]
            out_ref[lower:upper, cols] = local + skip_ref[0:1, cols] * conv_x[
                lower:upper, cols
            ].astype(F32)


def scan_bwd_kernel(
    x_ref, bc_ref, step_ref, tapx_ref, tapbc_ref, heads_ref, skip_ref, segc_ref, segr_ref,
    pos_ref, states_ref, dy_ref, out_ref, gtapx_ref, gtapbc_ref, gheads_ref, dx_ref, dbc_ref,
):
    rows, width = x_ref.shape
    position = pos_ref[...]
    segc, segr = segc_ref[...], segr_ref[...]
    pre_x = conv_rows(x_ref[...], tapx_ref, position)
    pre_bc = conv_rows(bc_ref[...], tapbc_ref, position)
    conv_x = jax.nn.silu(pre_x).astype(BF)
    conv_bc = jax.nn.silu(pre_bc).astype(BF)
    steps, rates = scan_setup(step_ref, heads_ref)
    spread = spread_matrix(width)
    steps_wide = dot_nn(steps, spread, PRECISE)
    lane = iota((BLK, LANES), 1)
    sub = iota((LANES, BLK), 0)
    last_row = iota((BLK, LANES), 0) == BLK - 1
    d_state = None
    g_bias = jnp.zeros((1, LANES), F32)
    g_rate = jnp.zeros((1, LANES), F32)
    g_skip = jnp.zeros((1, width), F32)
    for lower in range(rows - BLK, -1, -BLK):
        upper = lower + BLK
        b_part = conv_bc[lower:upper, :LANES]
        c_part = conv_bc[lower:upper, LANES:]
        decays, arrive, leave, lower_ones = block_decays(steps, rates, segc, lower)
        decays_t = decays.T
        allowed = (segc[lower:upper] == segr[:, lower:upper]) & (lower_ones > 0.0)
        inner = dot_nt(c_part, b_part)
        x_part = conv_x[lower:upper].astype(F32)
        scaled_part = x_part * steps_wide[lower:upper]
        scaled_low = scaled_part.astype(BF)
        grad = dy_ref[lower:upper, :]
        grad_low = grad.astype(BF)
        d_scaled = []
        d_inner = jnp.zeros((BLK, BLK), F32)
        row_sums = jnp.zeros((BLK, LANES), F32)
        col_sums = jnp.zeros((LANES, BLK), F32)
        for pair in range(width // LANES):
            cols = slice(pair * LANES, (pair + 1) * LANES)
            grad_pair = split_pair(grad_low[:, cols])
            d_mix = dot_nt(grad_pair, scaled_low[:, cols])
            mixes = []
            for side in range(2):
                head = 2 * pair + side
                mixing = block_mixing(decays, decays_t, head, allowed)
                mix = mixing * inner
                d_part = d_mix[side * BLK : (side + 1) * BLK]
                d_inner = d_inner + d_part * mixing
                both = d_part * mix
                row_sums = jnp.where(lane == head, jnp.sum(both, axis=1, keepdims=True), row_sums)
                col_sums = jnp.where(sub == head, jnp.sum(both, axis=0, keepdims=True), col_sums)
                mixes.append(mix.astype(BF))
            d_scaled.append(dot_tn(jnp.concatenate(mixes, axis=0), grad_pair))
        d_scaled = jnp.concatenate(d_scaled, axis=1)
        d_decays = row_sums - col_sums.T
        d_inner = d_inner.astype(BF)
        d_c = dot_nn(d_inner, b_part)
        d_b = dot_tn(d_inner, c_part)
        if lower > 0:
            arrive_wide = dot_nn(arrive, spread, PRECISE)
            state = states_ref[lower // BLK]
            state_low = state.astype(BF)
            recall = dot_nn(c_part, state_low) * arrive_wide
            d_decays = d_decays + dot_nt(recall * grad, spread, PRECISE)
            grad_in = (grad * arrive_wide).astype(BF)
            d_c = d_c + dot_nt(grad_in, state_low)
        if d_state is not None:
            state_grad = d_state.astype(BF)
            leave_wide = dot_nn(leave, spread, PRECISE)
            d_kept = dot_nn(b_part, state_grad) * leave_wide
            d_b = d_b + dot_nt((scaled_part * leave_wide).astype(BF), state_grad)
            d_leave = dot_nt(d_kept * scaled_part, spread, PRECISE)
            d_last = jnp.sum(d_leave, axis=0, keepdims=True)
            if lower > 0:
                lingering = jnp.sum(d_state * state, axis=0, keepdims=True)
                lingering = lingering * arrive_wide[BLK - 1 : BLK]
                d_last = d_last + dot_nt(
                    jnp.broadcast_to(lingering, (8, width)), spread, PRECISE
                )[0:1]
            d_decays = d_decays - d_leave + jnp.where(last_row, d_last, 0.0)
            d_scaled = d_scaled + d_kept
        if lower > 0:
            d_new = dot_tn(c_part, grad_in)
            if d_state is None:
                d_state = d_new
            else:
                d_state = d_state * arrive_wide[BLK - 1 : BLK] + d_new
        d_log = dot_tn(lower_ones, d_decays, PRECISE)
        steps_part = steps[lower:upper]
        d_steps = dot_nt(d_scaled * x_part, spread, PRECISE) + d_log * rates
        d_step_in = d_steps * jax.nn.sigmoid(step_ref[lower:upper, :] + heads_ref[0:1, :])
        g_bias = g_bias + jnp.sum(d_step_in, axis=0, keepdims=True)
        g_rate = g_rate + jnp.sum(d_log * steps_part, axis=0, keepdims=True) * rates
        g_skip = g_skip + jnp.sum(grad * x_part, axis=0, keepdims=True)
        out_ref[lower:upper, width + 2 * LANES :] = d_step_in.astype(BF)
        dx_ref[lower:upper, :] = d_scaled * steps_wide[lower:upper] + grad * skip_ref[0:1, :]
        dbc_ref[lower:upper, :LANES] = d_b
        dbc_ref[lower:upper, LANES:] = d_c
    gheads_ref[...] = jnp.zeros_like(gheads_ref)
    gheads_ref[0:1, :] = g_bias
    gheads_ref[1:2, :] = g_rate
    gheads_ref[2:3, :] = dot_nt(jnp.broadcast_to(g_skip, (8, width)), spread, PRECISE)[0:1]
    gate = jax.nn.sigmoid(pre_x)
    d_pre = dx_ref[...] * gate * (1.0 + pre_x * (1.0 - gate))
    out_ref[:, :width] = conv_back(x_ref[...], d_pre, tapx_ref, gtapx_ref, position).astype(BF)
    gate = jax.nn.sigmoid(pre_bc)
    d_pre = dbc_ref[...] * gate * (1.0 + pre_bc * (1.0 - gate))
    out_ref[:, width : width + 2 * LANES] = conv_back(
        bc_ref[...], d_pre, tapbc_ref, gtapbc_ref, position
    ).astype(BF)


VMEM_BYTES = 48 * 1024 * 1024


def column_block(rows, width, index):
    return pl.BlockSpec((rows, width), lambda i: (0, index))


def whole_block(shape):
    zeros = (0,) * len(shape)
    return pl.BlockSpec(shape, lambda i: zeros)


def single_step(kernel, in_specs, outs, scratch=(), flops=1000000):
    return pl.pallas_call(
        kernel,
        grid=(1,),
        in_specs=in_specs,
        out_specs=[whole_block(o.shape) for o in outs],
        out_shape=outs,
        scratch_shapes=list(scratch),
        compiler_params=pltpu.CompilerParams(vmem_limit_bytes=VMEM_BYTES),
        cost_estimate=pl.CostEstimate(flops=flops, bytes_accessed=4000000, transcendentals=0),
    )


def attention_specs(rows, width, gate_width):
    return [
        column_block(rows, width, gate_width // width),
        column_block(rows, LANES, (gate_width + width) // LANES),
        whole_block((rows, LANES)),
        whole_block((rows, LANES)),
        whole_block((rows, 1)),
        whole_block((1, rows)),
    ]


def attention_fwd(y_a, width, gate_width, cos, sin, segc, segr):
    rows = y_a.shape[0]
    return single_step(
        attention_fwd_kernel,
        attention_specs(rows, width, gate_width),
        [jax.ShapeDtypeStruct((rows, width), BF)],
        flops=3000000000,
    )(y_a, y_a, cos, sin, segc, segr)[0]


def attention_bwd(y_a, width, gate_width, cos, sin, segc, segr, d_attn):
    rows = y_a.shape[0]
    return single_step(
        attention_bwd_kernel,
        attention_specs(rows, width, gate_width) + [whole_block((rows, width))],
        [jax.ShapeDtypeStruct((rows, width + LANES), BF)],
        [pltpu.VMEM((rows, LANES), F32), pltpu.VMEM((rows, LANES), F32)],
        flops=8000000000,
    )(y_a, y_a, cos, sin, segc, segr, d_attn)[0]


def scan_specs(rows, width):
    return [
        column_block(rows, width, 0),
        column_block(rows, 2 * LANES, width // (2 * LANES)),
        column_block(rows, LANES, (width + 2 * LANES) // LANES),
        whole_block((8, width)),
        whole_block((8, 2 * LANES)),
        whole_block((8, LANES)),
        whole_block((1, width)),
        whole_block((rows, 1)),
        whole_block((1, rows)),
        whole_block((rows, 1)),
    ]


def scan_fwd(y_b, width, taps_x, taps_bc, heads, skip, segc, segr, position):
    rows = y_b.shape[0]
    return single_step(
        scan_fwd_kernel,
        scan_specs(rows, width),
        [
            jax.ShapeDtypeStruct((rows, width), F32),
            jax.ShapeDtypeStruct((rows // BLK, LANES, width), F32),
        ],
        flops=6000000000,
    )(y_b, y_b, y_b, taps_x, taps_bc, heads, skip, segc, segr, position)


def scan_bwd(y_b, width, taps_x, taps_bc, heads, skip, segc, segr, position, states, d_out):
    rows = y_b.shape[0]
    return single_step(
        scan_bwd_kernel,
        scan_specs(rows, width)
        + [whole_block(states.shape), whole_block((rows, width))],
        [
            jax.ShapeDtypeStruct(y_b.shape, BF),
            jax.ShapeDtypeStruct((8, width), F32),
            jax.ShapeDtypeStruct((8, 2 * LANES), F32),
            jax.ShapeDtypeStruct((8, LANES), F32),
        ],
        [pltpu.VMEM((rows, width), F32), pltpu.VMEM((rows, 2 * LANES), F32)],
        flops=15000000000,
    )(y_b, y_b, y_b, taps_x, taps_bc, heads, skip, segc, segr, position, states, d_out)


CORE_SWAP = [(0, 1), (1, 0), (2, 3), (3, 2)]
CHIP_SWAP = [(0, 2), (2, 0), (1, 3), (3, 1)]
PAIR_SWAP = [(0, 1), (1, 0)]
QUARTERS = (0, 2, 1, 3)
MOST_ROTATIONS = 8


def core_swap(v):
    return lax.ppermute(v, "ctx", CORE_SWAP)


def chip_swap(v):
    return lax.ppermute(v, "ctx", CHIP_SWAP)


def pair_swap(v):
    return lax.ppermute(v, "tp", PAIR_SWAP)


def rotate(v, by):
    size = lax.axis_size("fsdp")
    return lax.ppermute(v, "fsdp", [(i, (i + by) % size) for i in range(size)])


def few_shards():
    return lax.axis_size("fsdp") <= MOST_ROTATIONS


def quarter_perm(width):
    size = lax.axis_size("fsdp")
    shard = width // size
    piece = shard // 4
    spots = jnp.arange(width, dtype=jnp.int32)
    slot = spots // (size * piece)
    turn = (spots // piece) % size
    within = spots % piece
    quarter = jnp.where(slot == 1, 2, jnp.where(slot == 2, 1, slot)) ^ lax.axis_index("ctx")
    if few_shards():
        owner = lax.rem(lax.axis_index("fsdp") - turn + size, size)
    else:
        owner = turn
    column = owner * shard + quarter * piece + within
    return (spots[:, None] == column[None, :]).astype(BF)


def gather_rows(shard):
    piece = shard.shape[0] // 4
    own = lax.dynamic_slice_in_dim(shard, lax.axis_index("ctx") * piece, piece, 0)
    if few_shards():
        line = [own] + [rotate(own, by) for by in range(1, lax.axis_size("fsdp"))]
        line = jnp.concatenate(line, axis=0)
    else:
        line = lax.all_gather(own, "fsdp", axis=0, tiled=True)
    half = jnp.concatenate([line, chip_swap(line)], axis=0)
    return jnp.concatenate([half, core_swap(half)], axis=0)


def add_low(left, *others):
    total = left.astype(F32)
    for other in others:
        total = total + other.astype(F32)
    return total.astype(BF)


def reduce_rows(whole):
    half = whole.shape[0] // 2
    whole = add_low(whole[:half], core_swap(whole[half:]))
    half = half // 2
    line = add_low(whole[:half], chip_swap(whole[half:]))
    size = lax.axis_size("fsdp")
    if few_shards():
        piece = half // size
        parts = [line[by * piece : (by + 1) * piece] for by in range(size)]
        return add_low(parts[0], *[rotate(parts[by], size - by) for by in range(1, size)])
    return lax.psum_scatter(line, "fsdp", scatter_dimension=0, tiled=True)


def share_quarters(part):
    pair = (part, chip_swap(part))
    others = (core_swap(pair[0]), core_swap(pair[1]))
    by_gap = (pair[0], others[0], pair[1], others[1])
    index = lax.axis_index("ctx")
    core_bit, chip_bit = (index & 1) == 1, (index & 2) == 2
    rows = []
    for quarter in range(4):
        near = jnp.where(core_bit, by_gap[quarter ^ 1], by_gap[quarter])
        far = jnp.where(core_bit, by_gap[quarter ^ 3], by_gap[quarter ^ 2])
        rows.append(jnp.where(chip_bit, far, near))
    return jnp.concatenate(rows, axis=0).astype(F32)


def reduce_small(v):
    v = v + core_swap(v)
    v = v + chip_swap(v)
    if few_shards():
        total = v
        for by in range(1, lax.axis_size("fsdp")):
            total = total + rotate(v, by)
        return total
    return lax.psum(v, "fsdp")


def gather_small(v):
    size = lax.axis_size("fsdp")
    if not few_shards():
        return lax.all_gather(v, "fsdp", axis=0).astype(F32)
    rows = jnp.stack([v] + [rotate(v, by) for by in range(1, size)], axis=0)
    owner = jnp.arange(size, dtype=jnp.int32)
    turn = lax.rem(lax.axis_index("fsdp") - owner + size, size)
    chosen = (turn[:, None] == owner[None, :]).astype(BF)
    return dot_nn(chosen, rows)


def gather_group(rows):
    near = [rows, pair_swap(rows), chip_swap(rows)]
    near.append(lax.ppermute(rows, ("ctx", "tp"), [(i, i ^ 5) for i in range(8)]))
    near = jnp.concatenate(near, axis=0)
    return jnp.concatenate([near, core_swap(near)], axis=0)


def stack_spot(spot, rows):
    member = spot // rows
    gap = (member // 2) ^ lax.axis_index("ctx")
    turn = (member % 2) ^ lax.axis_index("tp")
    return ((gap & 1) * 4 + (gap >> 1) * 2 + turn) * rows + spot % rows


def pick_rows(spots, stack):
    numbers = jnp.arange(stack.shape[0], dtype=jnp.int32)
    chosen = (spots[:, None] == numbers[None, :]).astype(BF)
    return dot_nn(chosen, stack).astype(BF)


def dealt_order(lengths, dealing):
    numbers = jnp.arange(lengths.shape[0], dtype=jnp.int32)
    given_start = jnp.cumsum(lengths, dtype=jnp.int32) - lengths
    chosen = (dealing[:, None] == numbers[None, :]).astype(jnp.int32)
    dealt_len = jnp.sum(chosen * lengths[None, :], axis=1, dtype=jnp.int32)
    dealt_from = jnp.sum(chosen * given_start[None, :], axis=1, dtype=jnp.int32)
    dealt_start = jnp.cumsum(dealt_len, dtype=jnp.int32) - dealt_len
    return dealt_len, dealt_from, dealt_start


def look_up(spots, starts, counts, *tables):
    inside = (
        (spots[:, None] >= starts[None, :]) & (spots[:, None] < (starts + counts)[None, :])
    ).astype(jnp.int32)
    return [jnp.sum(inside * table[None, :], axis=1, dtype=jnp.int32) for table in tables]


def norm_back(grad_out, unit_rows, inverse, gain):
    scaled = grad_out * gain
    return inverse * (scaled - unit_rows * jnp.mean(scaled * unit_rows, axis=1, keepdims=True))


def inverse_norm(rows):
    return lax.rsqrt(jnp.mean(rows * rows, axis=1, keepdims=True) + EPSILON)


def padded(v, rows, cols):
    return jnp.pad(v, ((0, rows - v.shape[0]), (0, cols - v.shape[1])))


def per_device(
    tokens,
    cotangent,
    lengths,
    dealing,
    norm_in,
    w_query,
    w_keyval,
    w_attn_out,
    w_zx,
    w_bc,
    w_step,
    head_params,
    taps_x,
    taps_bc,
    gain_mamba,
    w_mamba_out,
    norm_mid,
    w_gate_up,
    w_down,
):
    tok_rows, model_width = tokens.shape
    tp_size = lax.axis_size("tp")
    fsdp_size = lax.axis_size("fsdp")
    rank_rows = tok_rows * tp_size
    tp_index = lax.axis_index("tp")
    fsdp_index = lax.axis_index("fsdp")
    ctx_index = lax.axis_index("ctx")
    shard = w_query.shape[0]
    heads = head_params.shape[1]
    scan_width = heads * HD
    query_width = w_query.shape[1]
    bc_width = w_bc.shape[1]
    ffn_width = w_gate_up.shape[2]
    own_start = tp_index * tok_rows
    peer_start = (tp_size - 1) * tok_rows - own_start

    dealt_len, dealt_from, dealt_start = dealt_order(lengths[0], dealing[0])
    numbers = jnp.arange(lengths.shape[1], dtype=jnp.int32)
    spots = ctx_index * rank_rows + jnp.arange(rank_rows, dtype=jnp.int32)
    segment, begins, anchor = look_up(
        spots, dealt_start, dealt_len, numbers, dealt_start, dealt_from
    )
    position = spots - begins
    sources = stack_spot(anchor + position, tok_rows)
    home = (ctx_index * tp_size + tp_index) * tok_rows + jnp.arange(tok_rows, dtype=jnp.int32)
    home_dealt, home_given = look_up(home, dealt_from, dealt_len, dealt_start, dealt_from)
    home_spots = stack_spot(home - home_given + home_dealt, tok_rows)
    segc, segr, posc = segment[:, None], segment[None, :], position[:, None]
    half_width = HD // 2
    freqs = ROPE_BASE ** (-jnp.arange(half_width, dtype=jnp.float32) / half_width)
    angles = position.astype(jnp.float32)[:, None] * freqs[None, :]
    cosine, sine = jnp.cos(angles), jnp.sin(angles)
    cos_table = jnp.concatenate([cosine] * 4, axis=1)
    sin_table = jnp.concatenate([-sine, sine, -sine, sine], axis=1)
    perm = quarter_perm(model_width)

    token_stack = gather_group(tokens)
    small = jnp.concatenate(
        [v.reshape(-1) for v in (norm_in, norm_mid, taps_x, taps_bc, gain_mamba)]
    )
    small_sizes = [v.size for v in (norm_in, norm_mid, taps_x, taps_bc, gain_mamba)]
    w_scan = gather_rows(
        jnp.concatenate([w_zx[:, 1, :], w_bc, padded(w_step, shard, LANES)], axis=1)
    )
    w_gate = gather_rows(
        jnp.concatenate([w_zx[:, 0, :], w_query, w_keyval.reshape(shard, -1)], axis=1)
    )
    w_out = gather_rows(jnp.concatenate([w_attn_out, w_mamba_out], axis=0).T)
    w_ffn = gather_rows(w_gate_up.reshape(shard, -1))
    w_back = gather_rows(w_down.T)
    cot_stack = gather_group(cotangent)

    small = gather_small(small)
    ends = [sum(small_sizes[: i + 1]) for i in range(len(small_sizes))]
    smalls = [small[:, end - size : end] for end, size in zip(ends, small_sizes)]
    gains = jnp.stack([smalls[0].reshape(-1), smalls[1].reshape(-1)], axis=0).astype(BF)
    gains = dot_nn(gains, perm)
    gain_in, gain_mid = gains[0:1], gains[1:2]
    taps_one = smalls[2].reshape((fsdp_size,) + taps_x.shape).transpose(1, 2, 0, 3)
    taps_one = padded(taps_one.reshape(taps_x.shape[0], -1), 8, scan_width)
    taps_two = smalls[3].reshape((fsdp_size,) + taps_bc.shape).transpose(1, 0, 2)
    taps_two = padded(taps_two.reshape(taps_bc.shape[0], -1), 8, bc_width)
    gain_flat = smalls[4].reshape((fsdp_size,) + gain_mamba.shape).transpose(1, 0, 2)
    gain_flat = gain_flat.reshape(1, -1)
    heads_pad = padded(head_params, 8, LANES)
    skip = jnp.repeat(head_params[2], HD)[None, :]

    x_rows = dot_nn(pick_rows(sources, token_stack), perm)
    cot_rows = dot_nn(pick_rows(sources, cot_stack), perm).astype(BF)
    inverse_in = inverse_norm(x_rows)
    unit_in = x_rows * inverse_in
    normed_in = (unit_in * gain_in).astype(BF)
    y_scan = dot_nn(normed_in, w_scan)
    y_gate = dot_nn(normed_in, w_gate)
    scan_args = (taps_one, taps_two, heads_pad, skip, segc, segr, posc)
    scan_out, states = scan_fwd(y_scan, scan_width, *scan_args)
    attn_args = (query_width, scan_width, cos_table, sin_table, segc, segr)
    attn_rows = attention_fwd(y_gate, *attn_args)
    gate_in = y_gate[:, :scan_width]
    sigma_in = jax.nn.sigmoid(gate_in)
    gated = scan_out * gate_in * sigma_in
    square_sum = jnp.sum(gated * gated, axis=1)
    square_sum = (square_sum + pair_swap(square_sum))[:, None]
    channels = scan_width * tp_size
    inverse_gate = lax.rsqrt(square_sum / channels + EPSILON)
    unit_gate = gated * inverse_gate
    mamba_rows = (unit_gate * gain_flat).astype(BF)
    branch_rows = jnp.concatenate([attn_rows, mamba_rows], axis=1)
    mixer = dot_nt(branch_rows, w_out).astype(BF)
    mixer = mixer.astype(F32) + pair_swap(mixer).astype(F32)
    hidden = x_rows + mixer
    inverse_mid = inverse_norm(hidden)
    unit_mid = hidden * inverse_mid
    normed_mid = (unit_mid * gain_mid).astype(BF)
    gate_up = dot_nn(normed_mid, w_ffn)
    gate_val, up_val = gate_up[:, :ffn_width], gate_up[:, ffn_width:]
    sigma = jax.nn.sigmoid(gate_val)
    activated = (gate_val * sigma * up_val).astype(BF)

    d_act = dot_nn(cot_rows, w_back)
    d_gate = d_act * up_val * sigma * (1.0 + gate_val * (1.0 - sigma))
    d_up = d_act * gate_val * sigma
    d_gate_up = jnp.concatenate([d_gate, d_up], axis=1).astype(BF)
    d_mid = dot_nt(d_gate_up, w_ffn).astype(BF)
    d_mid = d_mid.astype(F32) + pair_swap(d_mid).astype(F32)
    q_ffn = reduce_rows(dot_tn(normed_mid, d_gate_up).astype(BF))
    q_back = reduce_rows(dot_tn(cot_rows, activated).astype(BF))

    ffn_part = dot_nt(activated, w_back).astype(BF)
    ffn_own = lax.dynamic_slice_in_dim(ffn_part, own_start, tok_rows, 0).astype(F32)
    ffn_peer = pair_swap(lax.dynamic_slice_in_dim(ffn_part, peer_start, tok_rows, 0))
    hidden_own = lax.dynamic_slice_in_dim(hidden, own_start, tok_rows, 0)
    out_own = (hidden_own + ffn_own + ffn_peer.astype(F32)).astype(BF)
    out_stack = gather_group(dot_nt(out_own, perm).astype(BF))
    mixed_home = pick_rows(home_spots, out_stack)

    d_hidden = cot_rows.astype(F32) + norm_back(d_mid, unit_mid, inverse_mid, gain_mid)
    g_norm_mid = jnp.sum(d_mid * unit_mid, axis=0, keepdims=True)
    d_mix = d_hidden.astype(BF)
    d_branch = dot_nn(d_mix, w_out).astype(BF)
    q_out = reduce_rows(dot_tn(d_mix, branch_rows).astype(BF))
    d_attn = d_branch[:, :query_width]
    d_mamba = d_branch[:, query_width:].astype(F32)
    scaled_gate = d_mamba * gain_flat
    gate_stat = jnp.sum(scaled_gate * unit_gate, axis=1)
    gate_stat = (gate_stat + pair_swap(gate_stat))[:, None]
    d_query = attention_bwd(y_gate, *attn_args, d_attn)
    g_gain = jnp.sum(d_mamba * unit_gate, axis=0, keepdims=True)
    d_gated = inverse_gate * (scaled_gate - unit_gate * (gate_stat / channels))
    d_scan = d_gated * gate_in * sigma_in
    d_z = d_gated * scan_out * sigma_in * (1.0 + gate_in * (1.0 - sigma_in))
    dy_gate = jnp.concatenate([d_z.astype(BF), d_query], axis=1)
    q_gate = reduce_rows(dot_tn(normed_in, dy_gate).astype(BF))
    dy_scan, g_taps_one, g_taps_two, g_heads = scan_bwd(
        y_scan, scan_width, *scan_args, states, d_scan
    )
    d_in = (dot_nt(dy_gate, w_gate) + dot_nt(dy_scan, w_scan)).astype(BF)
    q_scan = reduce_rows(dot_tn(normed_in, dy_scan).astype(BF))
    d_in_own = lax.dynamic_slice_in_dim(d_in, own_start, tok_rows, 0).astype(F32)
    d_in_peer = pair_swap(lax.dynamic_slice_in_dim(d_in, peer_start, tok_rows, 0))
    d_in_own = d_in_own + d_in_peer.astype(F32)

    def own_rows(v):
        return lax.dynamic_slice_in_dim(v, own_start, tok_rows, 0)

    unit_own = own_rows(unit_in)
    grad_own = own_rows(d_hidden) + norm_back(d_in_own, unit_own, own_rows(inverse_in), gain_in)
    g_norm_in = jnp.sum(d_in_own * unit_own, axis=0, keepdims=True)
    grad_stack = gather_group(dot_nt(grad_own.astype(BF), perm).astype(BF))
    grad_home = pick_rows(home_spots, grad_stack)

    s_ffn = share_quarters(q_ffn)
    s_back = share_quarters(q_back)
    s_out = share_quarters(q_out)
    s_gate = share_quarters(q_gate)
    q_bc = q_scan[:, scan_width : scan_width + bc_width]
    q_bc = add_low(q_bc, pair_swap(q_bc))
    q_scan = jnp.concatenate(
        [q_scan[:, :scan_width], q_bc, q_scan[:, scan_width + bc_width :]], axis=1
    )
    s_scan = share_quarters(q_scan)
    g_norms = dot_nt(
        jnp.concatenate([g_norm_in, g_norm_mid], axis=0), perm.astype(F32), PRECISE
    )
    g_norms, g_taps_two = g_norms.reshape(-1), g_taps_two[: taps_bc.shape[0]].reshape(-1)
    g_taps_one = g_taps_one[: taps_x.shape[0]].reshape(-1)
    g_heads = g_heads[:3, :heads].reshape(-1)
    g_gain = g_gain.reshape(-1)
    parts = (g_norms[:model_width], g_taps_two, g_norms[model_width:], g_taps_one, g_heads, g_gain)
    paired = model_width + g_taps_two.shape[0]
    sums = reduce_small(jnp.concatenate(parts))
    sums = jnp.concatenate([sums[:paired] + pair_swap(sums[:paired]), sums[paired:]])
    ends = [sum(v.size for v in parts[: i + 1]) for i in range(len(parts))]
    sum_in, sum_two, sum_mid, sum_one, sum_heads, sum_gain = [
        sums[end - v.size : end] for end, v in zip(ends, parts)
    ]

    def shard_of(array, dim_index):
        piece = array.shape[dim_index] // fsdp_size
        return lax.dynamic_slice_in_dim(array, fsdp_index * piece, piece, dim_index)

    return (
        mixed_home,
        grad_home,
        shard_of(sum_in, 0),
        s_gate[:, scan_width : scan_width + query_width],
        s_gate[:, scan_width + query_width :].reshape(w_keyval.shape),
        s_out[:, :query_width].T,
        jnp.stack([s_gate[:, :scan_width], s_scan[:, :scan_width]], axis=1),
        s_scan[:, scan_width : scan_width + bc_width],
        s_scan[:, scan_width + bc_width :][:, : w_step.shape[1]],
        sum_heads.reshape(head_params.shape),
        shard_of(sum_one.reshape(taps_x.shape[0], heads, HD), 2),
        shard_of(sum_two.reshape(taps_bc.shape[0], -1), 1),
        shard_of(sum_gain.reshape(heads, HD), 1),
        s_out[:, query_width:].T,
        shard_of(sum_mid, 0),
        s_ffn.reshape(w_gate_up.shape),
        s_back.T,
    )


def solution(mesh):
    rows = P(("fsdp", "ctx", "tp"), None)
    in_specs = (
        rows,
        rows,
        P("fsdp", None),
        P("fsdp", None),
        P("fsdp"),
        P("fsdp", "tp"),
        P("fsdp", "tp", None),
        P("tp", "fsdp"),
        P("fsdp", None, "tp"),
        P("fsdp", None),
        P("fsdp", "tp"),
        P(None, "tp"),
        P(None, "tp", "fsdp"),
        P(None, "fsdp"),
        P("tp", "fsdp"),
        P("tp", "fsdp"),
        P("fsdp"),
        P("fsdp", None, "tp"),
        P("tp", "fsdp"),
    )
    out_specs = (
        rows,
        rows,
        P("fsdp"),
        P("fsdp", "tp"),
        P("fsdp", "tp", None),
        P("tp", "fsdp"),
        P("fsdp", None, "tp"),
        P("fsdp", None),
        P("fsdp", "tp"),
        P(None, "tp"),
        P(None, "tp", "fsdp"),
        P(None, "fsdp"),
        P("tp", "fsdp"),
        P("tp", "fsdp"),
        P("fsdp"),
        P("fsdp", None, "tp"),
        P("tp", "fsdp"),
    )
    return jax.shard_map(
        per_device, mesh=mesh, in_specs=in_specs, out_specs=out_specs, check_vma=False
    )
```

```python
import functools
import jax
import jax.numpy as jnp
from jax import lax
from jax.experimental import pallas as pl
from jax.experimental.pallas import tpu as pltpu
from jax.sharding import PartitionSpec as P

HD = 64
BLK = 128
LANES = 128
EPSILON = 1e-05
ROPE_BASE = 100000000000.0
PRECISE = lax.Precision.HIGHEST
F32 = jnp.float32
BF = jnp.bfloat16
FAR = -1e30


def dot_nn(a, b, precision=None):
    return lax.dot_general(
        a, b, (((1,), (0,)), ((), ())), precision=precision, preferred_element_type=F32
    )


def dot_nt(a, b, precision=None):
    return lax.dot_general(
        a, b, (((1,), (1,)), ((), ())), precision=precision, preferred_element_type=F32
    )


def dot_tn(a, b, precision=None):
    return lax.dot_general(
        a, b, (((0,), (0,)), ((), ())), precision=precision, preferred_element_type=F32
    )


def iota(shape, dim):
    return lax.broadcasted_iota(jnp.int32, shape, dim)


def swap_halves(v):
    lanes = v.shape[1]
    low = (iota(v.shape, 1) & (HD - 1)) < HD // 2
    return jnp.where(low, pltpu.roll(v, lanes - HD // 2, 1), pltpu.roll(v, HD // 2, 1))


def split_pair(v):
    first = iota(v.shape, 1) < HD
    zero = jnp.zeros_like(v)
    return jnp.concatenate([jnp.where(first, v, zero), jnp.where(first, zero, v)], axis=0)


def keys_values(kv, cos, sin):
    first = iota(kv.shape, 1) < HD
    roped = kv * cos + swap_halves(kv) * sin
    keys = jnp.where(first, roped, 0.0)
    values = jnp.where(first, 0.0, kv)
    key_pair = (keys.astype(BF), pltpu.roll(keys, HD, 1).astype(BF))
    value_pair = (pltpu.roll(values, HD, 1).astype(BF), values.astype(BF))
    return key_pair, value_pair


def attention_probs(query, key, allowed):
    scores = dot_nt(query, key) * HD ** (-0.5)
    scores = jnp.where(allowed, scores, FAR)
    weights = jnp.exp(scores - jnp.max(scores, axis=1, keepdims=True))
    return weights / jnp.sum(weights, axis=1, keepdims=True)


def allowed_rows(segc, segr, lower, count):
    keys = lower + count
    same = segc[lower:keys, :] == segr[:, :keys]
    return same & (iota((count, keys), 0) + lower >= iota((count, keys), 1))


def attention_fwd_kernel(q_ref, kv_ref, cos_ref, sin_ref, segc_ref, segr_ref, out_ref):
    rows, width = q_ref.shape
    cos, sin = cos_ref[...], sin_ref[...]
    key_pair, value_pair = keys_values(kv_ref[...], cos, sin)
    segc, segr = segc_ref[...], segr_ref[...]
    for pair in range(width // LANES):
        cols = slice(pair * LANES, (pair + 1) * LANES)
        raw = q_ref[:, cols]
        query = (raw * cos + swap_halves(raw) * sin).astype(BF)
        for lower in range(0, rows, BLK):
            keys = lower + BLK
            allowed = allowed_rows(segc, segr, lower, BLK)
            total = None
            for side in range(2):
                probs = attention_probs(query[lower:keys], key_pair[side][:keys], allowed)
                part = dot_nn(probs.astype(BF), value_pair[side][:keys])
                total = part if total is None else total + part
            out_ref[lower:keys, cols] = total.astype(BF)


def attention_bwd_kernel(
    q_ref, kv_ref, cos_ref, sin_ref, segc_ref, segr_ref, do_ref, out_ref, dk_ref, dv_ref
):
    rows, width = q_ref.shape
    cos, sin = cos_ref[...], sin_ref[...]
    key_pair, value_pair = keys_values(kv_ref[...], cos, sin)
    segc, segr = segc_ref[...], segr_ref[...]
    dk_ref[...] = jnp.zeros_like(dk_ref)
    dv_ref[...] = jnp.zeros_like(dv_ref)
    for pair in range(width // LANES):
        cols = slice(pair * LANES, (pair + 1) * LANES)
        raw = q_ref[:, cols]
        query = (raw * cos + swap_halves(raw) * sin).astype(BF)
        for lower in range(0, rows, BLK):
            keys = lower + BLK
            allowed = allowed_rows(segc, segr, lower, BLK)
            query_part = query[lower:keys]
            grad = do_ref[lower:keys, cols]
            d_query = None
            probs_all, scores_all = [], []
            for side in range(2):
                probs = attention_probs(query_part, key_pair[side][:keys], allowed)
                d_probs = dot_nt(grad, value_pair[side][:keys])
                inner = jnp.sum(d_probs * probs, axis=1, keepdims=True)
                d_scores = (probs * (d_probs - inner)).astype(BF)
                part = dot_nn(d_scores, key_pair[side][:keys])
                d_query = part if d_query is None else d_query + part
                probs_all.append(probs.astype(BF))
                scores_all.append(d_scores)
            dv_ref[:keys, :] += dot_tn(jnp.concatenate(probs_all, axis=0), split_pair(grad))
            dk_ref[:keys, :] += dot_tn(jnp.concatenate(scores_all, axis=0), split_pair(query_part))
            d_query = d_query * HD ** (-0.5)
            cos_part, sin_part = cos[lower:keys], sin[lower:keys]
            out_ref[lower:keys, cols] = (
                d_query * cos_part - swap_halves(d_query) * sin_part
            ).astype(BF)
    first = iota(dk_ref.shape, 1) < HD
    d_key = dk_ref[...]
    d_key = (d_key + pltpu.roll(d_key, HD, 1)) * HD ** (-0.5)
    d_key = d_key * cos - swap_halves(d_key) * sin
    d_value = dv_ref[...]
    d_value = d_value + pltpu.roll(d_value, HD, 1)
    out_ref[:, width:] = jnp.where(first, d_key, d_value).astype(BF)


def conv_rows(signal, taps_ref, position):
    total = taps_ref[4:5, :] + taps_ref[3:4, :] * signal
    for lag in range(1, 4):
        moved = jnp.where(position >= lag, pltpu.roll(signal, lag, 0), 0.0)
        total = total + taps_ref[3 - lag : 4 - lag, :] * moved
    return total


def conv_back(signal, d_pre, taps_ref, grad_ref, position):
    rows = signal.shape[0]
    grad_ref[...] = jnp.zeros_like(grad_ref)
    grad_ref[4:5, :] = jnp.sum(d_pre, axis=0, keepdims=True)
    grad_ref[3:4, :] = jnp.sum(d_pre * signal, axis=0, keepdims=True)
    total = taps_ref[3:4, :] * d_pre
    for lag in range(1, 4):
        kept = jnp.where(position >= lag, d_pre, 0.0)
        grad_ref[3 - lag : 4 - lag, :] = jnp.sum(
            kept * pltpu.roll(signal, lag, 0), axis=0, keepdims=True
        )
        total = total + taps_ref[3 - lag : 4 - lag, :] * pltpu.roll(kept, rows - lag, 0)
    return total


def softplus(v):
    return jnp.maximum(v, 0.0) + jnp.log1p(jnp.exp(-jnp.abs(v)))


def spread_matrix(width):
    shape = (LANES, width)
    return (iota(shape, 0) == (iota(shape, 1) >> 6)).astype(F32)


def scan_setup(step_ref, heads_ref):
    steps = softplus(step_ref[...] + heads_ref[0:1, :])
    rates = -jnp.exp(heads_ref[1:2, :])
    return steps, rates


def block_decays(steps, rates, segc, lower):
    upper = lower + BLK
    shape = (BLK, BLK)
    lower_ones = (iota(shape, 0) >= iota(shape, 1)).astype(F32)
    decays = dot_nn(lower_ones, steps[lower:upper] * rates, PRECISE)
    seg_part = segc[lower:upper]
    if lower == 0:
        arrive = None
    else:
        carried = seg_part == segc[lower - 1 : lower]
        arrive = jnp.where(carried, jnp.exp(decays), 0.0)
    kept = seg_part == segc[upper - 1 : upper]
    leave = jnp.where(kept, jnp.exp(decays[BLK - 1 : BLK] - decays), 0.0)
    return decays, arrive, leave, lower_ones


def block_mixing(decays, decays_t, head, allowed):
    gap = decays[:, head : head + 1] - decays_t[head : head + 1, :]
    return jnp.exp(jnp.where(allowed, gap, FAR))


def scan_fwd_kernel(
    x_ref, bc_ref, step_ref, tapx_ref, tapbc_ref, heads_ref, skip_ref, segc_ref, segr_ref,
    pos_ref, out_ref, states_ref,
):
    rows, width = x_ref.shape
    position = pos_ref[...]
    segc, segr = segc_ref[...], segr_ref[...]
    conv_x = jax.nn.silu(conv_rows(x_ref[...], tapx_ref, position)).astype(BF)
    conv_bc = jax.nn.silu(conv_rows(bc_ref[...], tapbc_ref, position)).astype(BF)
    steps, rates = scan_setup(step_ref, heads_ref)
    spread = spread_matrix(width)
    scaled = conv_x.astype(F32) * dot_nn(steps, spread, PRECISE)
    state = None
    for lower in range(0, rows, BLK):
        upper = lower + BLK
        b_part = conv_bc[lower:upper, :LANES]
        c_part = conv_bc[lower:upper, LANES:]
        decays, arrive, leave, lower_ones = block_decays(steps, rates, segc, lower)
        decays_t = decays.T
        allowed = (segc[lower:upper] == segr[:, lower:upper]) & (lower_ones > 0.0)
        inner = dot_nt(c_part, b_part)
        scaled_part = scaled[lower:upper]
        scaled_low = scaled_part.astype(BF)
        fresh = dot_tn(b_part, (scaled_part * dot_nn(leave, spread, PRECISE)).astype(BF))
        if state is None:
            recall = None
            states_ref[lower // BLK] = jnp.zeros(fresh.shape, F32)
            state = fresh
        else:
            arrive_wide = dot_nn(arrive, spread, PRECISE)
            recall = dot_nn(c_part, state.astype(BF)) * arrive_wide
            states_ref[lower // BLK] = state
            state = state * arrive_wide[BLK - 1 : BLK] + fresh
        for pair in range(width // LANES):
            cols = slice(pair * LANES, (pair + 1) * LANES)
            mixes = [
                (block_mixing(decays, decays_t, 2 * pair + side, allowed) * inner).astype(BF)
                for side in range(2)
            ]
            local = dot_nn(jnp.concatenate(mixes, axis=1), split_pair(scaled_low[:, cols]))
            if recall is not None:
                local = local + recall[:, cols]
            out_ref[lower:upper, cols] = local + skip_ref[0:1, cols] * conv_x[
                lower:upper, cols
            ].astype(F32)


def scan_bwd_kernel(
    x_ref, bc_ref, step_ref, tapx_ref, tapbc_ref, heads_ref, skip_ref, segc_ref, segr_ref,
    pos_ref, states_ref, dy_ref, out_ref, gtapx_ref, gtapbc_ref, gheads_ref, dx_ref, dbc_ref,
):
    rows, width = x_ref.shape
    position = pos_ref[...]
    segc, segr = segc_ref[...], segr_ref[...]
    pre_x = conv_rows(x_ref[...], tapx_ref, position)
    pre_bc = conv_rows(bc_ref[...], tapbc_ref, position)
    conv_x = jax.nn.silu(pre_x).astype(BF)
    conv_bc = jax.nn.silu(pre_bc).astype(BF)
    steps, rates = scan_setup(step_ref, heads_ref)
    spread = spread_matrix(width)
    steps_wide = dot_nn(steps, spread, PRECISE)
    lane = iota((BLK, LANES), 1)
    sub = iota((LANES, BLK), 0)
    last_row = iota((BLK, LANES), 0) == BLK - 1
    d_state = None
    g_bias = jnp.zeros((1, LANES), F32)
    g_rate = jnp.zeros((1, LANES), F32)
    g_skip = jnp.zeros((1, width), F32)
    for lower in range(rows - BLK, -1, -BLK):
        upper = lower + BLK
        b_part = conv_bc[lower:upper, :LANES]
        c_part = conv_bc[lower:upper, LANES:]
        decays, arrive, leave, lower_ones = block_decays(steps, rates, segc, lower)
        decays_t = decays.T
        allowed = (segc[lower:upper] == segr[:, lower:upper]) & (lower_ones > 0.0)
        inner = dot_nt(c_part, b_part)
        x_part = conv_x[lower:upper].astype(F32)
        scaled_part = x_part * steps_wide[lower:upper]
        scaled_low = scaled_part.astype(BF)
        grad = dy_ref[lower:upper, :]
        grad_low = grad.astype(BF)
        d_scaled = []
        d_inner = jnp.zeros((BLK, BLK), F32)
        row_sums = jnp.zeros((BLK, LANES), F32)
        col_sums = jnp.zeros((LANES, BLK), F32)
        for pair in range(width // LANES):
            cols = slice(pair * LANES, (pair + 1) * LANES)
            grad_pair = split_pair(grad_low[:, cols])
            d_mix = dot_nt(grad_pair, scaled_low[:, cols])
            mixes = []
            for side in range(2):
                head = 2 * pair + side
                mixing = block_mixing(decays, decays_t, head, allowed)
                mix = mixing * inner
                d_part = d_mix[side * BLK : (side + 1) * BLK]
                d_inner = d_inner + d_part * mixing
                both = d_part * mix
                row_sums = jnp.where(lane == head, jnp.sum(both, axis=1, keepdims=True), row_sums)
                col_sums = jnp.where(sub == head, jnp.sum(both, axis=0, keepdims=True), col_sums)
                mixes.append(mix.astype(BF))
            d_scaled.append(dot_tn(jnp.concatenate(mixes, axis=0), grad_pair))
        d_scaled = jnp.concatenate(d_scaled, axis=1)
        d_decays = row_sums - col_sums.T
        d_inner = d_inner.astype(BF)
        d_c = dot_nn(d_inner, b_part)
        d_b = dot_tn(d_inner, c_part)
        if lower > 0:
            arrive_wide = dot_nn(arrive, spread, PRECISE)
            state = states_ref[lower // BLK]
            state_low = state.astype(BF)
            recall = dot_nn(c_part, state_low) * arrive_wide
            d_decays = d_decays + dot_nt(recall * grad, spread, PRECISE)
            grad_in = (grad * arrive_wide).astype(BF)
            d_c = d_c + dot_nt(grad_in, state_low)
        if d_state is not None:
            state_grad = d_state.astype(BF)
            leave_wide = dot_nn(leave, spread, PRECISE)
            d_kept = dot_nn(b_part, state_grad) * leave_wide
            d_b = d_b + dot_nt((scaled_part * leave_wide).astype(BF), state_grad)
            d_leave = dot_nt(d_kept * scaled_part, spread, PRECISE)
            d_last = jnp.sum(d_leave, axis=0, keepdims=True)
            if lower > 0:
                lingering = jnp.sum(d_state * state, axis=0, keepdims=True)
                lingering = lingering * arrive_wide[BLK - 1 : BLK]
                d_last = d_last + dot_nt(
                    jnp.broadcast_to(lingering, (8, width)), spread, PRECISE
                )[0:1]
            d_decays = d_decays - d_leave + jnp.where(last_row, d_last, 0.0)
            d_scaled = d_scaled + d_kept
        if lower > 0:
            d_new = dot_tn(c_part, grad_in)
            if d_state is None:
                d_state = d_new
            else:
                d_state = d_state * arrive_wide[BLK - 1 : BLK] + d_new
        d_log = dot_tn(lower_ones, d_decays, PRECISE)
        steps_part = steps[lower:upper]
        d_steps = dot_nt(d_scaled * x_part, spread, PRECISE) + d_log * rates
        d_step_in = d_steps * jax.nn.sigmoid(step_ref[lower:upper, :] + heads_ref[0:1, :])
        g_bias = g_bias + jnp.sum(d_step_in, axis=0, keepdims=True)
        g_rate = g_rate + jnp.sum(d_log * steps_part, axis=0, keepdims=True) * rates
        g_skip = g_skip + jnp.sum(grad * x_part, axis=0, keepdims=True)
        out_ref[lower:upper, width + 2 * LANES :] = d_step_in.astype(BF)
        dx_ref[lower:upper, :] = d_scaled * steps_wide[lower:upper] + grad * skip_ref[0:1, :]
        dbc_ref[lower:upper, :LANES] = d_b
        dbc_ref[lower:upper, LANES:] = d_c
    gheads_ref[...] = jnp.zeros_like(gheads_ref)
    gheads_ref[0:1, :] = g_bias
    gheads_ref[1:2, :] = g_rate
    gheads_ref[2:3, :] = dot_nt(jnp.broadcast_to(g_skip, (8, width)), spread, PRECISE)[0:1]
    gate = jax.nn.sigmoid(pre_x)
    d_pre = dx_ref[...] * gate * (1.0 + pre_x * (1.0 - gate))
    out_ref[:, :width] = conv_back(x_ref[...], d_pre, tapx_ref, gtapx_ref, position).astype(BF)
    gate = jax.nn.sigmoid(pre_bc)
    d_pre = dbc_ref[...] * gate * (1.0 + pre_bc * (1.0 - gate))
    out_ref[:, width : width + 2 * LANES] = conv_back(
        bc_ref[...], d_pre, tapbc_ref, gtapbc_ref, position
    ).astype(BF)


def select_parts(spot_ref, part_refs):
    spots = spot_ref[...]
    total, first = None, 0
    for part_ref in part_refs:
        shape = (spots.shape[0], part_ref.shape[0])
        chosen = (spots == iota(shape, 1) + first).astype(F32).astype(BF)
        product = dot_nn(chosen, part_ref[...])
        total = product if total is None else total + product
        first += part_ref.shape[0]
    return total


def pick_kernel(spot_ref, *refs):
    refs[-1][...] = select_parts(spot_ref, refs[:-1]).astype(BF)


def pick_turn_kernel(spot_ref, perm_ref, *refs):
    rows = select_parts(spot_ref, refs[:-1]).astype(BF)
    refs[-1][...] = dot_nn(rows, perm_ref[...]).astype(BF)


def pick_norm_kernel(spot_ref, perm_ref, gain_ref, *refs):
    rows_ref, normed_ref, inverse_ref = refs[-3:]
    rows = select_parts(spot_ref, refs[:-3]).astype(BF)
    rows = dot_nn(rows, perm_ref[...])
    inverse = lax.rsqrt(jnp.mean(rows * rows, axis=1, keepdims=True) + EPSILON)
    rows_ref[...] = rows.astype(BF)
    normed_ref[...] = (rows * inverse * gain_ref[...]).astype(BF)
    inverse_ref[...] = inverse


def join_kernel(*refs):
    start = 0
    for ref in refs[:-1]:
        refs[-1][start : start + ref.shape[0], :] = ref[...]
        start += ref.shape[0]


def ffn_kernel(
    normed_ref, cot_ref, near_ref, far_ref, back_near_ref, back_far_ref, act_ref, grad_ref, mid_ref
):
    half = near_ref.shape[0]
    width = act_ref.shape[1]
    tile = 512
    total = [None, None]
    for first in range(0, width, tile):
        gate_cols = slice(first, first + tile)
        up_cols = slice(width + first, width + first + tile)

        def product(left_ref, near, far, cols):
            return dot_nn(left_ref[:, :half], near[:, cols]) + dot_nn(
                left_ref[:, half:], far[:, cols]
            )

        gate = product(normed_ref, near_ref, far_ref, gate_cols)
        up = product(normed_ref, near_ref, far_ref, up_cols)
        d_act = product(cot_ref, back_near_ref, back_far_ref, gate_cols)
        sigma = jax.nn.sigmoid(gate)
        silu = gate * sigma
        act_ref[:, gate_cols] = (silu * up).astype(BF)
        d_gate = (d_act * up * sigma * (1.0 + gate * (1.0 - sigma))).astype(BF)
        d_up = (d_act * silu).astype(BF)
        grad_ref[:, gate_cols] = d_gate
        grad_ref[:, up_cols] = d_up
        for i, ref in enumerate((near_ref, far_ref)):
            part = dot_nt(d_gate, ref[:, gate_cols]) + dot_nt(d_up, ref[:, up_cols])
            total[i] = part if total[i] is None else total[i] + part
    mid_ref[:, :half] = total[0].astype(BF)
    mid_ref[:, half:] = total[1].astype(BF)


def project_kernel(rows_ref, near_ref, far_ref, *outs):
    half = near_ref.shape[0]
    first = 0
    for out_ref in outs:
        cols = slice(first, first + out_ref.shape[1])
        out_ref[...] = dot_nn(rows_ref[:, :half], near_ref[:, cols]) + dot_nn(
            rows_ref[:, half:], far_ref[:, cols]
        )
        first += out_ref.shape[1]


def turn_back_kernel(rows_ref, near_ref, far_ref, out_ref):
    half = near_ref.shape[0]
    out_ref[...] = (
        dot_nn(rows_ref[:, :half], near_ref[...]) + dot_nn(rows_ref[:, half:], far_ref[...])
    ).astype(BF)


def unproject_kernel(count, *refs):
    out_ref = refs[-1]
    half = refs[count].shape[0]
    for side in range(2):
        total = None
        for i in range(count):
            part = dot_nt(refs[i][...], refs[count + 2 * i + side][...])
            total = part if total is None else total + part
        out_ref[:, side * half : (side + 1) * half] = total.astype(BF)


VMEM_BYTES = 48 * 1024 * 1024


def column_block(rows, width, index):
    return pl.BlockSpec((rows, width), lambda i: (0, index))


def whole_block(shape):
    zeros = (0,) * len(shape)
    return pl.BlockSpec(shape, lambda i: zeros)


def single_step(kernel, in_specs, outs, scratch=(), flops=1024):
    return pl.pallas_call(
        kernel,
        grid=(1,),
        in_specs=in_specs,
        out_specs=[whole_block(o.shape) for o in outs],
        out_shape=outs,
        scratch_shapes=list(scratch),
        compiler_params=pltpu.CompilerParams(vmem_limit_bytes=VMEM_BYTES),
        cost_estimate=pl.CostEstimate(flops=flops, bytes_accessed=1024, transcendentals=0),
    )


def attention_specs(rows, width, gate_width):
    return [
        column_block(rows, width, gate_width // width),
        column_block(rows, LANES, (gate_width + width) // LANES),
        whole_block((rows, LANES)),
        whole_block((rows, LANES)),
        whole_block((rows, 1)),
        whole_block((1, rows)),
    ]


def attention_fwd(y_a, width, gate_width, cos, sin, segc, segr):
    rows = y_a.shape[0]
    return single_step(
        attention_fwd_kernel,
        attention_specs(rows, width, gate_width),
        [jax.ShapeDtypeStruct((rows, width), BF)],
    )(y_a, y_a, cos, sin, segc, segr)[0]


def attention_bwd(y_a, width, gate_width, cos, sin, segc, segr, d_attn):
    rows = y_a.shape[0]
    return single_step(
        attention_bwd_kernel,
        attention_specs(rows, width, gate_width) + [whole_block((rows, width))],
        [jax.ShapeDtypeStruct((rows, width + LANES), BF)],
        [pltpu.VMEM((rows, LANES), F32), pltpu.VMEM((rows, LANES), F32)],
    )(y_a, y_a, cos, sin, segc, segr, d_attn)[0]


def scan_specs(rows, width):
    return [
        column_block(rows, width, 0),
        column_block(rows, 2 * LANES, width // (2 * LANES)),
        column_block(rows, LANES, (width + 2 * LANES) // LANES),
        whole_block((8, width)),
        whole_block((8, 2 * LANES)),
        whole_block((8, LANES)),
        whole_block((1, width)),
        whole_block((rows, 1)),
        whole_block((1, rows)),
        whole_block((rows, 1)),
    ]


def scan_fwd(y_b, width, taps_x, taps_bc, heads, skip, segc, segr, position):
    rows = y_b.shape[0]
    return single_step(
        scan_fwd_kernel,
        scan_specs(rows, width),
        [
            jax.ShapeDtypeStruct((rows, width), F32),
            jax.ShapeDtypeStruct((rows // BLK, LANES, width), F32),
        ],
    )(y_b, y_b, y_b, taps_x, taps_bc, heads, skip, segc, segr, position)


def scan_bwd(y_b, width, taps_x, taps_bc, heads, skip, segc, segr, position, states, d_out):
    rows = y_b.shape[0]
    return single_step(
        scan_bwd_kernel,
        scan_specs(rows, width)
        + [whole_block(states.shape), whole_block((rows, width))],
        [
            jax.ShapeDtypeStruct(y_b.shape, BF),
            jax.ShapeDtypeStruct((8, width), F32),
            jax.ShapeDtypeStruct((8, 2 * LANES), F32),
            jax.ShapeDtypeStruct((8, LANES), F32),
        ],
        [pltpu.VMEM((rows, width), F32), pltpu.VMEM((rows, 2 * LANES), F32)],
    )(y_b, y_b, y_b, taps_x, taps_bc, heads, skip, segc, segr, position, states, d_out)


def pick_rows(spots, parts):
    operands = (spots[:, None],) + tuple(parts)
    return single_step(
        pick_kernel,
        [whole_block(v.shape) for v in operands],
        [jax.ShapeDtypeStruct((spots.shape[0], parts[0].shape[1]), BF)],
    )(*operands)[0]


def pick_turned(spots, perm, parts):
    operands = (spots[:, None], perm) + tuple(parts)
    return single_step(
        pick_turn_kernel,
        [whole_block(v.shape) for v in operands],
        [jax.ShapeDtypeStruct((spots.shape[0], perm.shape[1]), BF)],
    )(*operands)[0]


def pick_normed(spots, perm, gain, parts):
    rows = spots.shape[0]
    operands = (spots[:, None], perm, gain) + tuple(parts)
    wide = jax.ShapeDtypeStruct((rows, perm.shape[1]), BF)
    return single_step(
        pick_norm_kernel,
        [whole_block(v.shape) for v in operands],
        [wide, wide, jax.ShapeDtypeStruct((rows, 1), F32)],
    )(*operands)


def join_blocks(operands, specs, width):
    rows = sum(spec.block_shape[0] for spec in specs)
    return single_step(join_kernel, specs, [jax.ShapeDtypeStruct((rows, width), BF)])(*operands)[0]


def ffn_both_ways(normed, cot_rows, near, far, back_near, back_far, width, back_index):
    rows, model_width = normed.shape
    half = near.shape[0]
    return single_step(
        ffn_kernel,
        [whole_block(normed.shape), whole_block(cot_rows.shape)]
        + [whole_block(near.shape), whole_block(far.shape)]
        + [column_block(half, width, back_index), column_block(half, width, back_index)],
        [
            jax.ShapeDtypeStruct((rows, width), BF),
            jax.ShapeDtypeStruct((rows, 2 * width), BF),
            jax.ShapeDtypeStruct((rows, model_width), BF),
        ],
    )(normed, cot_rows, near, far, back_near, back_far)


def project(rows, near, far, width):
    count = near.shape[1] // width
    shape = jax.ShapeDtypeStruct((rows.shape[0], width), F32)
    operands = (rows, near, far)
    return single_step(
        project_kernel, [whole_block(v.shape) for v in operands], [shape] * count
    )(*operands)


def turn_back(rows, near, far, width):
    half = near.shape[0]
    return single_step(
        turn_back_kernel,
        [whole_block(rows.shape), column_block(half, width, 0), column_block(half, width, 0)],
        [jax.ShapeDtypeStruct((rows.shape[0], width), BF)],
    )(rows, near, far)[0]


def unproject(lefts, blocks):
    specs = [whole_block(v.shape) for v in lefts]
    operands = list(lefts)
    for left, (near, far, index) in zip(lefts, blocks):
        specs += [column_block(near.shape[0], left.shape[1], index)] * 2
        operands += [near, far]
    rows, half = lefts[0].shape[0], blocks[0][0].shape[0]
    return single_step(
        functools.partial(unproject_kernel, len(lefts)),
        specs,
        [jax.ShapeDtypeStruct((rows, 2 * half), BF)],
    )(*operands)[0]


CORE_SWAP = [(0, 1), (1, 0), (2, 3), (3, 2)]
CHIP_SWAP = [(0, 2), (2, 0), (1, 3), (3, 1)]
PAIR_SWAP = [(0, 1), (1, 0)]
def core_swap(v):
    return lax.ppermute(v, "ctx", CORE_SWAP)


def chip_swap(v):
    return lax.ppermute(v, "ctx", CHIP_SWAP)


def pair_swap(v):
    return lax.ppermute(v, "tp", PAIR_SWAP)


def shard_swap(v, gap):
    size = lax.axis_size("fsdp")
    return lax.ppermute(v, "fsdp", [(i, i ^ gap) for i in range(size)])


def quarter_perm(width):
    size = lax.axis_size("fsdp")
    shard = width // size
    piece = shard // 4
    spots = jnp.arange(width, dtype=jnp.int32)
    slot = spots // (size * piece)
    turn = (spots // piece) % size
    within = spots % piece
    quarter = jnp.where(slot == 1, 2, jnp.where(slot == 2, 1, slot)) ^ lax.axis_index("ctx")
    owner = lax.axis_index("fsdp") ^ turn
    column = owner * shard + quarter * piece + within
    return (spots[:, None] == column[None, :]).astype(BF)


def after(v, *others):
    return lax.optimization_barrier((v,) + others)[0]


def own_quarters(shard, sideways=False):
    index = lax.axis_index("ctx")
    if sideways:
        count = shard.shape[1]
        piece = count // 4
        place = jnp.arange(2 * piece, dtype=jnp.int32)
        column = (index ^ (2 * (place // piece))) * piece + place % piece
        chosen = (jnp.arange(count, dtype=jnp.int32)[None, :] == column[:, None]).astype(BF)
        both = dot_nt(chosen, shard).astype(BF)
        return both[:piece], both[piece:]
    piece = shard.shape[0] // 4
    return tuple(
        lax.dynamic_slice_in_dim(shard, (index ^ gap) * piece, piece, 0) for gap in (0, 2)
    )


def stage(*values):
    return lax.optimization_barrier(values)


def gather_near(own):
    line, gap = own, 1
    while 2 * gap < lax.axis_size("fsdp"):
        line = jnp.concatenate([line, shard_swap(line, gap)], axis=0)
        gap *= 2
    return line


def gather_far(near):
    return shard_swap(near, lax.axis_size("fsdp") // 2)


def swap_line(near, far):
    piece = near.shape[0] * 2 // lax.axis_size("fsdp")
    return chip_swap(jnp.concatenate([near[piece:], far], axis=0))


def join_half(*parts):
    specs = [whole_block(v.shape) for v in parts]
    return join_blocks(parts, specs, parts[0].shape[1])


def order_shards(rows):
    owner = jnp.arange(rows.shape[0], dtype=jnp.int32)
    turn = lax.axis_index("fsdp") ^ owner
    return dot_nn((turn[:, None] == owner[None, :]).astype(BF), rows)


def add_low(left, right):
    return (left.astype(F32) + right.astype(F32)).astype(BF)


def grad_halves(left, right):
    half = left.shape[1] // 2
    return tuple(dot_tn(v, right).astype(BF) for v in (left[:, :half], left[:, half:]))


def add_parts(keeps, others, rows):
    return jnp.concatenate(
        [add_low(keep[rows], other[rows]) for keep, other in zip(keeps, others)], axis=1
    )


def halves(v):
    half = v.shape[0] // 2
    return v[:half], v[half:]


def assemble(pair, others):
    by_gap = (pair[0], others[0], pair[1], others[1])
    index = lax.axis_index("ctx")
    core_bit, chip_bit = (index & 1) == 1, (index & 2) == 2
    rows = []
    for quarter in range(4):
        near = jnp.where(core_bit, by_gap[quarter ^ 1], by_gap[quarter])
        far = jnp.where(core_bit, by_gap[quarter ^ 3], by_gap[quarter ^ 2])
        rows.append(jnp.where(chip_bit, far, near))
    return jnp.concatenate(rows, axis=0).astype(F32)


def reduce_small(v):
    v = v + core_swap(v)
    v = v + chip_swap(v)
    gap = 1
    while gap < lax.axis_size("fsdp"):
        v = v + shard_swap(v, gap)
        gap *= 2
    return v


def direct_near(rows):
    near = [rows, chip_swap(rows), pair_swap(rows)]
    return near + [lax.ppermute(rows, ("ctx", "tp"), [(i, i ^ 5) for i in range(8)])]


def stack_spot(spot, rows):
    member = spot // rows
    gap = (member // 2) ^ lax.axis_index("ctx")
    turn = (member % 2) ^ lax.axis_index("tp")
    return ((gap & 1) * 4 + turn * 2 + (gap >> 1)) * rows + spot % rows


def dealt_order(lengths, dealing):
    numbers = jnp.arange(lengths.shape[0], dtype=jnp.int32)
    given_start = jnp.cumsum(lengths, dtype=jnp.int32) - lengths
    chosen = (dealing[:, None] == numbers[None, :]).astype(jnp.int32)
    dealt_len = jnp.sum(chosen * lengths[None, :], axis=1, dtype=jnp.int32)
    dealt_from = jnp.sum(chosen * given_start[None, :], axis=1, dtype=jnp.int32)
    dealt_start = jnp.cumsum(dealt_len, dtype=jnp.int32) - dealt_len
    return dealt_len, dealt_from, dealt_start


def look_up(spots, starts, counts, *tables):
    inside = (
        (spots[:, None] >= starts[None, :]) & (spots[:, None] < (starts + counts)[None, :])
    ).astype(jnp.int32)
    return [jnp.sum(inside * table[None, :], axis=1, dtype=jnp.int32) for table in tables]


def norm_back(grad_out, unit_rows, inverse, gain):
    scaled = grad_out * gain
    return inverse * (scaled - unit_rows * jnp.mean(scaled * unit_rows, axis=1, keepdims=True))


def inverse_norm(rows):
    return lax.rsqrt(jnp.mean(rows * rows, axis=1, keepdims=True) + EPSILON)


def padded(v, rows, cols):
    return jnp.pad(v, ((0, rows - v.shape[0]), (0, cols - v.shape[1])))


def per_device(
    tokens,
    cotangent,
    lengths,
    dealing,
    norm_in,
    w_query,
    w_keyval,
    w_attn_out,
    w_zx,
    w_bc,
    w_step,
    head_params,
    taps_x,
    taps_bc,
    gain_mamba,
    w_mamba_out,
    norm_mid,
    w_gate_up,
    w_down,
):
    tok_rows, model_width = tokens.shape
    tp_size = lax.axis_size("tp")
    fsdp_size = lax.axis_size("fsdp")
    rank_rows = tok_rows * tp_size
    tp_index = lax.axis_index("tp")
    fsdp_index = lax.axis_index("fsdp")
    ctx_index = lax.axis_index("ctx")
    shard = w_query.shape[0]
    heads = head_params.shape[1]
    scan_width = heads * HD
    query_width = w_query.shape[1]
    bc_width = w_bc.shape[1]
    ffn_width = w_gate_up.shape[2]
    own_start = tp_index * tok_rows
    peer_start = (tp_size - 1) * tok_rows - own_start

    dealt_len, dealt_from, dealt_start = dealt_order(lengths[0], dealing[0])
    numbers = jnp.arange(lengths.shape[1], dtype=jnp.int32)
    spots = ctx_index * rank_rows + jnp.arange(rank_rows, dtype=jnp.int32)
    segment, begins, anchor = look_up(
        spots, dealt_start, dealt_len, numbers, dealt_start, dealt_from
    )
    position = spots - begins
    sources = stack_spot(anchor + position, tok_rows)
    home = (ctx_index * tp_size + tp_index) * tok_rows + jnp.arange(tok_rows, dtype=jnp.int32)
    home_dealt, home_given = look_up(home, dealt_from, dealt_len, dealt_start, dealt_from)
    home_spots = stack_spot(home - home_given + home_dealt, tok_rows)
    segc, segr, posc = segment[:, None], segment[None, :], position[:, None]
    half_width = HD // 2
    freqs = ROPE_BASE ** (-jnp.arange(half_width, dtype=jnp.float32) / half_width)
    angles = position.astype(jnp.float32)[:, None] * freqs[None, :]
    cosine, sine = jnp.cos(angles), jnp.sin(angles)
    cos_table = jnp.concatenate([cosine] * 4, axis=1)
    sin_table = jnp.concatenate([-sine, sine, -sine, sine], axis=1)
    perm = lax.optimization_barrier(quarter_perm(model_width))

    small = (norm_in, norm_mid, taps_x, taps_bc, gain_mamba)
    small_sizes = [v.size for v in small]
    piece = shard // 4
    small = jnp.concatenate([v.reshape(-1) for v in small]).reshape(piece, -1)
    small_width = small.shape[1]
    free = LANES - heads - small_width
    wide = scan_width + 2 * LANES + LANES

    def in_quarter(gap):
        def rows_of(v):
            return lax.dynamic_slice_in_dim(v, (ctx_index ^ gap) * piece, piece, 0)

        zx = rows_of(w_zx)
        parts = [zx[:, 1, :], rows_of(w_bc), rows_of(w_step), small]
        parts += [jnp.zeros((piece, free), BF), zx[:, 0, :], rows_of(w_query)]
        return jnp.concatenate(parts + [rows_of(w_keyval).reshape(piece, -1)], axis=1)

    in_own, in_twin = in_quarter(0), in_quarter(2)
    token_near = direct_near(tokens)
    cot_pair = jnp.concatenate([cotangent, chip_swap(cotangent)], axis=0)
    in_near = gather_near(in_own)
    in_far = gather_far(in_near)
    q_out = own_quarters(jnp.concatenate([w_attn_out, w_mamba_out], axis=0), True)
    q_back = own_quarters(w_down, True)
    q_late = [jnp.concatenate([q_out[i], q_back[i]], axis=1) for i in range(2)]
    late_near = gather_near(q_late[0])
    q_ffn = own_quarters(w_gate_up.reshape(shard, -1))
    places = (sources, home_spots, segc, segr, posc, cos_table, sin_table, perm)
    token_stack = token_near + [core_swap(v) for v in token_near]
    ffn_near = gather_near(q_ffn[0])
    places, token_stack, cot_pair, in_near, in_far, in_twin, late_near, ffn_near, twins = stage(
        places, token_stack, cot_pair, in_near, in_far, in_twin, late_near, ffn_near,
        (q_late[1], q_ffn[1]),
    )
    sources, home_spots, segc, segr, posc, cos_table, sin_table, perm = places

    in_across = swap_line(in_near, in_far)
    cot_near = [cot_pair, pair_swap(cot_pair)]
    late_far = gather_far(late_near)
    small_cols = slice(wide - LANES + heads, wide - free)
    small = jnp.concatenate([in_near[:, small_cols], in_far[:, small_cols]], axis=0)
    small = order_shards(small.reshape(fsdp_size, -1))
    ends = [sum(small_sizes[: i + 1]) for i in range(len(small_sizes))]
    smalls = [small[:, end - size : end] for end, size in zip(ends, small_sizes)]
    gains = jnp.stack([smalls[0].reshape(-1), smalls[1].reshape(-1)], axis=0).astype(BF)
    gains = dot_nn(gains, perm)
    gain_in, gain_mid = gains[0:1], gains[1:2]
    taps_one = smalls[2].reshape((fsdp_size,) + taps_x.shape).transpose(1, 2, 0, 3)
    taps_one = padded(taps_one.reshape(taps_x.shape[0], -1), 8, scan_width)
    taps_two = smalls[3].reshape((fsdp_size,) + taps_bc.shape).transpose(1, 0, 2)
    taps_two = padded(taps_two.reshape(taps_bc.shape[0], -1), 8, bc_width)
    gain_flat = smalls[4].reshape((fsdp_size,) + gain_mamba.shape).transpose(1, 0, 2)
    gain_flat = gain_flat.reshape(1, -1)
    heads_pad = padded(head_params, 8, LANES)
    skip = jnp.repeat(head_params[2], HD)[None, :]

    scan_args = (taps_one, taps_two, heads_pad, skip, segc, segr, posc)
    x_low, normed_in, inverse_in = pick_normed(sources, perm, gain_in, token_stack)
    in_across, normed_in, gain_mid, gain_flat, scan_args, late_far, cot_near = stage(
        in_across, normed_in, gain_mid, gain_flat, scan_args, late_far, cot_near
    )

    in_half = join_half(in_near, in_far, in_twin, in_across)
    in_other = core_swap(in_half)
    late_across = swap_line(late_near, late_far)
    ffn_far = gather_far(ffn_near)
    y_scan, y_gate = project(normed_in, in_half, in_other, wide)
    scan_out, states = scan_fwd(y_scan, scan_width, *scan_args)
    attn_args = (query_width, scan_width, cos_table, sin_table, segc, segr)
    attn_rows = attention_fwd(y_gate, *attn_args)
    scan_out, attn_rows, late_across, ffn_far = stage(
        scan_out, attn_rows, late_across, ffn_far
    )

    late_half = join_half(late_near, late_far, twins[0], late_across)
    late_other = core_swap(late_half)
    out_width = query_width + scan_width
    ffn_across = swap_line(ffn_near, ffn_far)
    gate_in = y_gate[:, :scan_width]
    sigma_in = jax.nn.sigmoid(gate_in)
    gated = scan_out * gate_in * sigma_in
    square_sum = jnp.sum(gated * gated, axis=1)
    square_sum = (square_sum + pair_swap(square_sum))[:, None]
    channels = scan_width * tp_size
    inverse_gate = lax.rsqrt(square_sum / channels + EPSILON)
    unit_gate = gated * inverse_gate
    mamba_rows = (unit_gate * gain_flat).astype(BF)
    branch_rows = jnp.concatenate([attn_rows, mamba_rows], axis=1)
    mixer = unproject([branch_rows], [(late_half, late_other, 0)])
    mixer_peer = pair_swap(mixer)
    ffn_half = join_half(ffn_near, ffn_far, twins[1], after(ffn_across, mixer))
    ffn_other = core_swap(ffn_half)
    cot_stack = cot_near + [core_swap(v) for v in cot_near]
    cot_rows = pick_turned(sources, perm, after(cot_stack, mixer))
    mixer, mixer_peer, ffn_other, cot_rows = stage(mixer, mixer_peer, ffn_other, cot_rows)
    hidden = x_low.astype(F32) + (mixer.astype(F32) + mixer_peer.astype(F32))

    inverse_mid = inverse_norm(hidden)
    unit_mid = hidden * inverse_mid
    normed_mid = (unit_mid * gain_mid).astype(BF)
    activated, d_gate_up, d_mid = ffn_both_ways(
        normed_mid, cot_rows, ffn_half, ffn_other, late_half, late_other, ffn_width, 1
    )

    d_mid_peer = pair_swap(d_mid)
    ffn_keep, ffn_send = grad_halves(normed_mid, d_gate_up)
    back_keep, back_send = grad_halves(cot_rows, activated)
    late_keeps = (ffn_keep, back_keep)
    late_others = core_swap(ffn_send), core_swap(back_send)
    quarter_rows = fsdp_size * piece
    far_sum = add_parts(late_keeps, late_others, slice(quarter_rows, 2 * quarter_rows))
    near_sum = add_parts(late_keeps, late_others, slice(0, quarter_rows))
    far_recv = chip_swap(far_sum)
    ffn_part = unproject([activated], [(late_half, late_other, 1)])
    d_mid, d_mid_peer, near_sum, far_sum, ffn_part = stage(
        d_mid, d_mid_peer, near_sum, far_sum, ffn_part
    )
    d_mid = d_mid.astype(F32) + d_mid_peer.astype(F32)

    ffn_own = lax.dynamic_slice_in_dim(ffn_part, own_start, tok_rows, 0).astype(F32)
    ffn_peer = pair_swap(lax.dynamic_slice_in_dim(ffn_part, peer_start, tok_rows, 0))
    d_hidden = cot_rows.astype(F32) + norm_back(d_mid, unit_mid, inverse_mid, gain_mid)
    g_norm_mid = jnp.sum(d_mid * unit_mid, axis=0, keepdims=True)
    d_mix = d_hidden.astype(BF)
    d_branch = turn_back(d_mix, late_half, late_other, out_width)
    out_keep, out_send = grad_halves(d_mix, branch_rows)
    out_other = core_swap(out_send)
    d_attn = d_branch[:, :query_width]
    d_mamba = d_branch[:, query_width:].astype(F32)
    scaled_gate = d_mamba * gain_flat
    gate_stat = jnp.sum(scaled_gate * unit_gate, axis=1)
    gate_stat = (gate_stat + pair_swap(gate_stat))[:, None]
    g_gain = jnp.sum(d_mamba * unit_gate, axis=0, keepdims=True)
    d_gated = inverse_gate * (scaled_gate - unit_gate * (gate_stat / channels))
    d_scan = d_gated * gate_in * sigma_in
    d_z = d_gated * scan_out * sigma_in * (1.0 + gate_in * (1.0 - sigma_in))
    out_keep, out_far = halves(add_low(out_keep, out_other))
    out_far = chip_swap(out_far)
    late_sum, late_rest = halves(add_low(near_sum, far_recv))
    d_scan, late_sum, late_rest = stage(d_scan, late_sum, late_rest)
    late_recv = shard_swap(late_rest, fsdp_size // 2)
    dy_scan, g_taps_one, g_taps_two, g_heads = scan_bwd(
        y_scan, scan_width, *scan_args, states, d_scan
    )
    hidden_own = lax.dynamic_slice_in_dim(hidden, own_start, tok_rows, 0)
    out_own = (hidden_own + ffn_own + after(ffn_peer, dy_scan).astype(F32)).astype(BF)
    out_own = dot_nt(out_own, perm).astype(BF)
    bc_cols = slice(scan_width, scan_width + bc_width)
    d_bc_peer = pair_swap(dy_scan[:, bc_cols])
    d_query = attention_bwd(y_gate, *attn_args, after(d_attn, dy_scan))
    dy_gate = jnp.concatenate([d_z.astype(BF), d_query], axis=1)
    dy_scan, dy_gate, d_bc_peer, out_far, out_keep, out_own, late_recv = stage(
        dy_scan, dy_gate, d_bc_peer, out_far, out_keep, out_own, late_recv
    )

    d_in = unproject([dy_scan, dy_gate], [(in_half, in_other, 0), (in_half, in_other, 1)])
    d_in_peer = pair_swap(lax.dynamic_slice_in_dim(d_in, peer_start, tok_rows, 0))
    d_bc = add_low(dy_scan[:, bc_cols], d_bc_peer)
    dy_all = jnp.concatenate(
        [dy_gate, dy_scan[:, :scan_width], d_bc, dy_scan[:, scan_width + bc_width :]], axis=1
    )
    in_keep, in_send = grad_halves(normed_in, after(dy_all, d_in))
    in_keep, in_far = halves(add_low(in_keep, core_swap(in_send)))
    out_keep, out_far = halves(add_low(out_keep, out_far))
    out_far = shard_swap(out_far, fsdp_size // 2)
    out_pair = jnp.concatenate([out_own, chip_swap(out_own)], axis=0)
    late_keep, late_rest = halves(add_low(late_sum, late_recv))
    late_recv = shard_swap(late_rest, fsdp_size // 4)
    in_keep, in_far, d_in, d_in_peer, out_keep, out_far, out_pair, late_keep, late_recv = stage(
        in_keep, in_far, d_in, d_in_peer, out_keep, out_far, out_pair, late_keep, late_recv
    )

    def own_rows(v):
        return lax.dynamic_slice_in_dim(v, own_start, tok_rows, 0)

    d_in_own = own_rows(d_in).astype(F32) + d_in_peer.astype(F32)
    unit_own = own_rows(x_low).astype(F32) * own_rows(inverse_in)
    grad_own = own_rows(d_hidden) + norm_back(d_in_own, unit_own, own_rows(inverse_in), gain_in)
    g_norm_in = jnp.sum(d_in_own * unit_own, axis=0, keepdims=True)
    grad_own = dot_nt(grad_own.astype(BF), perm).astype(BF)
    in_recv = chip_swap(in_far)
    out_near = [out_pair, pair_swap(out_pair)]
    grad_pair = jnp.concatenate([grad_own, chip_swap(grad_own)], axis=0)
    def shards_sum(keep, far, gap):
        total = add_low(keep, far)
        while gap > 1:
            gap //= 2
            keep, far = halves(total)
            total = add_low(keep, shard_swap(far, gap))
        return total

    late_sum = shards_sum(late_keep, late_recv, fsdp_size // 4)
    out_sum = shards_sum(out_keep, out_far, fsdp_size // 2)
    grad_pair, in_keep, in_recv, late_sum, out_sum, out_near = stage(
        grad_pair, in_keep, in_recv, late_sum, out_sum, out_near
    )

    in_keep, in_far = halves(add_low(in_keep, in_recv))
    in_recv = shard_swap(in_far, fsdp_size // 2)
    grad_near = [grad_pair, pair_swap(grad_pair)]
    late_twin, out_twin = chip_swap(late_sum), chip_swap(out_sum)
    mixed_home = pick_rows(home_spots, out_near + [core_swap(v) for v in out_near])
    in_keep, in_recv, grad_near, late_twin, out_twin, mixed_home = stage(
        in_keep, in_recv, grad_near, late_twin, out_twin, mixed_home
    )

    grad_home = pick_rows(home_spots, grad_near + [core_swap(v) for v in grad_near])
    in_sum = shards_sum(in_keep, in_recv, fsdp_size // 2)
    in_twin = chip_swap(in_sum)

    def finish(first, second):
        both = jnp.concatenate([first, second], axis=0)
        return assemble((first, second), halves(core_swap(both)))

    s_late = finish(late_sum, late_twin)
    s_ffn, s_back = s_late[:, : 2 * ffn_width], s_late[:, 2 * ffn_width :]
    s_out = finish(out_sum, out_twin)
    s_in = finish(in_sum, in_twin)
    gate_width = scan_width + query_width + LANES
    s_gate, s_scan = s_in[:, :gate_width], s_in[:, gate_width:]
    g_norms = dot_nt(
        jnp.concatenate([g_norm_in, g_norm_mid], axis=0), perm.astype(F32), PRECISE
    )
    g_norms, g_taps_two = g_norms.reshape(-1), g_taps_two[: taps_bc.shape[0]].reshape(-1)
    g_taps_one = g_taps_one[: taps_x.shape[0]].reshape(-1)
    g_heads = g_heads[:3, :heads].reshape(-1)
    g_gain = g_gain.reshape(-1)
    parts = (g_norms[:model_width], g_taps_two, g_norms[model_width:], g_taps_one, g_heads, g_gain)
    paired = model_width + g_taps_two.shape[0]
    sums = reduce_small(after(jnp.concatenate(parts), *grad_near))
    sums = jnp.concatenate([sums[:paired] + pair_swap(sums[:paired]), sums[paired:]])
    ends = [sum(v.size for v in parts[: i + 1]) for i in range(len(parts))]
    sum_in, sum_two, sum_mid, sum_one, sum_heads, sum_gain = [
        sums[end - v.size : end] for end, v in zip(ends, parts)
    ]

    def shard_of(array, dim_index):
        piece = array.shape[dim_index] // fsdp_size
        return lax.dynamic_slice_in_dim(array, fsdp_index * piece, piece, dim_index)

    return (
        mixed_home,
        grad_home,
        shard_of(sum_in, 0),
        s_gate[:, scan_width : scan_width + query_width],
        s_gate[:, scan_width + query_width :].reshape(w_keyval.shape),
        s_out[:, :query_width].T,
        jnp.stack([s_gate[:, :scan_width], s_scan[:, :scan_width]], axis=1),
        s_scan[:, scan_width : scan_width + bc_width],
        s_scan[:, scan_width + bc_width :][:, : w_step.shape[1]],
        sum_heads.reshape(head_params.shape),
        shard_of(sum_one.reshape(taps_x.shape[0], heads, HD), 2),
        shard_of(sum_two.reshape(taps_bc.shape[0], -1), 1),
        shard_of(sum_gain.reshape(heads, HD), 1),
        s_out[:, query_width:].T,
        shard_of(sum_mid, 0),
        s_ffn.reshape(w_gate_up.shape),
        s_back.T,
    )


def solution(mesh):
    rows = P(("fsdp", "ctx", "tp"), None)
    in_specs = (
        rows,
        rows,
        P("fsdp", None),
        P("fsdp", None),
        P("fsdp"),
        P("fsdp", "tp"),
        P("fsdp", "tp", None),
        P("tp", "fsdp"),
        P("fsdp", None, "tp"),
        P("fsdp", None),
        P("fsdp", "tp"),
        P(None, "tp"),
        P(None, "tp", "fsdp"),
        P(None, "fsdp"),
        P("tp", "fsdp"),
        P("tp", "fsdp"),
        P("fsdp"),
        P("fsdp", None, "tp"),
        P("tp", "fsdp"),
    )
    out_specs = (
        rows,
        rows,
        P("fsdp"),
        P("fsdp", "tp"),
        P("fsdp", "tp", None),
        P("tp", "fsdp"),
        P("fsdp", None, "tp"),
        P("fsdp", None),
        P("fsdp", "tp"),
        P(None, "tp"),
        P(None, "tp", "fsdp"),
        P(None, "fsdp"),
        P("tp", "fsdp"),
        P("tp", "fsdp"),
        P("fsdp"),
        P("fsdp", None, "tp"),
        P("tp", "fsdp"),
    )
    return jax.shard_map(
        per_device, mesh=mesh, in_specs=in_specs, out_specs=out_specs, check_vma=False
    )
```

```python
import functools
import jax
import jax.numpy as jnp
from jax import lax
from jax.experimental import pallas as pl
from jax.experimental.pallas import tpu as pltpu
from jax.sharding import PartitionSpec as P

HD = 64
BLK = 128
LANES = 128
EPSILON = 1e-05
ROPE_BASE = 100000000000.0
PRECISE = lax.Precision.HIGHEST
F32 = jnp.float32
BF = jnp.bfloat16
FAR = -1e30


def dot_nn(a, b, precision=None):
    return lax.dot_general(
        a, b, (((1,), (0,)), ((), ())), precision=precision, preferred_element_type=F32
    )


def dot_nt(a, b, precision=None):
    return lax.dot_general(
        a, b, (((1,), (1,)), ((), ())), precision=precision, preferred_element_type=F32
    )


def dot_tn(a, b, precision=None):
    return lax.dot_general(
        a, b, (((0,), (0,)), ((), ())), precision=precision, preferred_element_type=F32
    )


def iota(shape, dim):
    return lax.broadcasted_iota(jnp.int32, shape, dim)


def swap_halves(v):
    lanes = v.shape[1]
    low = (iota(v.shape, 1) & (HD - 1)) < HD // 2
    return jnp.where(low, pltpu.roll(v, lanes - HD // 2, 1), pltpu.roll(v, HD // 2, 1))


def split_pair(v):
    first = iota(v.shape, 1) < HD
    zero = jnp.zeros_like(v)
    return jnp.concatenate([jnp.where(first, v, zero), jnp.where(first, zero, v)], axis=0)


def keys_values(kv, cos, sin):
    first = iota(kv.shape, 1) < HD
    roped = kv * cos + swap_halves(kv) * sin
    keys = jnp.where(first, roped, 0.0)
    values = jnp.where(first, 0.0, kv)
    key_pair = (keys.astype(BF), pltpu.roll(keys, HD, 1).astype(BF))
    value_pair = (pltpu.roll(values, HD, 1).astype(BF), values.astype(BF))
    return key_pair, value_pair


def attention_probs(query, key, allowed):
    scores = dot_nt(query, key) * HD ** (-0.5)
    scores = jnp.where(allowed, scores, FAR)
    weights = jnp.exp(scores - jnp.max(scores, axis=1, keepdims=True))
    return weights / jnp.sum(weights, axis=1, keepdims=True)


def allowed_rows(segc, segr, lower, count):
    keys = lower + count
    same = segc[lower:keys, :] == segr[:, :keys]
    return same & (iota((count, keys), 0) + lower >= iota((count, keys), 1))


def attention_fwd_kernel(q_ref, kv_ref, cos_ref, sin_ref, segc_ref, segr_ref, out_ref):
    rows, width = q_ref.shape
    cos, sin = cos_ref[...], sin_ref[...]
    key_pair, value_pair = keys_values(kv_ref[...], cos, sin)
    segc, segr = segc_ref[...], segr_ref[...]
    for pair in range(width // LANES):
        cols = slice(pair * LANES, (pair + 1) * LANES)
        raw = q_ref[:, cols]
        query = (raw * cos + swap_halves(raw) * sin).astype(BF)
        for lower in range(0, rows, BLK):
            keys = lower + BLK
            allowed = allowed_rows(segc, segr, lower, BLK)
            total = None
            for side in range(2):
                probs = attention_probs(query[lower:keys], key_pair[side][:keys], allowed)
                part = dot_nn(probs.astype(BF), value_pair[side][:keys])
                total = part if total is None else total + part
            out_ref[lower:keys, cols] = total.astype(BF)


def attention_bwd_kernel(
    q_ref, kv_ref, cos_ref, sin_ref, segc_ref, segr_ref, do_ref, out_ref, dk_ref, dv_ref
):
    rows, width = q_ref.shape
    cos, sin = cos_ref[...], sin_ref[...]
    key_pair, value_pair = keys_values(kv_ref[...], cos, sin)
    segc, segr = segc_ref[...], segr_ref[...]
    dk_ref[...] = jnp.zeros_like(dk_ref)
    dv_ref[...] = jnp.zeros_like(dv_ref)
    for pair in range(width // LANES):
        cols = slice(pair * LANES, (pair + 1) * LANES)
        raw = q_ref[:, cols]
        query = (raw * cos + swap_halves(raw) * sin).astype(BF)
        for lower in range(0, rows, BLK):
            keys = lower + BLK
            allowed = allowed_rows(segc, segr, lower, BLK)
            query_part = query[lower:keys]
            grad = do_ref[lower:keys, cols]
            d_query = None
            probs_all, scores_all = [], []
            for side in range(2):
                probs = attention_probs(query_part, key_pair[side][:keys], allowed)
                d_probs = dot_nt(grad, value_pair[side][:keys])
                inner = jnp.sum(d_probs * probs, axis=1, keepdims=True)
                d_scores = (probs * (d_probs - inner)).astype(BF)
                part = dot_nn(d_scores, key_pair[side][:keys])
                d_query = part if d_query is None else d_query + part
                probs_all.append(probs.astype(BF))
                scores_all.append(d_scores)
            dv_ref[:keys, :] += dot_tn(jnp.concatenate(probs_all, axis=0), split_pair(grad))
            dk_ref[:keys, :] += dot_tn(jnp.concatenate(scores_all, axis=0), split_pair(query_part))
            d_query = d_query * HD ** (-0.5)
            cos_part, sin_part = cos[lower:keys], sin[lower:keys]
            out_ref[lower:keys, cols] = (
                d_query * cos_part - swap_halves(d_query) * sin_part
            ).astype(BF)
    first = iota(dk_ref.shape, 1) < HD
    d_key = dk_ref[...]
    d_key = (d_key + pltpu.roll(d_key, HD, 1)) * HD ** (-0.5)
    d_key = d_key * cos - swap_halves(d_key) * sin
    d_value = dv_ref[...]
    d_value = d_value + pltpu.roll(d_value, HD, 1)
    out_ref[:, width:] = jnp.where(first, d_key, d_value).astype(BF)


def conv_rows(signal, taps_ref, position):
    total = taps_ref[4:5, :] + taps_ref[3:4, :] * signal
    for lag in range(1, 4):
        moved = jnp.where(position >= lag, pltpu.roll(signal, lag, 0), 0.0)
        total = total + taps_ref[3 - lag : 4 - lag, :] * moved
    return total


def conv_back(signal, d_pre, taps_ref, grad_ref, position):
    rows = signal.shape[0]
    grad_ref[...] = jnp.zeros_like(grad_ref)
    grad_ref[4:5, :] = jnp.sum(d_pre, axis=0, keepdims=True)
    grad_ref[3:4, :] = jnp.sum(d_pre * signal, axis=0, keepdims=True)
    total = taps_ref[3:4, :] * d_pre
    for lag in range(1, 4):
        kept = jnp.where(position >= lag, d_pre, 0.0)
        grad_ref[3 - lag : 4 - lag, :] = jnp.sum(
            kept * pltpu.roll(signal, lag, 0), axis=0, keepdims=True
        )
        total = total + taps_ref[3 - lag : 4 - lag, :] * pltpu.roll(kept, rows - lag, 0)
    return total


def softplus(v):
    return jnp.maximum(v, 0.0) + jnp.log1p(jnp.exp(-jnp.abs(v)))


def spread_matrix(width):
    shape = (LANES, width)
    return (iota(shape, 0) == (iota(shape, 1) >> 6)).astype(F32)


def scan_setup(step_ref, heads_ref):
    steps = softplus(step_ref[...] + heads_ref[0:1, :])
    rates = -jnp.exp(heads_ref[1:2, :])
    return steps, rates


def block_decays(steps, rates, segc, lower):
    upper = lower + BLK
    shape = (BLK, BLK)
    lower_ones = (iota(shape, 0) >= iota(shape, 1)).astype(F32)
    decays = dot_nn(lower_ones, steps[lower:upper] * rates, PRECISE)
    seg_part = segc[lower:upper]
    if lower == 0:
        arrive = None
    else:
        carried = seg_part == segc[lower - 1 : lower]
        arrive = jnp.where(carried, jnp.exp(decays), 0.0)
    kept = seg_part == segc[upper - 1 : upper]
    leave = jnp.where(kept, jnp.exp(decays[BLK - 1 : BLK] - decays), 0.0)
    return decays, arrive, leave, lower_ones


def block_mixing(decays, decays_t, head, allowed):
    gap = decays[:, head : head + 1] - decays_t[head : head + 1, :]
    return jnp.exp(jnp.where(allowed, gap, FAR))


def scan_fwd_kernel(
    x_ref, bc_ref, step_ref, tapx_ref, tapbc_ref, heads_ref, skip_ref, segc_ref, segr_ref,
    pos_ref, out_ref, states_ref,
):
    rows, width = x_ref.shape
    position = pos_ref[...]
    segc, segr = segc_ref[...], segr_ref[...]
    conv_x = jax.nn.silu(conv_rows(x_ref[...], tapx_ref, position)).astype(BF)
    conv_bc = jax.nn.silu(conv_rows(bc_ref[...], tapbc_ref, position)).astype(BF)
    steps, rates = scan_setup(step_ref, heads_ref)
    spread = spread_matrix(width)
    scaled = conv_x.astype(F32) * dot_nn(steps, spread, PRECISE)
    state = None
    for lower in range(0, rows, BLK):
        upper = lower + BLK
        b_part = conv_bc[lower:upper, :LANES]
        c_part = conv_bc[lower:upper, LANES:]
        decays, arrive, leave, lower_ones = block_decays(steps, rates, segc, lower)
        decays_t = decays.T
        allowed = (segc[lower:upper] == segr[:, lower:upper]) & (lower_ones > 0.0)
        inner = dot_nt(c_part, b_part)
        scaled_part = scaled[lower:upper]
        scaled_low = scaled_part.astype(BF)
        fresh = dot_tn(b_part, (scaled_part * dot_nn(leave, spread, PRECISE)).astype(BF))
        if state is None:
            recall = None
            states_ref[lower // BLK] = jnp.zeros(fresh.shape, F32)
            state = fresh
        else:
            arrive_wide = dot_nn(arrive, spread, PRECISE)
            recall = dot_nn(c_part, state.astype(BF)) * arrive_wide
            states_ref[lower // BLK] = state
            state = state * arrive_wide[BLK - 1 : BLK] + fresh
        for pair in range(width // LANES):
            cols = slice(pair * LANES, (pair + 1) * LANES)
            mixes = [
                (block_mixing(decays, decays_t, 2 * pair + side, allowed) * inner).astype(BF)
                for side in range(2)
            ]
            local = dot_nn(jnp.concatenate(mixes, axis=1), split_pair(scaled_low[:, cols]))
            if recall is not None:
                local = local + recall[:, cols]
            out_ref[lower:upper, cols] = local + skip_ref[0:1, cols] * conv_x[
                lower:upper, cols
            ].astype(F32)


def scan_bwd_kernel(
    x_ref, bc_ref, step_ref, tapx_ref, tapbc_ref, heads_ref, skip_ref, segc_ref, segr_ref,
    pos_ref, states_ref, dy_ref, out_ref, gtapx_ref, gtapbc_ref, gheads_ref, dx_ref, dbc_ref,
):
    rows, width = x_ref.shape
    position = pos_ref[...]
    segc, segr = segc_ref[...], segr_ref[...]
    pre_x = conv_rows(x_ref[...], tapx_ref, position)
    pre_bc = conv_rows(bc_ref[...], tapbc_ref, position)
    conv_x = jax.nn.silu(pre_x).astype(BF)
    conv_bc = jax.nn.silu(pre_bc).astype(BF)
    steps, rates = scan_setup(step_ref, heads_ref)
    spread = spread_matrix(width)
    steps_wide = dot_nn(steps, spread, PRECISE)
    lane = iota((BLK, LANES), 1)
    sub = iota((LANES, BLK), 0)
    last_row = iota((BLK, LANES), 0) == BLK - 1
    d_state = None
    g_bias = jnp.zeros((1, LANES), F32)
    g_rate = jnp.zeros((1, LANES), F32)
    g_skip = jnp.zeros((1, width), F32)
    for lower in range(rows - BLK, -1, -BLK):
        upper = lower + BLK
        b_part = conv_bc[lower:upper, :LANES]
        c_part = conv_bc[lower:upper, LANES:]
        decays, arrive, leave, lower_ones = block_decays(steps, rates, segc, lower)
        decays_t = decays.T
        allowed = (segc[lower:upper] == segr[:, lower:upper]) & (lower_ones > 0.0)
        inner = dot_nt(c_part, b_part)
        x_part = conv_x[lower:upper].astype(F32)
        scaled_part = x_part * steps_wide[lower:upper]
        scaled_low = scaled_part.astype(BF)
        grad = dy_ref[lower:upper, :]
        grad_low = grad.astype(BF)
        d_scaled = []
        d_inner = jnp.zeros((BLK, BLK), F32)
        row_sums = jnp.zeros((BLK, LANES), F32)
        col_sums = jnp.zeros((LANES, BLK), F32)
        for pair in range(width // LANES):
            cols = slice(pair * LANES, (pair + 1) * LANES)
            grad_pair = split_pair(grad_low[:, cols])
            d_mix = dot_nt(grad_pair, scaled_low[:, cols])
            mixes = []
            for side in range(2):
                head = 2 * pair + side
                mixing = block_mixing(decays, decays_t, head, allowed)
                mix = mixing * inner
                d_part = d_mix[side * BLK : (side + 1) * BLK]
                d_inner = d_inner + d_part * mixing
                both = d_part * mix
                row_sums = jnp.where(lane == head, jnp.sum(both, axis=1, keepdims=True), row_sums)
                col_sums = jnp.where(sub == head, jnp.sum(both, axis=0, keepdims=True), col_sums)
                mixes.append(mix.astype(BF))
            d_scaled.append(dot_tn(jnp.concatenate(mixes, axis=0), grad_pair))
        d_scaled = jnp.concatenate(d_scaled, axis=1)
        d_decays = row_sums - col_sums.T
        d_inner = d_inner.astype(BF)
        d_c = dot_nn(d_inner, b_part)
        d_b = dot_tn(d_inner, c_part)
        if lower > 0:
            arrive_wide = dot_nn(arrive, spread, PRECISE)
            state = states_ref[lower // BLK]
            state_low = state.astype(BF)
            recall = dot_nn(c_part, state_low) * arrive_wide
            d_decays = d_decays + dot_nt(recall * grad, spread, PRECISE)
            grad_in = (grad * arrive_wide).astype(BF)
            d_c = d_c + dot_nt(grad_in, state_low)
        if d_state is not None:
            state_grad = d_state.astype(BF)
            leave_wide = dot_nn(leave, spread, PRECISE)
            d_kept = dot_nn(b_part, state_grad) * leave_wide
            d_b = d_b + dot_nt((scaled_part * leave_wide).astype(BF), state_grad)
            d_leave = dot_nt(d_kept * scaled_part, spread, PRECISE)
            d_last = jnp.sum(d_leave, axis=0, keepdims=True)
            if lower > 0:
                lingering = jnp.sum(d_state * state, axis=0, keepdims=True)
                lingering = lingering * arrive_wide[BLK - 1 : BLK]
                d_last = d_last + dot_nt(
                    jnp.broadcast_to(lingering, (8, width)), spread, PRECISE
                )[0:1]
            d_decays = d_decays - d_leave + jnp.where(last_row, d_last, 0.0)
            d_scaled = d_scaled + d_kept
        if lower > 0:
            d_new = dot_tn(c_part, grad_in)
            if d_state is None:
                d_state = d_new
            else:
                d_state = d_state * arrive_wide[BLK - 1 : BLK] + d_new
        d_log = dot_tn(lower_ones, d_decays, PRECISE)
        steps_part = steps[lower:upper]
        d_steps = dot_nt(d_scaled * x_part, spread, PRECISE) + d_log * rates
        d_step_in = d_steps * jax.nn.sigmoid(step_ref[lower:upper, :] + heads_ref[0:1, :])
        g_bias = g_bias + jnp.sum(d_step_in, axis=0, keepdims=True)
        g_rate = g_rate + jnp.sum(d_log * steps_part, axis=0, keepdims=True) * rates
        g_skip = g_skip + jnp.sum(grad * x_part, axis=0, keepdims=True)
        out_ref[lower:upper, width + 2 * LANES :] = d_step_in.astype(BF)
        dx_ref[lower:upper, :] = d_scaled * steps_wide[lower:upper] + grad * skip_ref[0:1, :]
        dbc_ref[lower:upper, :LANES] = d_b
        dbc_ref[lower:upper, LANES:] = d_c
    gheads_ref[...] = jnp.zeros_like(gheads_ref)
    gheads_ref[0:1, :] = g_bias
    gheads_ref[1:2, :] = g_rate
    gheads_ref[2:3, :] = dot_nt(jnp.broadcast_to(g_skip, (8, width)), spread, PRECISE)[0:1]
    gate = jax.nn.sigmoid(pre_x)
    d_pre = dx_ref[...] * gate * (1.0 + pre_x * (1.0 - gate))
    out_ref[:, :width] = conv_back(x_ref[...], d_pre, tapx_ref, gtapx_ref, position).astype(BF)
    gate = jax.nn.sigmoid(pre_bc)
    d_pre = dbc_ref[...] * gate * (1.0 + pre_bc * (1.0 - gate))
    out_ref[:, width : width + 2 * LANES] = conv_back(
        bc_ref[...], d_pre, tapbc_ref, gtapbc_ref, position
    ).astype(BF)


def select_parts(spot_ref, part_refs):
    spots = spot_ref[...]
    total, first = None, 0
    for part_ref in part_refs:
        shape = (spots.shape[0], part_ref.shape[0])
        chosen = (spots == iota(shape, 1) + first).astype(F32).astype(BF)
        product = dot_nn(chosen, part_ref[...])
        total = product if total is None else total + product
        first += part_ref.shape[0]
    return total


def pick_kernel(spot_ref, *refs):
    refs[-1][...] = select_parts(spot_ref, refs[:-1]).astype(BF)


def pick_turn_kernel(spot_ref, perm_ref, *refs):
    rows = select_parts(spot_ref, refs[:-1]).astype(BF)
    refs[-1][...] = dot_nn(rows, perm_ref[...]).astype(BF)


def pick_norm_kernel(spot_ref, perm_ref, gain_ref, *refs):
    rows_ref, normed_ref, inverse_ref = refs[-3:]
    rows = select_parts(spot_ref, refs[:-3]).astype(BF)
    rows = dot_nn(rows, perm_ref[...])
    inverse = lax.rsqrt(jnp.mean(rows * rows, axis=1, keepdims=True) + EPSILON)
    rows_ref[...] = rows.astype(BF)
    normed_ref[...] = (rows * inverse * gain_ref[...]).astype(BF)
    inverse_ref[...] = inverse


def join_kernel(*refs):
    start = 0
    for ref in refs[:-1]:
        refs[-1][start : start + ref.shape[0], :] = ref[...]
        start += ref.shape[0]


def join_tail_kernel(piece, near_ref, far_ref, out_ref):
    start = near_ref.shape[0] - piece
    out_ref[:start, :] = near_ref[piece:, :]
    out_ref[start:, :] = far_ref[...]


def grad_kernel(*refs):
    first = 0
    for left_ref, right_ref in zip(refs[:-1:2], refs[1:-1:2]):
        width = right_ref.shape[1]
        refs[-1][:, first : first + width] = dot_tn(left_ref[...], right_ref[...]).astype(BF)
        first += width


def ordered_rows(index_ref, own_ref, other_ref):
    index = index_ref[0]
    core_bit, chip_bit = (index & 1) == 1, (index & 2) == 2
    piece = own_ref.shape[0] // 2
    own, other = own_ref[...].astype(F32), other_ref[...].astype(F32)
    by_gap = (own[:piece], other[:piece], own[piece:], other[piece:])
    rows = []
    for quarter in range(4):
        near = jnp.where(core_bit, by_gap[quarter ^ 1], by_gap[quarter])
        far = jnp.where(core_bit, by_gap[quarter ^ 3], by_gap[quarter ^ 2])
        rows.append(jnp.where(chip_bit, far, near))
    return jnp.concatenate(rows, axis=0)


def finish_late_kernel(index_ref, own_ref, other_ref, up_ref, down_ref):
    rows = ordered_rows(index_ref, own_ref, other_ref)
    width = up_ref.shape[2]
    up_ref[:, 0, :] = rows[:, :width]
    up_ref[:, 1, :] = rows[:, width : 2 * width]
    down_ref[...] = rows[:, 2 * width :].T


def finish_out_kernel(
    index_ref, own_ref, other_ref, attn_ref, mamba_ref, z_ref, query_ref, keyval_ref
):
    rows = ordered_rows(index_ref, own_ref, other_ref)
    first = 0
    for ref in (attn_ref, mamba_ref):
        ref[...] = rows[:, first : first + ref.shape[0]].T
        first += ref.shape[0]
    for ref in (z_ref, query_ref, keyval_ref):
        ref[...] = rows[:, first : first + ref.shape[1]]
        first += ref.shape[1]


def finish_scan_kernel(index_ref, own_ref, other_ref, z_ref, zx_ref, bc_ref, step_ref):
    rows = ordered_rows(index_ref, own_ref, other_ref)
    width = z_ref.shape[1]
    zx_ref[:, 0, :] = z_ref[...]
    zx_ref[:, 1, :] = rows[:, :width]
    bc_ref[...] = rows[:, width : width + bc_ref.shape[1]]
    step_ref[...] = rows[:, width + bc_ref.shape[1] :]


def ffn_kernel(
    normed_ref, cot_ref, near_ref, far_ref, back_near_ref, back_far_ref, act_ref, grad_ref, mid_ref
):
    half = near_ref.shape[0]
    width = act_ref.shape[1]
    tile = 512
    total = [None, None]
    for first in range(0, width, tile):
        gate_cols = slice(first, first + tile)
        up_cols = slice(width + first, width + first + tile)

        def product(left_ref, near, far, cols):
            return dot_nn(left_ref[:, :half], near[:, cols]) + dot_nn(
                left_ref[:, half:], far[:, cols]
            )

        gate = product(normed_ref, near_ref, far_ref, gate_cols)
        up = product(normed_ref, near_ref, far_ref, up_cols)
        d_act = product(cot_ref, back_near_ref, back_far_ref, gate_cols)
        sigma = jax.nn.sigmoid(gate)
        silu = gate * sigma
        act_ref[:, gate_cols] = (silu * up).astype(BF)
        d_gate = (d_act * up * sigma * (1.0 + gate * (1.0 - sigma))).astype(BF)
        d_up = (d_act * silu).astype(BF)
        grad_ref[:, gate_cols] = d_gate
        grad_ref[:, up_cols] = d_up
        for i, ref in enumerate((near_ref, far_ref)):
            part = dot_nt(d_gate, ref[:, gate_cols]) + dot_nt(d_up, ref[:, up_cols])
            total[i] = part if total[i] is None else total[i] + part
    mid_ref[:, :half] = total[0].astype(BF)
    mid_ref[:, half:] = total[1].astype(BF)


def project_kernel(rows_ref, near_ref, far_ref, *outs):
    half = near_ref.shape[0]
    first = 0
    for out_ref in outs:
        cols = slice(first, first + out_ref.shape[1])
        out_ref[...] = dot_nn(rows_ref[:, :half], near_ref[:, cols]) + dot_nn(
            rows_ref[:, half:], far_ref[:, cols]
        )
        first += out_ref.shape[1]


def turn_back_kernel(rows_ref, near_ref, far_ref, out_ref):
    half = near_ref.shape[0]
    out_ref[...] = (
        dot_nn(rows_ref[:, :half], near_ref[...]) + dot_nn(rows_ref[:, half:], far_ref[...])
    ).astype(BF)


def unproject_kernel(count, *refs):
    out_ref = refs[-1]
    half = refs[count].shape[0]
    for side in range(2):
        total = None
        for i in range(count):
            part = dot_nt(refs[i][...], refs[count + 2 * i + side][...])
            total = part if total is None else total + part
        out_ref[:, side * half : (side + 1) * half] = total.astype(BF)


VMEM_BYTES = 48 * 1024 * 1024


def column_block(rows, width, index):
    return pl.BlockSpec((rows, width), lambda i: (0, index))


def whole_block(shape):
    zeros = (0,) * len(shape)
    return pl.BlockSpec(shape, lambda i: zeros)


def single_step(kernel, in_specs, outs, scratch=(), flops=1024):
    return pl.pallas_call(
        kernel,
        grid=(1,),
        in_specs=in_specs,
        out_specs=[whole_block(o.shape) for o in outs],
        out_shape=outs,
        scratch_shapes=list(scratch),
        compiler_params=pltpu.CompilerParams(vmem_limit_bytes=VMEM_BYTES),
        cost_estimate=pl.CostEstimate(flops=flops, bytes_accessed=1024, transcendentals=0),
    )


def attention_specs(rows, width, gate_width):
    return [
        column_block(rows, width, gate_width // width),
        column_block(rows, LANES, (gate_width + width) // LANES),
        whole_block((rows, LANES)),
        whole_block((rows, LANES)),
        whole_block((rows, 1)),
        whole_block((1, rows)),
    ]


def attention_fwd(y_a, width, gate_width, cos, sin, segc, segr):
    rows = y_a.shape[0]
    return single_step(
        attention_fwd_kernel,
        attention_specs(rows, width, gate_width),
        [jax.ShapeDtypeStruct((rows, width), BF)],
    )(y_a, y_a, cos, sin, segc, segr)[0]


def attention_bwd(y_a, width, gate_width, cos, sin, segc, segr, d_attn):
    rows = y_a.shape[0]
    return single_step(
        attention_bwd_kernel,
        attention_specs(rows, width, gate_width) + [whole_block((rows, width))],
        [jax.ShapeDtypeStruct((rows, width + LANES), BF)],
        [pltpu.VMEM((rows, LANES), F32), pltpu.VMEM((rows, LANES), F32)],
    )(y_a, y_a, cos, sin, segc, segr, d_attn)[0]


def scan_specs(rows, width):
    return [
        column_block(rows, width, 0),
        column_block(rows, 2 * LANES, width // (2 * LANES)),
        column_block(rows, LANES, (width + 2 * LANES) // LANES),
        whole_block((8, width)),
        whole_block((8, 2 * LANES)),
        whole_block((8, LANES)),
        whole_block((1, width)),
        whole_block((rows, 1)),
        whole_block((1, rows)),
        whole_block((rows, 1)),
    ]


def scan_fwd(y_b, width, taps_x, taps_bc, heads, skip, segc, segr, position):
    rows = y_b.shape[0]
    return single_step(
        scan_fwd_kernel,
        scan_specs(rows, width),
        [
            jax.ShapeDtypeStruct((rows, width), F32),
            jax.ShapeDtypeStruct((rows // BLK, LANES, width), F32),
        ],
    )(y_b, y_b, y_b, taps_x, taps_bc, heads, skip, segc, segr, position)


def scan_bwd(y_b, width, taps_x, taps_bc, heads, skip, segc, segr, position, states, d_out):
    rows = y_b.shape[0]
    return single_step(
        scan_bwd_kernel,
        scan_specs(rows, width)
        + [whole_block(states.shape), whole_block((rows, width))],
        [
            jax.ShapeDtypeStruct(y_b.shape, BF),
            jax.ShapeDtypeStruct((8, width), F32),
            jax.ShapeDtypeStruct((8, 2 * LANES), F32),
            jax.ShapeDtypeStruct((8, LANES), F32),
        ],
        [pltpu.VMEM((rows, width), F32), pltpu.VMEM((rows, 2 * LANES), F32)],
    )(y_b, y_b, y_b, taps_x, taps_bc, heads, skip, segc, segr, position, states, d_out)


def pick_rows(spots, parts):
    operands = (spots[:, None],) + tuple(parts)
    return single_step(
        pick_kernel,
        [whole_block(v.shape) for v in operands],
        [jax.ShapeDtypeStruct((spots.shape[0], parts[0].shape[1]), BF)],
    )(*operands)[0]


def pick_turned(spots, perm, parts):
    operands = (spots[:, None], perm) + tuple(parts)
    return single_step(
        pick_turn_kernel,
        [whole_block(v.shape) for v in operands],
        [jax.ShapeDtypeStruct((spots.shape[0], perm.shape[1]), BF)],
    )(*operands)[0]


def pick_normed(spots, perm, gain, parts):
    rows = spots.shape[0]
    operands = (spots[:, None], perm, gain) + tuple(parts)
    wide = jax.ShapeDtypeStruct((rows, perm.shape[1]), BF)
    return single_step(
        pick_norm_kernel,
        [whole_block(v.shape) for v in operands],
        [wide, wide, jax.ShapeDtypeStruct((rows, 1), F32)],
    )(*operands)


def join_blocks(operands, specs, width):
    rows = sum(spec.block_shape[0] for spec in specs)
    return single_step(join_kernel, specs, [jax.ShapeDtypeStruct((rows, width), BF)])(*operands)[0]


def ffn_both_ways(normed, cot_rows, near, far, back_near, back_far, width, back_index):
    rows, model_width = normed.shape
    half = near.shape[0]
    return single_step(
        ffn_kernel,
        [whole_block(normed.shape), whole_block(cot_rows.shape)]
        + [whole_block(near.shape), whole_block(far.shape)]
        + [column_block(half, width, back_index), column_block(half, width, back_index)],
        [
            jax.ShapeDtypeStruct((rows, width), BF),
            jax.ShapeDtypeStruct((rows, 2 * width), BF),
            jax.ShapeDtypeStruct((rows, model_width), BF),
        ],
    )(normed, cot_rows, near, far, back_near, back_far)


def project(rows, near, far, width):
    count = near.shape[1] // width
    shape = jax.ShapeDtypeStruct((rows.shape[0], width), F32)
    operands = (rows, near, far)
    return single_step(
        project_kernel, [whole_block(v.shape) for v in operands], [shape] * count
    )(*operands)


def turn_back(rows, near, far, width):
    half = near.shape[0]
    return single_step(
        turn_back_kernel,
        [whole_block(rows.shape), column_block(half, width, 0), column_block(half, width, 0)],
        [jax.ShapeDtypeStruct((rows.shape[0], width), BF)],
    )(rows, near, far)[0]


def unproject(lefts, blocks):
    specs = [whole_block(v.shape) for v in lefts]
    operands = list(lefts)
    for left, (near, far, index) in zip(lefts, blocks):
        specs += [column_block(near.shape[0], left.shape[1], index)] * 2
        operands += [near, far]
    rows, half = lefts[0].shape[0], blocks[0][0].shape[0]
    return single_step(
        functools.partial(unproject_kernel, len(lefts)),
        specs,
        [jax.ShapeDtypeStruct((rows, 2 * half), BF)],
    )(*operands)[0]


def join_tail(near, far, piece):
    rows = near.shape[0] + far.shape[0] - piece
    return single_step(
        functools.partial(join_tail_kernel, piece),
        [whole_block(near.shape), whole_block(far.shape)],
        [jax.ShapeDtypeStruct((rows, near.shape[1]), BF)],
    )(near, far)[0]


def grad_product(pairs, side):
    half = pairs[0][0].shape[1] // 2
    specs, operands = [], []
    for left, right in pairs:
        specs += [column_block(left.shape[0], half, side), whole_block(right.shape)]
        operands += [left, right]
    width = sum(right.shape[1] for left, right in pairs)
    return single_step(grad_kernel, specs, [jax.ShapeDtypeStruct((half, width), BF)])(*operands)[0]


def finish(kernel, index, operands, shapes):
    return single_step(
        kernel,
        [pl.BlockSpec(memory_space=pltpu.SMEM)] + [whole_block(v.shape) for v in operands],
        [jax.ShapeDtypeStruct(shape, F32) for shape in shapes],
    )(index.astype(jnp.int32).reshape(1), *operands)


def finish_late(index, own, other, width):
    rows = 2 * own.shape[0]
    shapes = [(rows, 2, width), (own.shape[1] - 2 * width, rows)]
    return finish(finish_late_kernel, index, (own, other), shapes)


def finish_out(index, own, other, query_width, scan_width):
    rows = 2 * own.shape[0]
    shapes = [(query_width, rows), (scan_width, rows)]
    shapes += [(rows, scan_width), (rows, query_width), (rows, LANES)]
    return finish(finish_out_kernel, index, (own, other), shapes)


def finish_scan(index, own, other, grad_z, bc_width):
    rows, scan_width = grad_z.shape
    shapes = [(rows, 2, scan_width), (rows, bc_width), (rows, LANES)]
    return finish(finish_scan_kernel, index, (own, other, grad_z), shapes)


CORE_SWAP = [(0, 1), (1, 0), (2, 3), (3, 2)]
CHIP_SWAP = [(0, 2), (2, 0), (1, 3), (3, 1)]
PAIR_SWAP = [(0, 1), (1, 0)]
def core_swap(v):
    return lax.ppermute(v, "ctx", CORE_SWAP)


def chip_swap(v):
    return lax.ppermute(v, "ctx", CHIP_SWAP)


def pair_swap(v):
    return lax.ppermute(v, "tp", PAIR_SWAP)


def shard_swap(v, gap):
    size = lax.axis_size("fsdp")
    return lax.ppermute(v, "fsdp", [(i, i ^ gap) for i in range(size)])


def quarter_perm(width):
    size = lax.axis_size("fsdp")
    shard = width // size
    piece = shard // 4
    spots = jnp.arange(width, dtype=jnp.int32)
    slot = spots // (size * piece)
    turn = (spots // piece) % size
    within = spots % piece
    quarter = jnp.where(slot == 1, 2, jnp.where(slot == 2, 1, slot)) ^ lax.axis_index("ctx")
    owner = lax.axis_index("fsdp") ^ turn
    column = owner * shard + quarter * piece + within
    return (spots[:, None] == column[None, :]).astype(BF)


def after(v, *others):
    return lax.optimization_barrier((v,) + others)[0]


def own_quarters(shard, sideways=False):
    index = lax.axis_index("ctx")
    if sideways:
        count = shard.shape[1]
        piece = count // 4
        place = jnp.arange(2 * piece, dtype=jnp.int32)
        column = (index ^ (2 * (place // piece))) * piece + place % piece
        chosen = (jnp.arange(count, dtype=jnp.int32)[None, :] == column[:, None]).astype(BF)
        both = dot_nt(chosen, shard).astype(BF)
        return both[:piece], both[piece:]
    piece = shard.shape[0] // 4
    return tuple(
        lax.dynamic_slice_in_dim(shard, (index ^ gap) * piece, piece, 0) for gap in (0, 2)
    )


def stage(*values):
    return lax.optimization_barrier(values)


def gather_near(own):
    line, gap = own, 1
    while 2 * gap < lax.axis_size("fsdp"):
        line = jnp.concatenate([line, shard_swap(line, gap)], axis=0)
        gap *= 2
    return line


def gather_far(near):
    return shard_swap(near, lax.axis_size("fsdp") // 2)


def swap_line(near, far):
    return chip_swap(join_tail(near, far, near.shape[0] * 2 // lax.axis_size("fsdp")))


def join_half(*parts):
    specs = [whole_block(v.shape) for v in parts]
    return join_blocks(parts, specs, parts[0].shape[1])


def order_shards(rows):
    owner = jnp.arange(rows.shape[0], dtype=jnp.int32)
    turn = lax.axis_index("fsdp") ^ owner
    return dot_nn((turn[:, None] == owner[None, :]).astype(BF), rows)


def add_low(left, right):
    return (left.astype(F32) + right.astype(F32)).astype(BF)


def halves(v):
    half = v.shape[0] // 2
    return v[:half], v[half:]


def direct_near(rows):
    near = [rows, chip_swap(rows), pair_swap(rows)]
    return near + [lax.ppermute(rows, ("ctx", "tp"), [(i, i ^ 5) for i in range(8)])]


def stack_spot(spot, rows):
    member = spot // rows
    gap = (member // 2) ^ lax.axis_index("ctx")
    turn = (member % 2) ^ lax.axis_index("tp")
    return ((gap & 1) * 4 + turn * 2 + (gap >> 1)) * rows + spot % rows


def dealt_order(lengths, dealing):
    numbers = jnp.arange(lengths.shape[0], dtype=jnp.int32)
    given_start = jnp.cumsum(lengths, dtype=jnp.int32) - lengths
    chosen = (dealing[:, None] == numbers[None, :]).astype(jnp.int32)
    dealt_len = jnp.sum(chosen * lengths[None, :], axis=1, dtype=jnp.int32)
    dealt_from = jnp.sum(chosen * given_start[None, :], axis=1, dtype=jnp.int32)
    dealt_start = jnp.cumsum(dealt_len, dtype=jnp.int32) - dealt_len
    return dealt_len, dealt_from, dealt_start


def look_up(spots, starts, counts, *tables):
    inside = (
        (spots[:, None] >= starts[None, :]) & (spots[:, None] < (starts + counts)[None, :])
    ).astype(jnp.int32)
    return [jnp.sum(inside * table[None, :], axis=1, dtype=jnp.int32) for table in tables]


def norm_back(grad_out, unit_rows, inverse, gain):
    scaled = grad_out * gain
    return inverse * (scaled - unit_rows * jnp.mean(scaled * unit_rows, axis=1, keepdims=True))


def inverse_norm(rows):
    return lax.rsqrt(jnp.mean(rows * rows, axis=1, keepdims=True) + EPSILON)


def padded(v, rows, cols):
    return jnp.pad(v, ((0, rows - v.shape[0]), (0, cols - v.shape[1])))


def per_device(
    tokens,
    cotangent,
    lengths,
    dealing,
    norm_in,
    w_query,
    w_keyval,
    w_attn_out,
    w_zx,
    w_bc,
    w_step,
    head_params,
    taps_x,
    taps_bc,
    gain_mamba,
    w_mamba_out,
    norm_mid,
    w_gate_up,
    w_down,
):
    tok_rows, model_width = tokens.shape
    tp_size = lax.axis_size("tp")
    fsdp_size = lax.axis_size("fsdp")
    rank_rows = tok_rows * tp_size
    tp_index = lax.axis_index("tp")
    fsdp_index = lax.axis_index("fsdp")
    ctx_index = lax.axis_index("ctx")
    shard = w_query.shape[0]
    heads = head_params.shape[1]
    scan_width = heads * HD
    query_width = w_query.shape[1]
    bc_width = w_bc.shape[1]
    ffn_width = w_gate_up.shape[2]
    own_start = tp_index * tok_rows
    peer_start = (tp_size - 1) * tok_rows - own_start

    dealt_len, dealt_from, dealt_start = dealt_order(lengths[0], dealing[0])
    numbers = jnp.arange(lengths.shape[1], dtype=jnp.int32)
    spots = ctx_index * rank_rows + jnp.arange(rank_rows, dtype=jnp.int32)
    segment, begins, anchor = look_up(
        spots, dealt_start, dealt_len, numbers, dealt_start, dealt_from
    )
    position = spots - begins
    sources = stack_spot(anchor + position, tok_rows)
    home = (ctx_index * tp_size + tp_index) * tok_rows + jnp.arange(tok_rows, dtype=jnp.int32)
    home_dealt, home_given = look_up(home, dealt_from, dealt_len, dealt_start, dealt_from)
    home_spots = stack_spot(home - home_given + home_dealt, tok_rows)
    segc, segr, posc = segment[:, None], segment[None, :], position[:, None]
    half_width = HD // 2
    freqs = ROPE_BASE ** (-jnp.arange(half_width, dtype=jnp.float32) / half_width)
    angles = position.astype(jnp.float32)[:, None] * freqs[None, :]
    cosine, sine = jnp.cos(angles), jnp.sin(angles)
    cos_table = jnp.concatenate([cosine] * 4, axis=1)
    sin_table = jnp.concatenate([-sine, sine, -sine, sine], axis=1)
    perm = lax.optimization_barrier(quarter_perm(model_width))

    small = (norm_in, norm_mid, taps_x, taps_bc, gain_mamba)
    small_sizes = [v.size for v in small]
    piece = shard // 4
    small = jnp.concatenate([v.reshape(-1) for v in small]).reshape(piece, -1)
    small_width = small.shape[1]
    free = LANES - heads - small_width
    wide = scan_width + 2 * LANES + LANES

    def in_quarter(gap):
        def rows_of(v):
            return lax.dynamic_slice_in_dim(v, (ctx_index ^ gap) * piece, piece, 0)

        zx = rows_of(w_zx)
        parts = [zx[:, 1, :], rows_of(w_bc), rows_of(w_step), small]
        parts += [jnp.zeros((piece, free), BF), zx[:, 0, :], rows_of(w_query)]
        return jnp.concatenate(parts + [rows_of(w_keyval).reshape(piece, -1)], axis=1)

    in_own, in_twin = in_quarter(0), in_quarter(2)
    token_near = direct_near(tokens)
    in_near = gather_near(in_own)
    in_far = gather_far(in_near)
    q_out = own_quarters(jnp.concatenate([w_attn_out, w_mamba_out], axis=0), True)
    q_back = own_quarters(w_down, True)
    q_late = [jnp.concatenate([q_out[i], q_back[i]], axis=1) for i in range(2)]
    late_near = gather_near(q_late[0])
    q_ffn = own_quarters(w_gate_up.reshape(shard, -1))
    places = (sources, home_spots, segc, segr, posc, cos_table, sin_table, perm)
    token_stack = token_near + [core_swap(v) for v in token_near]
    places, token_stack, cotangent, in_near, in_far, in_twin, late_near, q_ffn, late_twin = stage(
        places, token_stack, cotangent, in_near, in_far, in_twin, late_near, q_ffn, q_late[1]
    )
    sources, home_spots, segc, segr, posc, cos_table, sin_table, perm = places

    in_across = swap_line(in_near, in_far)
    ffn_near = gather_near(q_ffn[0])
    cot_pair = jnp.concatenate([cotangent, chip_swap(cotangent)], axis=0)
    late_far = gather_far(late_near)
    small_cols = slice(wide - LANES + heads, wide - free)
    small = jnp.concatenate([in_near[:, small_cols], in_far[:, small_cols]], axis=0)
    small = order_shards(small.reshape(fsdp_size, -1))
    ends = [sum(small_sizes[: i + 1]) for i in range(len(small_sizes))]
    smalls = [small[:, end - size : end] for end, size in zip(ends, small_sizes)]
    gains = jnp.stack([smalls[0].reshape(-1), smalls[1].reshape(-1)], axis=0).astype(BF)
    gains = dot_nn(gains, perm)
    gain_in, gain_mid = gains[0:1], gains[1:2]
    taps_one = smalls[2].reshape((fsdp_size,) + taps_x.shape).transpose(1, 2, 0, 3)
    taps_one = padded(taps_one.reshape(taps_x.shape[0], -1), 8, scan_width)
    taps_two = smalls[3].reshape((fsdp_size,) + taps_bc.shape).transpose(1, 0, 2)
    taps_two = padded(taps_two.reshape(taps_bc.shape[0], -1), 8, bc_width)
    gain_flat = smalls[4].reshape((fsdp_size,) + gain_mamba.shape).transpose(1, 0, 2)
    gain_flat = gain_flat.reshape(1, -1)
    heads_pad = padded(head_params, 8, LANES)
    skip = jnp.repeat(head_params[2], HD)[None, :]

    scan_args = (taps_one, taps_two, heads_pad, skip, segc, segr, posc)
    x_low, normed_in, inverse_in = pick_normed(sources, perm, gain_in, token_stack)
    in_across, normed_in, gain_mid, gain_flat, scan_args, late_far, cot_pair, ffn_near = stage(
        in_across, normed_in, gain_mid, gain_flat, scan_args, late_far, cot_pair, ffn_near
    )

    cot_near = [cot_pair, pair_swap(cot_pair)]
    in_half = join_half(in_near, in_far, in_twin, in_across)
    in_other = core_swap(in_half)
    late_across = swap_line(late_near, late_far)
    ffn_far = gather_far(ffn_near)
    y_scan, y_gate = project(normed_in, in_half, in_other, wide)
    scan_out, states = scan_fwd(y_scan, scan_width, *scan_args)
    attn_args = (query_width, scan_width, cos_table, sin_table, segc, segr)
    attn_rows = attention_fwd(y_gate, *attn_args)
    scan_out, attn_rows, late_across, ffn_far, cot_near = stage(
        scan_out, attn_rows, late_across, ffn_far, cot_near
    )

    ffn_operand = join_tail(ffn_near, ffn_far, 2 * ffn_near.shape[0] // fsdp_size)
    ffn_across = chip_swap(ffn_operand)
    late_half = join_half(late_near, late_far, late_twin, after(late_across, ffn_operand))
    late_rest = core_swap(late_half)
    out_width = query_width + scan_width
    gate_in = y_gate[:, :scan_width]
    sigma_in = jax.nn.sigmoid(gate_in)
    gated = scan_out * gate_in * sigma_in
    square_sum = jnp.sum(gated * gated, axis=1)
    square_sum = (square_sum + pair_swap(square_sum))[:, None]
    channels = scan_width * tp_size
    inverse_gate = lax.rsqrt(square_sum / channels + EPSILON)
    unit_gate = gated * inverse_gate
    mamba_rows = (unit_gate * gain_flat).astype(BF)
    branch_rows = jnp.concatenate([attn_rows, mamba_rows], axis=1)
    mixer = unproject([branch_rows], [(late_half, late_rest, 0)])
    mixer_half, mixer_rest = (pair_swap(v) for v in halves(mixer))
    ffn_half = join_half(ffn_near, ffn_far, q_ffn[1], after(ffn_across, mixer_half))
    ffn_other = core_swap(ffn_half)
    cot_stack = cot_near + [core_swap(v) for v in cot_near]
    cot_rows = pick_turned(sources, perm, after(cot_stack, mixer))
    mixer, mixer_half, mixer_rest, ffn_other, cot_rows = stage(
        mixer, mixer_half, mixer_rest, ffn_other, cot_rows
    )
    mixer_peer = jnp.concatenate([mixer_half, mixer_rest], axis=0)
    hidden = x_low.astype(F32) + (mixer.astype(F32) + mixer_peer.astype(F32))

    inverse_mid = inverse_norm(hidden)
    unit_mid = hidden * inverse_mid
    normed_mid = (unit_mid * gain_mid).astype(BF)
    activated, d_gate_up, d_mid = ffn_both_ways(
        normed_mid, cot_rows, ffn_half, ffn_other, late_half, late_rest, ffn_width, 1
    )

    d_mid_peer = pair_swap(d_mid)
    late_pairs = [(normed_mid, d_gate_up), (cot_rows, activated)]
    late_other = core_swap(grad_product(late_pairs, 1))
    late_grad = grad_product(late_pairs, 0)
    quarter_rows = fsdp_size * piece
    far_sum = add_low(late_grad[quarter_rows:], late_other[quarter_rows:])
    far_recv = chip_swap(far_sum)
    ffn_part = unproject([after(activated, d_mid_peer)], [(late_half, late_rest, 1)])
    d_mid, d_mid_peer, late_grad, late_other, far_sum, ffn_part = stage(
        d_mid, d_mid_peer, late_grad, late_other, far_sum, ffn_part
    )
    near_sum = add_low(late_grad[:quarter_rows], late_other[:quarter_rows])
    d_mid = d_mid.astype(F32) + d_mid_peer.astype(F32)

    ffn_own = lax.dynamic_slice_in_dim(ffn_part, own_start, tok_rows, 0).astype(F32)
    ffn_peer = pair_swap(lax.dynamic_slice_in_dim(ffn_part, peer_start, tok_rows, 0))
    d_hidden = cot_rows.astype(F32) + norm_back(d_mid, unit_mid, inverse_mid, gain_mid)
    g_norm_mid = jnp.sum(d_mid * unit_mid, axis=0, keepdims=True)
    d_mix = d_hidden.astype(BF)
    d_branch = turn_back(d_mix, late_half, late_rest, out_width)
    d_attn = d_branch[:, :query_width]
    d_mamba = d_branch[:, query_width:].astype(F32)
    scaled_gate = d_mamba * gain_flat
    gate_stat = jnp.sum(scaled_gate * unit_gate, axis=1)
    gate_stat = (gate_stat + pair_swap(gate_stat))[:, None]
    d_query = attention_bwd(y_gate, *attn_args, d_attn)
    g_gain = jnp.sum(d_mamba * unit_gate, axis=0, keepdims=True)
    gate_stat, d_query, far_recv = stage(gate_stat, d_query, far_recv)
    d_gated = inverse_gate * (scaled_gate - unit_gate * (gate_stat / channels))
    d_scan = d_gated * gate_in * sigma_in
    d_z = d_gated * scan_out * sigma_in * (1.0 + gate_in * (1.0 - sigma_in))
    dy_gate = jnp.concatenate([d_z.astype(BF), d_query], axis=1)
    out_pairs = [(d_mix, branch_rows), (normed_in, dy_gate)]
    out_other = core_swap(grad_product(out_pairs, 1))
    out_keep, out_far = halves(add_low(grad_product(out_pairs, 0), out_other))
    late_sum, late_send = halves(add_low(near_sum, far_recv))
    d_scan, late_sum, late_send, out_keep, out_far = stage(
        d_scan, late_sum, late_send, out_keep, out_far
    )
    out_far = chip_swap(out_far)
    late_recv = shard_swap(late_send, fsdp_size // 2)
    dy_scan, g_taps_one, g_taps_two, g_heads = scan_bwd(
        y_scan, scan_width, *scan_args, states, d_scan
    )
    hidden_own = lax.dynamic_slice_in_dim(hidden, own_start, tok_rows, 0)
    out_own = (hidden_own + ffn_own + after(ffn_peer, dy_scan).astype(F32)).astype(BF)
    out_own = dot_nt(out_own, perm).astype(BF)
    bc_cols = slice(scan_width, scan_width + bc_width)
    d_bc_peer = pair_swap(dy_scan[:, bc_cols])
    dy_scan, dy_gate, d_bc_peer, out_far, out_keep, out_own, late_recv = stage(
        dy_scan, dy_gate, d_bc_peer, out_far, out_keep, out_own, late_recv
    )

    out_keep, out_far = halves(add_low(out_keep, out_far))
    dy_gate, out_keep, out_far = stage(dy_gate, out_keep, out_far)
    out_far = shard_swap(out_far, fsdp_size // 2)
    d_in = unproject([dy_scan, dy_gate], [(in_half, in_other, 0), (in_half, in_other, 1)])
    d_in_peer = pair_swap(lax.dynamic_slice_in_dim(d_in, peer_start, tok_rows, 0))
    d_bc = add_low(dy_scan[:, bc_cols], d_bc_peer)
    dy_full = jnp.concatenate(
        [dy_scan[:, :scan_width], d_bc, dy_scan[:, scan_width + bc_width :]], axis=1
    )
    out_across = chip_swap(out_own)
    out_pair = jnp.concatenate([out_own, out_across], axis=0)
    late_keep, late_send = halves(add_low(late_sum, late_recv))
    late_recv = shard_swap(late_send, fsdp_size // 4)
    in_pairs = [(normed_in, after(dy_full, d_in_peer, out_far, late_recv, out_across))]
    in_other = core_swap(grad_product(in_pairs, 1))
    in_keep, in_far = halves(add_low(grad_product(in_pairs, 0), in_other))
    in_keep, in_far, d_in, d_in_peer, out_keep, out_far, out_pair, late_keep, late_recv = stage(
        in_keep, in_far, d_in, d_in_peer, out_keep, out_far, out_pair, late_keep, late_recv
    )

    def own_rows(v):
        return lax.dynamic_slice_in_dim(v, own_start, tok_rows, 0)

    d_in_own = own_rows(d_in).astype(F32) + d_in_peer.astype(F32)
    unit_own = own_rows(x_low).astype(F32) * own_rows(inverse_in)
    grad_own = own_rows(d_hidden) + norm_back(d_in_own, unit_own, own_rows(inverse_in), gain_in)
    g_norm_in = jnp.sum(d_in_own * unit_own, axis=0, keepdims=True)
    grad_own = dot_nt(grad_own.astype(BF), perm).astype(BF)
    in_recv = chip_swap(in_far)
    out_near = [out_pair, pair_swap(out_pair)]
    grad_pair = jnp.concatenate([grad_own, chip_swap(grad_own)], axis=0)
    def shards_sum(keep, far, gap):
        total = add_low(keep, far)
        while gap > 1:
            gap //= 2
            keep, far = halves(total)
            total = add_low(keep, shard_swap(far, gap))
        return total

    late_sum = shards_sum(late_keep, late_recv, fsdp_size // 4)
    out_sum = shards_sum(out_keep, out_far, fsdp_size // 2)
    grad_pair, in_keep, in_recv, late_sum, out_sum, out_near, g_norm_in = stage(
        grad_pair, in_keep, in_recv, late_sum, out_sum, out_near, g_norm_in
    )

    in_keep, in_far = halves(add_low(in_keep, in_recv))
    in_recv = shard_swap(in_far, fsdp_size // 2)
    grad_near = [grad_pair, pair_swap(grad_pair)]
    out_twin, late_twin = chip_swap(out_sum), chip_swap(late_sum)
    in_keep, in_recv, out_twin, late_twin = stage(in_keep, in_recv, out_twin, late_twin)

    out_sums = jnp.concatenate([out_sum, out_twin], axis=0)
    late_sums = jnp.concatenate([late_sum, late_twin], axis=0)
    in_sum = shards_sum(in_keep, in_recv, fsdp_size // 2)
    out_others, late_others = core_swap(out_sums), core_swap(late_sums)
    g_norms = dot_nt(
        jnp.concatenate([g_norm_in, g_norm_mid], axis=0), perm.astype(F32), PRECISE
    )
    g_norms, g_taps_two = g_norms.reshape(-1), g_taps_two[: taps_bc.shape[0]].reshape(-1)
    g_taps_one = g_taps_one[: taps_x.shape[0]].reshape(-1)
    g_heads = g_heads[:3, :heads].reshape(-1)
    g_gain = g_gain.reshape(-1)
    parts = (g_norms[:model_width], g_taps_two, g_norms[model_width:], g_taps_one, g_heads, g_gain)
    paired = model_width + g_taps_two.shape[0]
    sums = jnp.concatenate(parts)
    sums = after(sums, in_recv)
    sums = sums + core_swap(sums)
    sums = sums + chip_swap(sums)
    mixed_stack = out_near + [core_swap(v) for v in out_near]
    mixed_home = pick_rows(home_spots, [after(mixed_stack[0], in_recv)] + mixed_stack[1:])
    in_sum, out_others, late_others, mixed_home, sums, grad_near = stage(
        in_sum, out_others, late_others, mixed_home, sums, grad_near
    )

    in_twin = chip_swap(in_sum)
    grad_near += [core_swap(v) for v in grad_near]
    grad_attn_out, grad_mamba_out, grad_z, grad_query, grad_keyval = finish_out(
        ctx_index, out_sums, out_others, query_width, scan_width
    )
    sums = sums + shard_swap(sums, 1)
    in_twin, grad_near, grad_z, sums = stage(in_twin, grad_near, grad_z, sums)
    in_sums = jnp.concatenate([in_sum, in_twin], axis=0)
    grad_home = pick_rows(home_spots, grad_near)
    grad_gate_up, grad_down = finish_late(ctx_index, late_sums, late_others, ffn_width)
    gap = 2
    while gap < fsdp_size:
        sums = sums + shard_swap(sums, gap)
        gap *= 2
    sums = jnp.concatenate([sums[:paired] + pair_swap(sums[:paired]), sums[paired:]])
    grad_zx, grad_bc, grad_step = finish_scan(
        ctx_index, in_sums, core_swap(in_sums), grad_z, bc_width
    )
    ends = [sum(v.size for v in parts[: i + 1]) for i in range(len(parts))]
    sum_in, sum_two, sum_mid, sum_one, sum_heads, sum_gain = [
        sums[end - v.size : end] for end, v in zip(ends, parts)
    ]

    def shard_of(array, dim_index):
        piece = array.shape[dim_index] // fsdp_size
        return lax.dynamic_slice_in_dim(array, fsdp_index * piece, piece, dim_index)

    return (
        mixed_home,
        grad_home,
        shard_of(sum_in, 0),
        grad_query,
        grad_keyval.reshape(w_keyval.shape),
        grad_attn_out,
        grad_zx,
        grad_bc,
        grad_step[:, : w_step.shape[1]],
        sum_heads.reshape(head_params.shape),
        shard_of(sum_one.reshape(taps_x.shape[0], heads, HD), 2),
        shard_of(sum_two.reshape(taps_bc.shape[0], -1), 1),
        shard_of(sum_gain.reshape(heads, HD), 1),
        grad_mamba_out,
        shard_of(sum_mid, 0),
        grad_gate_up,
        grad_down,
    )


def solution(mesh):
    rows = P(("fsdp", "ctx", "tp"), None)
    in_specs = (
        rows,
        rows,
        P("fsdp", None),
        P("fsdp", None),
        P("fsdp"),
        P("fsdp", "tp"),
        P("fsdp", "tp", None),
        P("tp", "fsdp"),
        P("fsdp", None, "tp"),
        P("fsdp", None),
        P("fsdp", "tp"),
        P(None, "tp"),
        P(None, "tp", "fsdp"),
        P(None, "fsdp"),
        P("tp", "fsdp"),
        P("tp", "fsdp"),
        P("fsdp"),
        P("fsdp", None, "tp"),
        P("tp", "fsdp"),
    )
    out_specs = (
        rows,
        rows,
        P("fsdp"),
        P("fsdp", "tp"),
        P("fsdp", "tp", None),
        P("tp", "fsdp"),
        P("fsdp", None, "tp"),
        P("fsdp", None),
        P("fsdp", "tp"),
        P(None, "tp"),
        P(None, "tp", "fsdp"),
        P(None, "fsdp"),
        P("tp", "fsdp"),
        P("tp", "fsdp"),
        P("fsdp"),
        P("fsdp", None, "tp"),
        P("tp", "fsdp"),
    )
    return jax.shard_map(
        per_device, mesh=mesh, in_specs=in_specs, out_specs=out_specs, check_vma=False
    )
```

```python
import functools
import jax
import jax.numpy as jnp
from jax import lax
from jax.experimental import pallas as pl
from jax.experimental.pallas import tpu as pltpu
from jax.sharding import PartitionSpec as P

HD = 64
BLK = 128
LANES = 128
EPSILON = 1e-05
ROPE_BASE = 100000000000.0
PRECISE = lax.Precision.HIGHEST
F32 = jnp.float32
BF = jnp.bfloat16
FAR = -1e30


def dot_nn(a, b, precision=None):
    return lax.dot_general(
        a, b, (((1,), (0,)), ((), ())), precision=precision, preferred_element_type=F32
    )


def dot_nt(a, b, precision=None):
    return lax.dot_general(
        a, b, (((1,), (1,)), ((), ())), precision=precision, preferred_element_type=F32
    )


def dot_tn(a, b, precision=None):
    return lax.dot_general(
        a, b, (((0,), (0,)), ((), ())), precision=precision, preferred_element_type=F32
    )


def iota(shape, dim):
    return lax.broadcasted_iota(jnp.int32, shape, dim)


def two_terms(v):
    high = v.astype(BF)
    return high, (v - high.astype(F32)).astype(BF)


def spread_heads(v, spread):
    return dot_nn(jnp.concatenate(two_terms(v), axis=1), spread)


def sum_heads(v, spread):
    rows = v.shape[0]
    both = dot_nt(jnp.concatenate(two_terms(v), axis=0), spread[:LANES])
    return both[:rows] + both[rows:]


def swap_halves(v):
    lanes = v.shape[1]
    low = (iota(v.shape, 1) & (HD - 1)) < HD // 2
    return jnp.where(low, pltpu.roll(v, lanes - HD // 2, 1), pltpu.roll(v, HD // 2, 1))


def split_pair(v):
    first = iota(v.shape, 1) < HD
    zero = jnp.zeros_like(v)
    return jnp.concatenate([jnp.where(first, v, zero), jnp.where(first, zero, v)], axis=0)


def keys_values(kv, cos, sin):
    first = iota(kv.shape, 1) < HD
    roped = kv * cos + swap_halves(kv) * sin
    keys = jnp.where(first, roped, 0.0)
    values = jnp.where(first, 0.0, kv)
    key_pair = (keys.astype(BF), pltpu.roll(keys, HD, 1).astype(BF))
    value_pair = (pltpu.roll(values, HD, 1).astype(BF), values.astype(BF))
    return key_pair, value_pair


def attention_probs(query, key, allowed):
    scores = dot_nt(query, key) * HD ** (-0.5)
    scores = jnp.where(allowed, scores, FAR)
    weights = jnp.exp(scores - jnp.max(scores, axis=1, keepdims=True))
    return weights / jnp.sum(weights, axis=1, keepdims=True)


def allowed_rows(segc, segr, lower, count):
    keys = lower + count
    same = segc[lower:keys, :] == segr[:, :keys]
    return same & (iota((count, keys), 0) + lower >= iota((count, keys), 1))


def attention_fwd_kernel(q_ref, kv_ref, cos_ref, sin_ref, segc_ref, segr_ref, out_ref):
    rows, width = q_ref.shape
    cos, sin = cos_ref[...], sin_ref[...]
    key_pair, value_pair = keys_values(kv_ref[...], cos, sin)
    segc, segr = segc_ref[...], segr_ref[...]
    for pair in range(width // LANES):
        cols = slice(pair * LANES, (pair + 1) * LANES)
        raw = q_ref[:, cols]
        query = (raw * cos + swap_halves(raw) * sin).astype(BF)
        for lower in range(0, rows, BLK):
            keys = lower + BLK
            allowed = allowed_rows(segc, segr, lower, BLK)
            total = None
            for side in range(2):
                probs = attention_probs(query[lower:keys], key_pair[side][:keys], allowed)
                part = dot_nn(probs.astype(BF), value_pair[side][:keys])
                total = part if total is None else total + part
            out_ref[lower:keys, cols] = total.astype(BF)


def attention_bwd_kernel(
    q_ref, kv_ref, cos_ref, sin_ref, segc_ref, segr_ref, do_ref, out_ref, dk_ref, dv_ref
):
    rows, width = q_ref.shape
    cos, sin = cos_ref[...], sin_ref[...]
    key_pair, value_pair = keys_values(kv_ref[...], cos, sin)
    segc, segr = segc_ref[...], segr_ref[...]
    dk_ref[...] = jnp.zeros_like(dk_ref)
    dv_ref[...] = jnp.zeros_like(dv_ref)
    for pair in range(width // LANES):
        cols = slice(pair * LANES, (pair + 1) * LANES)
        raw = q_ref[:, cols]
        query = (raw * cos + swap_halves(raw) * sin).astype(BF)
        for lower in range(0, rows, BLK):
            keys = lower + BLK
            allowed = allowed_rows(segc, segr, lower, BLK)
            query_part = query[lower:keys]
            grad = do_ref[lower:keys, cols]
            d_query = None
            probs_all, scores_all = [], []
            for side in range(2):
                probs = attention_probs(query_part, key_pair[side][:keys], allowed)
                d_probs = dot_nt(grad, value_pair[side][:keys])
                inner = jnp.sum(d_probs * probs, axis=1, keepdims=True)
                d_scores = (probs * (d_probs - inner)).astype(BF)
                part = dot_nn(d_scores, key_pair[side][:keys])
                d_query = part if d_query is None else d_query + part
                probs_all.append(probs.astype(BF))
                scores_all.append(d_scores)
            dv_ref[:keys, :] += dot_tn(jnp.concatenate(probs_all, axis=0), split_pair(grad))
            dk_ref[:keys, :] += dot_tn(jnp.concatenate(scores_all, axis=0), split_pair(query_part))
            d_query = d_query * HD ** (-0.5)
            cos_part, sin_part = cos[lower:keys], sin[lower:keys]
            out_ref[lower:keys, cols] = (
                d_query * cos_part - swap_halves(d_query) * sin_part
            ).astype(BF)
    first = iota(dk_ref.shape, 1) < HD
    d_key = dk_ref[...]
    d_key = (d_key + pltpu.roll(d_key, HD, 1)) * HD ** (-0.5)
    d_key = d_key * cos - swap_halves(d_key) * sin
    d_value = dv_ref[...]
    d_value = d_value + pltpu.roll(d_value, HD, 1)
    out_ref[:, width:] = jnp.where(first, d_key, d_value).astype(BF)


def conv_rows(signal, taps_ref, position):
    total = taps_ref[4:5, :] + taps_ref[3:4, :] * signal
    for lag in range(1, 4):
        moved = jnp.where(position >= lag, pltpu.roll(signal, lag, 0), 0.0)
        total = total + taps_ref[3 - lag : 4 - lag, :] * moved
    return total


def conv_back(signal, d_pre, taps_ref, grad_ref, position):
    rows = signal.shape[0]
    grad_ref[...] = jnp.zeros_like(grad_ref)
    grad_ref[4:5, :] = jnp.sum(d_pre, axis=0, keepdims=True)
    grad_ref[3:4, :] = jnp.sum(d_pre * signal, axis=0, keepdims=True)
    total = taps_ref[3:4, :] * d_pre
    for lag in range(1, 4):
        kept = jnp.where(position >= lag, d_pre, 0.0)
        grad_ref[3 - lag : 4 - lag, :] = jnp.sum(
            kept * pltpu.roll(signal, lag, 0), axis=0, keepdims=True
        )
        total = total + taps_ref[3 - lag : 4 - lag, :] * pltpu.roll(kept, rows - lag, 0)
    return total


def softplus(v):
    return jnp.maximum(v, 0.0) + jnp.log1p(jnp.exp(-jnp.abs(v)))


def spread_matrix(width):
    shape = (2 * LANES, width)
    return ((iota(shape, 0) & (LANES - 1)) == (iota(shape, 1) >> 6)).astype(F32).astype(BF)


def scan_setup(step_ref, heads_ref):
    steps = softplus(step_ref[...] + heads_ref[0:1, :])
    rates = -jnp.exp(heads_ref[1:2, :])
    return steps, rates


def block_decays(steps, rates, segc, lower):
    upper = lower + BLK
    shape = (BLK, BLK)
    lower_ones = (iota(shape, 0) >= iota(shape, 1)).astype(F32)
    low_ones = lower_ones.astype(BF)
    decays = dot_nn(
        jnp.concatenate([low_ones, low_ones], axis=1),
        jnp.concatenate(two_terms(steps[lower:upper] * rates), axis=0),
    )
    seg_part = segc[lower:upper]
    if lower == 0:
        arrive = None
    else:
        carried = seg_part == segc[lower - 1 : lower]
        arrive = jnp.where(carried, jnp.exp(decays), 0.0)
    kept = seg_part == segc[upper - 1 : upper]
    leave = jnp.where(kept, jnp.exp(decays[BLK - 1 : BLK] - decays), 0.0)
    return decays, arrive, leave, lower_ones


def block_mixing(decays, decays_t, head, allowed):
    gap = decays[:, head : head + 1] - decays_t[head : head + 1, :]
    return jnp.exp(jnp.where(allowed, gap, FAR))


def scan_fwd_kernel(
    x_ref, bc_ref, step_ref, tapx_ref, tapbc_ref, heads_ref, skip_ref, segc_ref, segr_ref,
    pos_ref, out_ref, states_ref,
):
    rows, width = x_ref.shape
    position = pos_ref[...]
    segc, segr = segc_ref[...], segr_ref[...]
    conv_x = jax.nn.silu(conv_rows(x_ref[...], tapx_ref, position)).astype(BF)
    conv_bc = jax.nn.silu(conv_rows(bc_ref[...], tapbc_ref, position)).astype(BF)
    steps, rates = scan_setup(step_ref, heads_ref)
    spread = spread_matrix(width)
    scaled = conv_x.astype(F32) * spread_heads(steps, spread)
    state = None
    for lower in range(0, rows, BLK):
        upper = lower + BLK
        b_part = conv_bc[lower:upper, :LANES]
        c_part = conv_bc[lower:upper, LANES:]
        decays, arrive, leave, lower_ones = block_decays(steps, rates, segc, lower)
        decays_t = decays.T
        allowed = (segc[lower:upper] == segr[:, lower:upper]) & (lower_ones > 0.0)
        inner = dot_nt(c_part, b_part)
        scaled_part = scaled[lower:upper]
        scaled_low = scaled_part.astype(BF)
        fresh = dot_tn(b_part, (scaled_part * spread_heads(leave, spread)).astype(BF))
        if state is None:
            recall = None
            states_ref[lower // BLK] = jnp.zeros(fresh.shape, F32)
            state = fresh
        else:
            arrive_wide = spread_heads(arrive, spread)
            recall = dot_nn(c_part, state.astype(BF)) * arrive_wide
            states_ref[lower // BLK] = state
            state = state * arrive_wide[BLK - 1 : BLK] + fresh
        for pair in range(width // LANES):
            cols = slice(pair * LANES, (pair + 1) * LANES)
            mixes = [
                (block_mixing(decays, decays_t, 2 * pair + side, allowed) * inner).astype(BF)
                for side in range(2)
            ]
            local = dot_nn(jnp.concatenate(mixes, axis=1), split_pair(scaled_low[:, cols]))
            if recall is not None:
                local = local + recall[:, cols]
            out_ref[lower:upper, cols] = local + skip_ref[0:1, cols] * conv_x[
                lower:upper, cols
            ].astype(F32)


def scan_bwd_kernel(
    x_ref, bc_ref, step_ref, tapx_ref, tapbc_ref, heads_ref, skip_ref, segc_ref, segr_ref,
    pos_ref, states_ref, dy_ref, out_ref, gtapx_ref, gtapbc_ref, gheads_ref, dx_ref, dbc_ref,
):
    rows, width = x_ref.shape
    position = pos_ref[...]
    segc, segr = segc_ref[...], segr_ref[...]
    pre_x = conv_rows(x_ref[...], tapx_ref, position)
    pre_bc = conv_rows(bc_ref[...], tapbc_ref, position)
    conv_x = jax.nn.silu(pre_x).astype(BF)
    conv_bc = jax.nn.silu(pre_bc).astype(BF)
    steps, rates = scan_setup(step_ref, heads_ref)
    spread = spread_matrix(width)
    steps_wide = spread_heads(steps, spread)
    lane = iota((BLK, LANES), 1)
    sub = iota((LANES, BLK), 0)
    last_row = iota((BLK, LANES), 0) == BLK - 1
    d_state = None
    g_bias = jnp.zeros((1, LANES), F32)
    g_rate = jnp.zeros((1, LANES), F32)
    g_skip = jnp.zeros((1, width), F32)
    for lower in range(rows - BLK, -1, -BLK):
        upper = lower + BLK
        b_part = conv_bc[lower:upper, :LANES]
        c_part = conv_bc[lower:upper, LANES:]
        decays, arrive, leave, lower_ones = block_decays(steps, rates, segc, lower)
        decays_t = decays.T
        allowed = (segc[lower:upper] == segr[:, lower:upper]) & (lower_ones > 0.0)
        inner = dot_nt(c_part, b_part)
        x_part = conv_x[lower:upper].astype(F32)
        scaled_part = x_part * steps_wide[lower:upper]
        scaled_low = scaled_part.astype(BF)
        grad = dy_ref[lower:upper, :]
        grad_low = grad.astype(BF)
        d_scaled = []
        d_inner = jnp.zeros((BLK, BLK), F32)
        row_sums = jnp.zeros((BLK, LANES), F32)
        col_sums = jnp.zeros((LANES, BLK), F32)
        for pair in range(width // LANES):
            cols = slice(pair * LANES, (pair + 1) * LANES)
            grad_pair = split_pair(grad_low[:, cols])
            d_mix = dot_nt(grad_pair, scaled_low[:, cols])
            mixes = []
            for side in range(2):
                head = 2 * pair + side
                mixing = block_mixing(decays, decays_t, head, allowed)
                mix = mixing * inner
                d_part = d_mix[side * BLK : (side + 1) * BLK]
                d_inner = d_inner + d_part * mixing
                both = d_part * mix
                row_sums = jnp.where(lane == head, jnp.sum(both, axis=1, keepdims=True), row_sums)
                col_sums = jnp.where(sub == head, jnp.sum(both, axis=0, keepdims=True), col_sums)
                mixes.append(mix.astype(BF))
            d_scaled.append(dot_tn(jnp.concatenate(mixes, axis=0), grad_pair))
        d_scaled = jnp.concatenate(d_scaled, axis=1)
        d_decays = row_sums - col_sums.T
        d_inner = d_inner.astype(BF)
        d_c = dot_nn(d_inner, b_part)
        d_b = dot_tn(d_inner, c_part)
        if lower > 0:
            arrive_wide = spread_heads(arrive, spread)
            state = states_ref[lower // BLK]
            state_low = state.astype(BF)
            recall = dot_nn(c_part, state_low) * arrive_wide
            d_decays = d_decays + sum_heads(recall * grad, spread)
            grad_in = (grad * arrive_wide).astype(BF)
            d_c = d_c + dot_nt(grad_in, state_low)
        if d_state is not None:
            state_grad = d_state.astype(BF)
            leave_wide = spread_heads(leave, spread)
            d_kept = dot_nn(b_part, state_grad) * leave_wide
            d_b = d_b + dot_nt((scaled_part * leave_wide).astype(BF), state_grad)
            d_leave = sum_heads(d_kept * scaled_part, spread)
            d_last = jnp.sum(d_leave, axis=0, keepdims=True)
            if lower > 0:
                lingering = jnp.sum(d_state * state, axis=0, keepdims=True)
                lingering = lingering * arrive_wide[BLK - 1 : BLK]
                d_last = d_last + sum_heads(jnp.broadcast_to(lingering, (16, width)), spread)[0:1]
            d_decays = d_decays - d_leave + jnp.where(last_row, d_last, 0.0)
            d_scaled = d_scaled + d_kept
        if lower > 0:
            d_new = dot_tn(c_part, grad_in)
            if d_state is None:
                d_state = d_new
            else:
                d_state = d_state * arrive_wide[BLK - 1 : BLK] + d_new
        low_ones = lower_ones.astype(BF)
        d_log = dot_tn(
            jnp.concatenate([low_ones, low_ones], axis=0),
            jnp.concatenate(two_terms(d_decays), axis=0),
        )
        steps_part = steps[lower:upper]
        d_steps = sum_heads(d_scaled * x_part, spread) + d_log * rates
        d_step_in = d_steps * jax.nn.sigmoid(step_ref[lower:upper, :] + heads_ref[0:1, :])
        g_bias = g_bias + jnp.sum(d_step_in, axis=0, keepdims=True)
        g_rate = g_rate + jnp.sum(d_log * steps_part, axis=0, keepdims=True) * rates
        g_skip = g_skip + jnp.sum(grad * x_part, axis=0, keepdims=True)
        out_ref[lower:upper, width + 2 * LANES :] = d_step_in.astype(BF)
        dx_ref[lower:upper, :] = d_scaled * steps_wide[lower:upper] + grad * skip_ref[0:1, :]
        dbc_ref[lower:upper, :LANES] = d_b
        dbc_ref[lower:upper, LANES:] = d_c
    gheads_ref[...] = jnp.zeros_like(gheads_ref)
    gheads_ref[0:1, :] = g_bias
    gheads_ref[1:2, :] = g_rate
    gheads_ref[2:3, :] = sum_heads(jnp.broadcast_to(g_skip, (16, width)), spread)[0:1]
    gate = jax.nn.sigmoid(pre_x)
    d_pre = dx_ref[...] * gate * (1.0 + pre_x * (1.0 - gate))
    out_ref[:, :width] = conv_back(x_ref[...], d_pre, tapx_ref, gtapx_ref, position).astype(BF)
    gate = jax.nn.sigmoid(pre_bc)
    d_pre = dbc_ref[...] * gate * (1.0 + pre_bc * (1.0 - gate))
    out_ref[:, width : width + 2 * LANES] = conv_back(
        bc_ref[...], d_pre, tapbc_ref, gtapbc_ref, position
    ).astype(BF)


def select_parts(spot_ref, part_refs):
    spots = spot_ref[...]
    total, first = None, 0
    for part_ref in part_refs:
        shape = (spots.shape[0], part_ref.shape[0])
        chosen = (spots == iota(shape, 1) + first).astype(F32).astype(BF)
        product = dot_nn(chosen, part_ref[...])
        total = product if total is None else total + product
        first += part_ref.shape[0]
    return total


def pick_kernel(spot_ref, *refs):
    refs[-1][...] = select_parts(spot_ref, refs[:-1]).astype(BF)


def pick_turn_kernel(spot_ref, perm_ref, *refs):
    rows = select_parts(spot_ref, refs[:-1]).astype(BF)
    refs[-1][...] = dot_nn(rows, perm_ref[...]).astype(BF)


def pick_norm_kernel(spot_ref, perm_ref, gain_ref, *refs):
    rows_ref, normed_ref, inverse_ref = refs[-3:]
    rows = select_parts(spot_ref, refs[:-3]).astype(BF)
    rows = dot_nn(rows, perm_ref[...])
    inverse = lax.rsqrt(jnp.mean(rows * rows, axis=1, keepdims=True) + EPSILON)
    rows_ref[...] = rows.astype(BF)
    normed_ref[...] = (rows * inverse * gain_ref[...]).astype(BF)
    inverse_ref[...] = inverse


def join_kernel(*refs):
    start = 0
    for ref in refs[:-1]:
        refs[-1][start : start + ref.shape[0], :] = ref[...]
        start += ref.shape[0]


def join_tail_kernel(piece, near_ref, far_ref, out_ref):
    start = near_ref.shape[0] - piece
    out_ref[:start, :] = near_ref[piece:, :]
    out_ref[start:, :] = far_ref[...]


def grad_kernel(*refs):
    first = 0
    for left_ref, right_ref in zip(refs[:-1:2], refs[1:-1:2]):
        width = right_ref.shape[1]
        refs[-1][:, first : first + width] = dot_tn(left_ref[...], right_ref[...]).astype(BF)
        first += width


def ordered_rows(index_ref, own_ref, other_ref):
    index = index_ref[0]
    core_bit, chip_bit = (index & 1) == 1, (index & 2) == 2
    piece = own_ref.shape[0] // 2
    own, other = own_ref[...].astype(F32), other_ref[...].astype(F32)
    by_gap = (own[:piece], other[:piece], own[piece:], other[piece:])
    rows = []
    for quarter in range(4):
        near = jnp.where(core_bit, by_gap[quarter ^ 1], by_gap[quarter])
        far = jnp.where(core_bit, by_gap[quarter ^ 3], by_gap[quarter ^ 2])
        rows.append(jnp.where(chip_bit, far, near))
    return jnp.concatenate(rows, axis=0)


def finish_late_kernel(index_ref, own_ref, other_ref, up_ref, down_ref):
    rows = ordered_rows(index_ref, own_ref, other_ref)
    width = up_ref.shape[2]
    up_ref[:, 0, :] = rows[:, :width]
    up_ref[:, 1, :] = rows[:, width : 2 * width]
    down_ref[...] = rows[:, 2 * width :].T


def finish_out_kernel(
    index_ref, own_ref, other_ref, attn_ref, mamba_ref, z_ref, query_ref, keyval_ref
):
    rows = ordered_rows(index_ref, own_ref, other_ref)
    first = 0
    for ref in (attn_ref, mamba_ref):
        ref[...] = rows[:, first : first + ref.shape[0]].T
        first += ref.shape[0]
    for ref in (z_ref, query_ref, keyval_ref):
        ref[...] = rows[:, first : first + ref.shape[1]]
        first += ref.shape[1]


def finish_scan_kernel(index_ref, own_ref, other_ref, z_ref, zx_ref, bc_ref, step_ref):
    rows = ordered_rows(index_ref, own_ref, other_ref)
    width = z_ref.shape[1]
    zx_ref[:, 0, :] = z_ref[...]
    zx_ref[:, 1, :] = rows[:, :width]
    bc_ref[...] = rows[:, width : width + bc_ref.shape[1]]
    step_ref[...] = rows[:, width + bc_ref.shape[1] :]


def ffn_kernel(
    normed_ref, cot_ref, near_ref, far_ref, back_near_ref, back_far_ref, act_ref, grad_ref, mid_ref
):
    half = near_ref.shape[0]
    width = act_ref.shape[1]
    tile = 512
    total = [None, None]
    for first in range(0, width, tile):
        gate_cols = slice(first, first + tile)
        up_cols = slice(width + first, width + first + tile)

        def product(left_ref, near, far, cols):
            return dot_nn(left_ref[:, :half], near[:, cols]) + dot_nn(
                left_ref[:, half:], far[:, cols]
            )

        gate = product(normed_ref, near_ref, far_ref, gate_cols)
        up = product(normed_ref, near_ref, far_ref, up_cols)
        d_act = product(cot_ref, back_near_ref, back_far_ref, gate_cols)
        sigma = jax.nn.sigmoid(gate)
        silu = gate * sigma
        act_ref[:, gate_cols] = (silu * up).astype(BF)
        d_gate = (d_act * up * sigma * (1.0 + gate * (1.0 - sigma))).astype(BF)
        d_up = (d_act * silu).astype(BF)
        grad_ref[:, gate_cols] = d_gate
        grad_ref[:, up_cols] = d_up
        for i, ref in enumerate((near_ref, far_ref)):
            part = dot_nt(d_gate, ref[:, gate_cols]) + dot_nt(d_up, ref[:, up_cols])
            total[i] = part if total[i] is None else total[i] + part
    mid_ref[:, :half] = total[0].astype(BF)
    mid_ref[:, half:] = total[1].astype(BF)


def project_kernel(rows_ref, near_ref, far_ref, *outs):
    half = near_ref.shape[0]
    first = 0
    for out_ref in outs:
        cols = slice(first, first + out_ref.shape[1])
        out_ref[...] = dot_nn(rows_ref[:, :half], near_ref[:, cols]) + dot_nn(
            rows_ref[:, half:], far_ref[:, cols]
        )
        first += out_ref.shape[1]


def turn_back_kernel(rows_ref, near_ref, far_ref, out_ref):
    half = near_ref.shape[0]
    out_ref[...] = (
        dot_nn(rows_ref[:, :half], near_ref[...]) + dot_nn(rows_ref[:, half:], far_ref[...])
    ).astype(BF)


def unproject_kernel(count, *refs):
    out_ref = refs[-1]
    half = refs[count].shape[0]
    for side in range(2):
        total = None
        for i in range(count):
            part = dot_nt(refs[i][...], refs[count + 2 * i + side][...])
            total = part if total is None else total + part
        out_ref[:, side * half : (side + 1) * half] = total.astype(BF)


VMEM_BYTES = 48 * 1024 * 1024


def column_block(rows, width, index):
    return pl.BlockSpec((rows, width), lambda i: (0, index))


def whole_block(shape):
    zeros = (0,) * len(shape)
    return pl.BlockSpec(shape, lambda i: zeros)


def single_step(kernel, in_specs, outs, scratch=(), flops=1024):
    return pl.pallas_call(
        kernel,
        grid=(1,),
        in_specs=in_specs,
        out_specs=[whole_block(o.shape) for o in outs],
        out_shape=outs,
        scratch_shapes=list(scratch),
        compiler_params=pltpu.CompilerParams(vmem_limit_bytes=VMEM_BYTES),
        cost_estimate=pl.CostEstimate(flops=flops, bytes_accessed=1024, transcendentals=0),
    )


def attention_specs(rows, width, gate_width):
    return [
        column_block(rows, width, gate_width // width),
        column_block(rows, LANES, (gate_width + width) // LANES),
        whole_block((rows, LANES)),
        whole_block((rows, LANES)),
        whole_block((rows, 1)),
        whole_block((1, rows)),
    ]


def attention_fwd(y_a, width, gate_width, cos, sin, segc, segr):
    rows = y_a.shape[0]
    return single_step(
        attention_fwd_kernel,
        attention_specs(rows, width, gate_width),
        [jax.ShapeDtypeStruct((rows, width), BF)],
    )(y_a, y_a, cos, sin, segc, segr)[0]


def attention_bwd(y_a, width, gate_width, cos, sin, segc, segr, d_attn):
    rows = y_a.shape[0]
    return single_step(
        attention_bwd_kernel,
        attention_specs(rows, width, gate_width) + [whole_block((rows, width))],
        [jax.ShapeDtypeStruct((rows, width + LANES), BF)],
        [pltpu.VMEM((rows, LANES), F32), pltpu.VMEM((rows, LANES), F32)],
    )(y_a, y_a, cos, sin, segc, segr, d_attn)[0]


def scan_specs(rows, width):
    return [
        column_block(rows, width, 0),
        column_block(rows, 2 * LANES, width // (2 * LANES)),
        column_block(rows, LANES, (width + 2 * LANES) // LANES),
        whole_block((8, width)),
        whole_block((8, 2 * LANES)),
        whole_block((8, LANES)),
        whole_block((1, width)),
        whole_block((rows, 1)),
        whole_block((1, rows)),
        whole_block((rows, 1)),
    ]


def scan_fwd(y_b, width, taps_x, taps_bc, heads, skip, segc, segr, position):
    rows = y_b.shape[0]
    return single_step(
        scan_fwd_kernel,
        scan_specs(rows, width),
        [
            jax.ShapeDtypeStruct((rows, width), F32),
            jax.ShapeDtypeStruct((rows // BLK, LANES, width), F32),
        ],
    )(y_b, y_b, y_b, taps_x, taps_bc, heads, skip, segc, segr, position)


def scan_bwd(y_b, width, taps_x, taps_bc, heads, skip, segc, segr, position, states, d_out):
    rows = y_b.shape[0]
    return single_step(
        scan_bwd_kernel,
        scan_specs(rows, width)
        + [whole_block(states.shape), whole_block((rows, width))],
        [
            jax.ShapeDtypeStruct(y_b.shape, BF),
            jax.ShapeDtypeStruct((8, width), F32),
            jax.ShapeDtypeStruct((8, 2 * LANES), F32),
            jax.ShapeDtypeStruct((8, LANES), F32),
        ],
        [pltpu.VMEM((rows, width), F32), pltpu.VMEM((rows, 2 * LANES), F32)],
    )(y_b, y_b, y_b, taps_x, taps_bc, heads, skip, segc, segr, position, states, d_out)


def pick_rows(spots, parts):
    operands = (spots[:, None],) + tuple(parts)
    return single_step(
        pick_kernel,
        [whole_block(v.shape) for v in operands],
        [jax.ShapeDtypeStruct((spots.shape[0], parts[0].shape[1]), BF)],
    )(*operands)[0]


def pick_turned(spots, perm, parts):
    operands = (spots[:, None], perm) + tuple(parts)
    return single_step(
        pick_turn_kernel,
        [whole_block(v.shape) for v in operands],
        [jax.ShapeDtypeStruct((spots.shape[0], perm.shape[1]), BF)],
    )(*operands)[0]


def pick_normed(spots, perm, gain, parts):
    rows = spots.shape[0]
    operands = (spots[:, None], perm, gain) + tuple(parts)
    wide = jax.ShapeDtypeStruct((rows, perm.shape[1]), BF)
    return single_step(
        pick_norm_kernel,
        [whole_block(v.shape) for v in operands],
        [wide, wide, jax.ShapeDtypeStruct((rows, 1), F32)],
    )(*operands)


def join_blocks(operands, specs, width):
    rows = sum(spec.block_shape[0] for spec in specs)
    return single_step(join_kernel, specs, [jax.ShapeDtypeStruct((rows, width), BF)])(*operands)[0]


def ffn_both_ways(normed, cot_rows, near, far, back_near, back_far, width, back_index):
    rows, model_width = normed.shape
    half = near.shape[0]
    return single_step(
        ffn_kernel,
        [whole_block(normed.shape), whole_block(cot_rows.shape)]
        + [whole_block(near.shape), whole_block(far.shape)]
        + [column_block(half, width, back_index), column_block(half, width, back_index)],
        [
            jax.ShapeDtypeStruct((rows, width), BF),
            jax.ShapeDtypeStruct((rows, 2 * width), BF),
            jax.ShapeDtypeStruct((rows, model_width), BF),
        ],
    )(normed, cot_rows, near, far, back_near, back_far)


def project(rows, near, far, width):
    count = near.shape[1] // width
    shape = jax.ShapeDtypeStruct((rows.shape[0], width), F32)
    operands = (rows, near, far)
    return single_step(
        project_kernel, [whole_block(v.shape) for v in operands], [shape] * count
    )(*operands)


def turn_back(rows, near, far, width):
    half = near.shape[0]
    return single_step(
        turn_back_kernel,
        [whole_block(rows.shape), column_block(half, width, 0), column_block(half, width, 0)],
        [jax.ShapeDtypeStruct((rows.shape[0], width), BF)],
    )(rows, near, far)[0]


def unproject(lefts, blocks):
    specs = [whole_block(v.shape) for v in lefts]
    operands = list(lefts)
    for left, (near, far, index) in zip(lefts, blocks):
        specs += [column_block(near.shape[0], left.shape[1], index)] * 2
        operands += [near, far]
    rows, half = lefts[0].shape[0], blocks[0][0].shape[0]
    return single_step(
        functools.partial(unproject_kernel, len(lefts)),
        specs,
        [jax.ShapeDtypeStruct((rows, 2 * half), BF)],
    )(*operands)[0]


def join_tail(near, far, piece):
    rows = near.shape[0] + far.shape[0] - piece
    return single_step(
        functools.partial(join_tail_kernel, piece),
        [whole_block(near.shape), whole_block(far.shape)],
        [jax.ShapeDtypeStruct((rows, near.shape[1]), BF)],
    )(near, far)[0]


def grad_product(pairs, side):
    half = pairs[0][0].shape[1] // 2
    specs, operands = [], []
    for left, right in pairs:
        specs += [column_block(left.shape[0], half, side), whole_block(right.shape)]
        operands += [left, right]
    width = sum(right.shape[1] for left, right in pairs)
    return single_step(grad_kernel, specs, [jax.ShapeDtypeStruct((half, width), BF)])(*operands)[0]


def finish(kernel, index, operands, shapes):
    return single_step(
        kernel,
        [pl.BlockSpec(memory_space=pltpu.SMEM)] + [whole_block(v.shape) for v in operands],
        [jax.ShapeDtypeStruct(shape, F32) for shape in shapes],
    )(index.astype(jnp.int32).reshape(1), *operands)


def finish_late(index, own, other, width):
    rows = 2 * own.shape[0]
    shapes = [(rows, 2, width), (own.shape[1] - 2 * width, rows)]
    return finish(finish_late_kernel, index, (own, other), shapes)


def finish_out(index, own, other, query_width, scan_width):
    rows = 2 * own.shape[0]
    shapes = [(query_width, rows), (scan_width, rows)]
    shapes += [(rows, scan_width), (rows, query_width), (rows, LANES)]
    return finish(finish_out_kernel, index, (own, other), shapes)


def finish_scan(index, own, other, grad_z, bc_width):
    rows, scan_width = grad_z.shape
    shapes = [(rows, 2, scan_width), (rows, bc_width), (rows, LANES)]
    return finish(finish_scan_kernel, index, (own, other, grad_z), shapes)


CORE_SWAP = [(0, 1), (1, 0), (2, 3), (3, 2)]
CHIP_SWAP = [(0, 2), (2, 0), (1, 3), (3, 1)]
PAIR_SWAP = [(0, 1), (1, 0)]
def core_swap(v):
    return lax.ppermute(v, "ctx", CORE_SWAP)


def chip_swap(v):
    return lax.ppermute(v, "ctx", CHIP_SWAP)


def pair_swap(v):
    return lax.ppermute(v, "tp", PAIR_SWAP)


def shard_swap(v, gap):
    size = lax.axis_size("fsdp")
    return lax.ppermute(v, "fsdp", [(i, i ^ gap) for i in range(size)])


def quarter_perm(width):
    size = lax.axis_size("fsdp")
    shard = width // size
    piece = shard // 4
    spots = jnp.arange(width, dtype=jnp.int32)
    slot = spots // (size * piece)
    turn = (spots // piece) % size
    within = spots % piece
    quarter = jnp.where(slot == 1, 2, jnp.where(slot == 2, 1, slot)) ^ lax.axis_index("ctx")
    owner = lax.axis_index("fsdp") ^ turn
    column = owner * shard + quarter * piece + within
    return (spots[:, None] == column[None, :]).astype(BF)


def after(v, *others):
    return lax.optimization_barrier((v,) + others)[0]


def own_quarters(shard, sideways=False):
    index = lax.axis_index("ctx")
    if sideways:
        count = shard.shape[1]
        piece = count // 4
        place = jnp.arange(2 * piece, dtype=jnp.int32)
        column = (index ^ (2 * (place // piece))) * piece + place % piece
        chosen = (jnp.arange(count, dtype=jnp.int32)[None, :] == column[:, None]).astype(BF)
        both = dot_nt(chosen, shard).astype(BF)
        return both[:piece], both[piece:]
    piece = shard.shape[0] // 4
    return tuple(
        lax.dynamic_slice_in_dim(shard, (index ^ gap) * piece, piece, 0) for gap in (0, 2)
    )


def stage(*values):
    return lax.optimization_barrier(values)


def gather_near(own):
    line, gap = own, 1
    while 2 * gap < lax.axis_size("fsdp"):
        line = jnp.concatenate([line, shard_swap(line, gap)], axis=0)
        gap *= 2
    return line


def gather_far(near):
    return shard_swap(near, lax.axis_size("fsdp") // 2)


def swap_line(near, far):
    return chip_swap(join_tail(near, far, near.shape[0] * 2 // lax.axis_size("fsdp")))


def join_half(*parts):
    specs = [whole_block(v.shape) for v in parts]
    return join_blocks(parts, specs, parts[0].shape[1])


def order_shards(rows):
    owner = jnp.arange(rows.shape[0], dtype=jnp.int32)
    turn = lax.axis_index("fsdp") ^ owner
    return dot_nn((turn[:, None] == owner[None, :]).astype(BF), rows)


def add_low(left, right):
    return (left.astype(F32) + right.astype(F32)).astype(BF)


def halves(v):
    half = v.shape[0] // 2
    return v[:half], v[half:]


def direct_near(rows):
    near = [rows, chip_swap(rows), pair_swap(rows)]
    return near + [lax.ppermute(rows, ("ctx", "tp"), [(i, i ^ 5) for i in range(8)])]


def stack_spot(spot, rows):
    member = spot // rows
    gap = (member // 2) ^ lax.axis_index("ctx")
    turn = (member % 2) ^ lax.axis_index("tp")
    return ((gap & 1) * 4 + turn * 2 + (gap >> 1)) * rows + spot % rows


def dealt_order(lengths, dealing):
    numbers = jnp.arange(lengths.shape[0], dtype=jnp.int32)
    given_start = jnp.cumsum(lengths, dtype=jnp.int32) - lengths
    chosen = (dealing[:, None] == numbers[None, :]).astype(jnp.int32)
    dealt_len = jnp.sum(chosen * lengths[None, :], axis=1, dtype=jnp.int32)
    dealt_from = jnp.sum(chosen * given_start[None, :], axis=1, dtype=jnp.int32)
    dealt_start = jnp.cumsum(dealt_len, dtype=jnp.int32) - dealt_len
    return dealt_len, dealt_from, dealt_start


def look_up(spots, starts, counts, *tables):
    inside = (
        (spots[:, None] >= starts[None, :]) & (spots[:, None] < (starts + counts)[None, :])
    ).astype(jnp.int32)
    return [jnp.sum(inside * table[None, :], axis=1, dtype=jnp.int32) for table in tables]


def norm_back(grad_out, unit_rows, inverse, gain):
    scaled = grad_out * gain
    return inverse * (scaled - unit_rows * jnp.mean(scaled * unit_rows, axis=1, keepdims=True))


def inverse_norm(rows):
    return lax.rsqrt(jnp.mean(rows * rows, axis=1, keepdims=True) + EPSILON)


def padded(v, rows, cols):
    return jnp.pad(v, ((0, rows - v.shape[0]), (0, cols - v.shape[1])))


def per_device(
    tokens,
    cotangent,
    lengths,
    dealing,
    norm_in,
    w_query,
    w_keyval,
    w_attn_out,
    w_zx,
    w_bc,
    w_step,
    head_params,
    taps_x,
    taps_bc,
    gain_mamba,
    w_mamba_out,
    norm_mid,
    w_gate_up,
    w_down,
):
    tok_rows, model_width = tokens.shape
    tp_size = lax.axis_size("tp")
    fsdp_size = lax.axis_size("fsdp")
    rank_rows = tok_rows * tp_size
    tp_index = lax.axis_index("tp")
    fsdp_index = lax.axis_index("fsdp")
    ctx_index = lax.axis_index("ctx")
    shard = w_query.shape[0]
    heads = head_params.shape[1]
    scan_width = heads * HD
    query_width = w_query.shape[1]
    bc_width = w_bc.shape[1]
    ffn_width = w_gate_up.shape[2]
    own_start = tp_index * tok_rows
    peer_start = (tp_size - 1) * tok_rows - own_start

    dealt_len, dealt_from, dealt_start = dealt_order(lengths[0], dealing[0])
    numbers = jnp.arange(lengths.shape[1], dtype=jnp.int32)
    spots = ctx_index * rank_rows + jnp.arange(rank_rows, dtype=jnp.int32)
    segment, begins, anchor = look_up(
        spots, dealt_start, dealt_len, numbers, dealt_start, dealt_from
    )
    position = spots - begins
    sources = stack_spot(anchor + position, tok_rows)
    home = (ctx_index * tp_size + tp_index) * tok_rows + jnp.arange(tok_rows, dtype=jnp.int32)
    home_dealt, home_given = look_up(home, dealt_from, dealt_len, dealt_start, dealt_from)
    home_spots = stack_spot(home - home_given + home_dealt, tok_rows)
    segc, segr, posc = segment[:, None], segment[None, :], position[:, None]
    half_width = HD // 2
    freqs = ROPE_BASE ** (-jnp.arange(half_width, dtype=jnp.float32) / half_width)
    angles = position.astype(jnp.float32)[:, None] * freqs[None, :]
    cosine, sine = jnp.cos(angles), jnp.sin(angles)
    cos_table = jnp.concatenate([cosine] * 4, axis=1)
    sin_table = jnp.concatenate([-sine, sine, -sine, sine], axis=1)
    perm = lax.optimization_barrier(quarter_perm(model_width))

    small = (norm_in, norm_mid, taps_x, taps_bc, gain_mamba)
    small_sizes = [v.size for v in small]
    piece = shard // 4
    small = jnp.concatenate([v.reshape(-1) for v in small]).reshape(piece, -1)
    small_width = small.shape[1]
    free = LANES - heads - small_width
    wide = scan_width + 2 * LANES + LANES

    def in_quarter(gap):
        def rows_of(v):
            return lax.dynamic_slice_in_dim(v, (ctx_index ^ gap) * piece, piece, 0)

        zx = rows_of(w_zx)
        parts = [zx[:, 1, :], rows_of(w_bc), rows_of(w_step), small]
        parts += [jnp.zeros((piece, free), BF), zx[:, 0, :], rows_of(w_query)]
        return jnp.concatenate(parts + [rows_of(w_keyval).reshape(piece, -1)], axis=1)

    in_own, in_twin = in_quarter(0), in_quarter(2)
    token_near = direct_near(tokens)
    in_near = gather_near(in_own)
    in_far = gather_far(in_near)
    q_out = own_quarters(jnp.concatenate([w_attn_out, w_mamba_out], axis=0), True)
    q_back = own_quarters(w_down, True)
    q_late = [jnp.concatenate([q_out[i], q_back[i]], axis=1) for i in range(2)]
    late_near = gather_near(q_late[0])
    q_ffn = own_quarters(w_gate_up.reshape(shard, -1))
    places = (sources, home_spots, segc, segr, posc, cos_table, sin_table, perm)
    token_stack = token_near + [core_swap(v) for v in token_near]
    places, token_stack, cotangent, in_near, in_far, in_twin, late_near, q_ffn, late_twin = stage(
        places, token_stack, cotangent, in_near, in_far, in_twin, late_near, q_ffn, q_late[1]
    )
    sources, home_spots, segc, segr, posc, cos_table, sin_table, perm = places

    in_across = swap_line(in_near, in_far)
    ffn_near = gather_near(q_ffn[0])
    cot_pair = jnp.concatenate([cotangent, chip_swap(cotangent)], axis=0)
    late_far = gather_far(late_near)
    small_cols = slice(wide - LANES + heads, wide - free)
    small = jnp.concatenate([in_near[:, small_cols], in_far[:, small_cols]], axis=0)
    small = order_shards(small.reshape(fsdp_size, -1))
    ends = [sum(small_sizes[: i + 1]) for i in range(len(small_sizes))]
    smalls = [small[:, end - size : end] for end, size in zip(ends, small_sizes)]
    gains = jnp.stack([smalls[0].reshape(-1), smalls[1].reshape(-1)], axis=0).astype(BF)
    gains = dot_nn(gains, perm)
    gain_in, gain_mid = gains[0:1], gains[1:2]
    taps_one = smalls[2].reshape((fsdp_size,) + taps_x.shape).transpose(1, 2, 0, 3)
    taps_one = padded(taps_one.reshape(taps_x.shape[0], -1), 8, scan_width)
    taps_two = smalls[3].reshape((fsdp_size,) + taps_bc.shape).transpose(1, 0, 2)
    taps_two = padded(taps_two.reshape(taps_bc.shape[0], -1), 8, bc_width)
    gain_flat = smalls[4].reshape((fsdp_size,) + gain_mamba.shape).transpose(1, 0, 2)
    gain_flat = gain_flat.reshape(1, -1)
    heads_pad = padded(head_params, 8, LANES)
    skip = jnp.repeat(head_params[2], HD)[None, :]

    scan_args = (taps_one, taps_two, heads_pad, skip, segc, segr, posc)
    x_low, normed_in, inverse_in = pick_normed(sources, perm, gain_in, token_stack)
    in_across, normed_in, gain_mid, gain_flat, scan_args, late_far, cot_pair, ffn_near = stage(
        in_across, normed_in, gain_mid, gain_flat, scan_args, late_far, cot_pair, ffn_near
    )

    cot_near = [cot_pair, pair_swap(cot_pair)]
    in_half = join_half(in_near, in_far, in_twin, in_across)
    in_other = core_swap(in_half)
    late_across = swap_line(late_near, late_far)
    ffn_far = gather_far(ffn_near)
    y_scan, y_gate = project(normed_in, in_half, in_other, wide)
    scan_out, states = scan_fwd(y_scan, scan_width, *scan_args)
    attn_args = (query_width, scan_width, cos_table, sin_table, segc, segr)
    attn_rows = attention_fwd(y_gate, *attn_args)
    scan_out, attn_rows, late_across, ffn_far, cot_near = stage(
        scan_out, attn_rows, late_across, ffn_far, cot_near
    )

    ffn_operand = join_tail(ffn_near, ffn_far, 2 * ffn_near.shape[0] // fsdp_size)
    ffn_across = chip_swap(ffn_operand)
    late_half = join_half(late_near, late_far, late_twin, after(late_across, ffn_operand))
    late_rest = core_swap(late_half)
    out_width = query_width + scan_width
    gate_in = y_gate[:, :scan_width]
    sigma_in = jax.nn.sigmoid(gate_in)
    gated = scan_out * gate_in * sigma_in
    square_sum = jnp.sum(gated * gated, axis=1)
    square_sum = (square_sum + pair_swap(square_sum))[:, None]
    channels = scan_width * tp_size
    inverse_gate = lax.rsqrt(square_sum / channels + EPSILON)
    unit_gate = gated * inverse_gate
    mamba_rows = (unit_gate * gain_flat).astype(BF)
    branch_rows = jnp.concatenate([attn_rows, mamba_rows], axis=1)
    mixer = unproject([branch_rows], [(late_half, late_rest, 0)])
    mixer_half, mixer_rest = (pair_swap(v) for v in halves(mixer))
    ffn_half = join_half(ffn_near, ffn_far, q_ffn[1], after(ffn_across, mixer_half))
    ffn_other = core_swap(ffn_half)
    cot_stack = cot_near + [core_swap(v) for v in cot_near]
    cot_rows = pick_turned(sources, perm, after(cot_stack, mixer))
    mixer, mixer_half, mixer_rest, ffn_other, cot_rows = stage(
        mixer, mixer_half, mixer_rest, ffn_other, cot_rows
    )
    mixer_peer = jnp.concatenate([mixer_half, mixer_rest], axis=0)
    hidden = x_low.astype(F32) + (mixer.astype(F32) + mixer_peer.astype(F32))

    inverse_mid = inverse_norm(hidden)
    unit_mid = hidden * inverse_mid
    normed_mid = (unit_mid * gain_mid).astype(BF)
    activated, d_gate_up, d_mid = ffn_both_ways(
        normed_mid, cot_rows, ffn_half, ffn_other, late_half, late_rest, ffn_width, 1
    )

    d_mid_peer = pair_swap(d_mid)
    late_pairs = [(normed_mid, d_gate_up), (cot_rows, activated)]
    late_other = core_swap(grad_product(late_pairs, 1))
    late_grad = grad_product(late_pairs, 0)
    quarter_rows = fsdp_size * piece
    far_sum = add_low(late_grad[quarter_rows:], late_other[quarter_rows:])
    far_recv = chip_swap(far_sum)
    ffn_part = unproject([after(activated, d_mid_peer)], [(late_half, late_rest, 1)])
    d_mid, d_mid_peer, late_grad, late_other, far_sum, ffn_part = stage(
        d_mid, d_mid_peer, late_grad, late_other, far_sum, ffn_part
    )
    near_sum = add_low(late_grad[:quarter_rows], late_other[:quarter_rows])
    d_mid = d_mid.astype(F32) + d_mid_peer.astype(F32)

    ffn_own = lax.dynamic_slice_in_dim(ffn_part, own_start, tok_rows, 0).astype(F32)
    ffn_peer = pair_swap(lax.dynamic_slice_in_dim(ffn_part, peer_start, tok_rows, 0))
    d_hidden = cot_rows.astype(F32) + norm_back(d_mid, unit_mid, inverse_mid, gain_mid)
    g_norm_mid = jnp.sum(d_mid * unit_mid, axis=0, keepdims=True)
    d_mix = d_hidden.astype(BF)
    d_branch = turn_back(d_mix, late_half, late_rest, out_width)
    d_attn = d_branch[:, :query_width]
    d_mamba = d_branch[:, query_width:].astype(F32)
    scaled_gate = d_mamba * gain_flat
    gate_stat = jnp.sum(scaled_gate * unit_gate, axis=1)
    gate_stat = (gate_stat + pair_swap(gate_stat))[:, None]
    d_query = attention_bwd(y_gate, *attn_args, d_attn)
    g_gain = jnp.sum(d_mamba * unit_gate, axis=0, keepdims=True)
    gate_stat, d_query, far_recv = stage(gate_stat, d_query, far_recv)
    d_gated = inverse_gate * (scaled_gate - unit_gate * (gate_stat / channels))
    d_scan = d_gated * gate_in * sigma_in
    d_z = d_gated * scan_out * sigma_in * (1.0 + gate_in * (1.0 - sigma_in))
    dy_gate = jnp.concatenate([d_z.astype(BF), d_query], axis=1)
    out_pairs = [(d_mix, branch_rows), (normed_in, dy_gate)]
    out_other = core_swap(grad_product(out_pairs, 1))
    out_keep, out_far = halves(add_low(grad_product(out_pairs, 0), out_other))
    late_sum, late_send = halves(add_low(near_sum, far_recv))
    d_scan, late_sum, late_send, out_keep, out_far = stage(
        d_scan, late_sum, late_send, out_keep, out_far
    )
    out_far = chip_swap(out_far)
    late_recv = shard_swap(late_send, fsdp_size // 2)
    dy_scan, g_taps_one, g_taps_two, g_heads = scan_bwd(
        y_scan, scan_width, *scan_args, states, d_scan
    )
    hidden_own = lax.dynamic_slice_in_dim(hidden, own_start, tok_rows, 0)
    out_own = (hidden_own + ffn_own + after(ffn_peer, dy_scan).astype(F32)).astype(BF)
    out_own = dot_nt(out_own, perm).astype(BF)
    bc_cols = slice(scan_width, scan_width + bc_width)
    d_bc_peer = pair_swap(dy_scan[:, bc_cols])
    dy_scan, dy_gate, d_bc_peer, out_far, out_keep, out_own, late_recv = stage(
        dy_scan, dy_gate, d_bc_peer, out_far, out_keep, out_own, late_recv
    )

    out_keep, out_far = halves(add_low(out_keep, out_far))
    dy_gate, out_keep, out_far = stage(dy_gate, out_keep, out_far)
    out_far = shard_swap(out_far, fsdp_size // 2)
    d_in = unproject([dy_scan, dy_gate], [(in_half, in_other, 0), (in_half, in_other, 1)])
    d_in_peer = pair_swap(lax.dynamic_slice_in_dim(d_in, peer_start, tok_rows, 0))
    d_bc = add_low(dy_scan[:, bc_cols], d_bc_peer)
    dy_full = jnp.concatenate(
        [dy_scan[:, :scan_width], d_bc, dy_scan[:, scan_width + bc_width :]], axis=1
    )
    out_across = chip_swap(out_own)
    out_pair = jnp.concatenate([out_own, out_across], axis=0)
    late_keep, late_send = halves(add_low(late_sum, late_recv))
    late_recv = shard_swap(late_send, fsdp_size // 4)
    in_pairs = [(normed_in, after(dy_full, d_in_peer, out_far, late_recv, out_across))]
    in_other = core_swap(grad_product(in_pairs, 1))
    in_keep, in_far = halves(add_low(grad_product(in_pairs, 0), in_other))
    in_keep, in_far, d_in, d_in_peer, out_keep, out_far, out_pair, late_keep, late_recv = stage(
        in_keep, in_far, d_in, d_in_peer, out_keep, out_far, out_pair, late_keep, late_recv
    )

    def own_rows(v):
        return lax.dynamic_slice_in_dim(v, own_start, tok_rows, 0)

    d_in_own = own_rows(d_in).astype(F32) + d_in_peer.astype(F32)
    unit_own = own_rows(x_low).astype(F32) * own_rows(inverse_in)
    grad_own = own_rows(d_hidden) + norm_back(d_in_own, unit_own, own_rows(inverse_in), gain_in)
    g_norm_in = jnp.sum(d_in_own * unit_own, axis=0, keepdims=True)
    grad_own = dot_nt(grad_own.astype(BF), perm).astype(BF)
    in_recv = chip_swap(in_far)
    out_near = [out_pair, pair_swap(out_pair)]
    grad_pair = jnp.concatenate([grad_own, chip_swap(grad_own)], axis=0)
    def shards_sum(keep, far, gap):
        total = add_low(keep, far)
        while gap > 1:
            gap //= 2
            keep, far = halves(total)
            total = add_low(keep, shard_swap(far, gap))
        return total

    late_sum = shards_sum(late_keep, late_recv, fsdp_size // 4)
    out_sum = shards_sum(out_keep, out_far, fsdp_size // 2)
    grad_pair, in_keep, in_recv, late_sum, out_sum, out_near, g_norm_in = stage(
        grad_pair, in_keep, in_recv, late_sum, out_sum, out_near, g_norm_in
    )

    in_keep, in_far = halves(add_low(in_keep, in_recv))
    in_recv = shard_swap(in_far, fsdp_size // 2)
    grad_near = [grad_pair, pair_swap(grad_pair)]
    out_twin, late_twin = chip_swap(out_sum), chip_swap(late_sum)
    mixed_home = pick_rows(home_spots, out_near + [core_swap(v) for v in out_near])
    in_keep, in_recv, out_twin, late_twin, mixed_home = stage(
        in_keep, in_recv, out_twin, late_twin, mixed_home
    )

    out_sums = jnp.concatenate([out_sum, out_twin], axis=0)
    late_sums = jnp.concatenate([late_sum, late_twin], axis=0)
    in_sum = shards_sum(in_keep, in_recv, fsdp_size // 2)
    out_others, late_others = core_swap(out_sums), core_swap(late_sums)
    g_norms = dot_nt(
        jnp.concatenate([g_norm_in, g_norm_mid], axis=0), perm.astype(F32), PRECISE
    )
    g_norms, g_taps_two = g_norms.reshape(-1), g_taps_two[: taps_bc.shape[0]].reshape(-1)
    g_taps_one = g_taps_one[: taps_x.shape[0]].reshape(-1)
    g_heads = g_heads[:3, :heads].reshape(-1)
    g_gain = g_gain.reshape(-1)
    parts = (g_norms[:model_width], g_taps_two, g_norms[model_width:], g_taps_one, g_heads, g_gain)
    paired = model_width + g_taps_two.shape[0]
    sums = jnp.concatenate(parts)
    sums = after(sums, in_recv)
    sums = sums + core_swap(sums)
    sums = sums + chip_swap(sums)
    in_sum, out_others, late_others, sums, grad_near = stage(
        in_sum, out_others, late_others, sums, grad_near
    )

    in_twin = chip_swap(in_sum)
    grad_near += [core_swap(v) for v in grad_near]
    grad_attn_out, grad_mamba_out, grad_z, grad_query, grad_keyval = finish_out(
        ctx_index, out_sums, out_others, query_width, scan_width
    )
    sums = sums + shard_swap(sums, 1)
    in_twin, grad_near, grad_z, sums = stage(in_twin, grad_near, grad_z, sums)
    in_sums = jnp.concatenate([in_sum, in_twin], axis=0)
    grad_home = pick_rows(home_spots, grad_near)
    grad_gate_up, grad_down = finish_late(ctx_index, late_sums, late_others, ffn_width)
    gap = 2
    while gap < fsdp_size:
        sums = sums + shard_swap(sums, gap)
        gap *= 2
    sums = jnp.concatenate([sums[:paired] + pair_swap(sums[:paired]), sums[paired:]])
    grad_zx, grad_bc, grad_step = finish_scan(
        ctx_index, in_sums, core_swap(in_sums), grad_z, bc_width
    )
    ends = [sum(v.size for v in parts[: i + 1]) for i in range(len(parts))]
    sum_in, sum_two, sum_mid, sum_one, sum_heads, sum_gain = [
        sums[end - v.size : end] for end, v in zip(ends, parts)
    ]

    def shard_of(array, dim_index):
        piece = array.shape[dim_index] // fsdp_size
        return lax.dynamic_slice_in_dim(array, fsdp_index * piece, piece, dim_index)

    return (
        mixed_home,
        grad_home,
        shard_of(sum_in, 0),
        grad_query,
        grad_keyval.reshape(w_keyval.shape),
        grad_attn_out,
        grad_zx,
        grad_bc,
        grad_step[:, : w_step.shape[1]],
        sum_heads.reshape(head_params.shape),
        shard_of(sum_one.reshape(taps_x.shape[0], heads, HD), 2),
        shard_of(sum_two.reshape(taps_bc.shape[0], -1), 1),
        shard_of(sum_gain.reshape(heads, HD), 1),
        grad_mamba_out,
        shard_of(sum_mid, 0),
        grad_gate_up,
        grad_down,
    )


def solution(mesh):
    rows = P(("fsdp", "ctx", "tp"), None)
    in_specs = (
        rows,
        rows,
        P("fsdp", None),
        P("fsdp", None),
        P("fsdp"),
        P("fsdp", "tp"),
        P("fsdp", "tp", None),
        P("tp", "fsdp"),
        P("fsdp", None, "tp"),
        P("fsdp", None),
        P("fsdp", "tp"),
        P(None, "tp"),
        P(None, "tp", "fsdp"),
        P(None, "fsdp"),
        P("tp", "fsdp"),
        P("tp", "fsdp"),
        P("fsdp"),
        P("fsdp", None, "tp"),
        P("tp", "fsdp"),
    )
    out_specs = (
        rows,
        rows,
        P("fsdp"),
        P("fsdp", "tp"),
        P("fsdp", "tp", None),
        P("tp", "fsdp"),
        P("fsdp", None, "tp"),
        P("fsdp", None),
        P("fsdp", "tp"),
        P(None, "tp"),
        P(None, "tp", "fsdp"),
        P(None, "fsdp"),
        P("tp", "fsdp"),
        P("tp", "fsdp"),
        P("fsdp"),
        P("fsdp", None, "tp"),
        P("tp", "fsdp"),
    )
    return jax.shard_map(
        per_device, mesh=mesh, in_specs=in_specs, out_specs=out_specs, check_vma=False
    )
```

```python
import functools
import jax
import jax.numpy as jnp
from jax import lax
from jax.experimental import pallas as pl
from jax.experimental.pallas import tpu as pltpu
from jax.sharding import PartitionSpec as P

HD = 64
BLK = 128
LANES = 128
EPSILON = 1e-05
ROPE_BASE = 100000000000.0
PRECISE = lax.Precision.HIGHEST
F32 = jnp.float32
BF = jnp.bfloat16
FAR = -1e30


def dot_nn(a, b, precision=None):
    return lax.dot_general(
        a, b, (((1,), (0,)), ((), ())), precision=precision, preferred_element_type=F32
    )


def dot_nt(a, b, precision=None):
    return lax.dot_general(
        a, b, (((1,), (1,)), ((), ())), precision=precision, preferred_element_type=F32
    )


def dot_tn(a, b, precision=None):
    return lax.dot_general(
        a, b, (((0,), (0,)), ((), ())), precision=precision, preferred_element_type=F32
    )


def iota(shape, dim):
    return lax.broadcasted_iota(jnp.int32, shape, dim)


def two_terms(v):
    high = v.astype(BF)
    return high, (v - high.astype(F32)).astype(BF)


def spread_heads(v, spread):
    return dot_nn(jnp.concatenate(two_terms(v), axis=1), spread)


def sum_heads(v, spread):
    rows = v.shape[0]
    both = dot_nt(jnp.concatenate(two_terms(v), axis=0), spread[:LANES])
    return both[:rows] + both[rows:]


def swap_halves(v):
    lanes = v.shape[1]
    low = (iota(v.shape, 1) & (HD - 1)) < HD // 2
    return jnp.where(low, pltpu.roll(v, lanes - HD // 2, 1), pltpu.roll(v, HD // 2, 1))


def split_pair(v):
    first = iota(v.shape, 1) < HD
    zero = jnp.zeros_like(v)
    return jnp.concatenate([jnp.where(first, v, zero), jnp.where(first, zero, v)], axis=0)


def keys_values(kv, cos, sin):
    first = iota(kv.shape, 1) < HD
    roped = kv * cos + swap_halves(kv) * sin
    keys = jnp.where(first, roped, 0.0)
    values = jnp.where(first, 0.0, kv)
    key_pair = (keys.astype(BF), pltpu.roll(keys, HD, 1).astype(BF))
    value_pair = (pltpu.roll(values, HD, 1).astype(BF), values.astype(BF))
    return key_pair, value_pair


def attention_probs(query, key, allowed):
    scores = dot_nt(query, key) * HD ** (-0.5)
    scores = jnp.where(allowed, scores, FAR)
    weights = jnp.exp(scores - jnp.max(scores, axis=1, keepdims=True))
    return weights / jnp.sum(weights, axis=1, keepdims=True)


def allowed_rows(segc, segr, lower, count):
    keys = lower + count
    same = segc[lower:keys, :] == segr[:, :keys]
    return same & (iota((count, keys), 0) + lower >= iota((count, keys), 1))


def attention_fwd_kernel(q_ref, kv_ref, cos_ref, sin_ref, segc_ref, segr_ref, out_ref):
    rows, width = q_ref.shape
    cos, sin = cos_ref[...], sin_ref[...]
    key_pair, value_pair = keys_values(kv_ref[...], cos, sin)
    segc, segr = segc_ref[...], segr_ref[...]
    for pair in range(width // LANES):
        cols = slice(pair * LANES, (pair + 1) * LANES)
        raw = q_ref[:, cols]
        query = (raw * cos + swap_halves(raw) * sin).astype(BF)
        for lower in range(0, rows, BLK):
            keys = lower + BLK
            allowed = allowed_rows(segc, segr, lower, BLK)
            total = None
            for side in range(2):
                probs = attention_probs(query[lower:keys], key_pair[side][:keys], allowed)
                part = dot_nn(probs.astype(BF), value_pair[side][:keys])
                total = part if total is None else total + part
            out_ref[lower:keys, cols] = total.astype(BF)


def attention_bwd_kernel(
    q_ref, kv_ref, cos_ref, sin_ref, segc_ref, segr_ref, do_ref, out_ref, dk_ref, dv_ref
):
    rows, width = q_ref.shape
    cos, sin = cos_ref[...], sin_ref[...]
    key_pair, value_pair = keys_values(kv_ref[...], cos, sin)
    segc, segr = segc_ref[...], segr_ref[...]
    dk_ref[...] = jnp.zeros_like(dk_ref)
    dv_ref[...] = jnp.zeros_like(dv_ref)
    for pair in range(width // LANES):
        cols = slice(pair * LANES, (pair + 1) * LANES)
        raw = q_ref[:, cols]
        query = (raw * cos + swap_halves(raw) * sin).astype(BF)
        for lower in range(0, rows, BLK):
            keys = lower + BLK
            allowed = allowed_rows(segc, segr, lower, BLK)
            query_part = query[lower:keys]
            grad = do_ref[lower:keys, cols]
            d_query = None
            probs_all, scores_all = [], []
            for side in range(2):
                probs = attention_probs(query_part, key_pair[side][:keys], allowed)
                d_probs = dot_nt(grad, value_pair[side][:keys])
                inner = jnp.sum(d_probs * probs, axis=1, keepdims=True)
                d_scores = (probs * (d_probs - inner)).astype(BF)
                part = dot_nn(d_scores, key_pair[side][:keys])
                d_query = part if d_query is None else d_query + part
                probs_all.append(probs.astype(BF))
                scores_all.append(d_scores)
            dv_ref[:keys, :] += dot_tn(jnp.concatenate(probs_all, axis=0), split_pair(grad))
            dk_ref[:keys, :] += dot_tn(jnp.concatenate(scores_all, axis=0), split_pair(query_part))
            d_query = d_query * HD ** (-0.5)
            cos_part, sin_part = cos[lower:keys], sin[lower:keys]
            out_ref[lower:keys, cols] = (
                d_query * cos_part - swap_halves(d_query) * sin_part
            ).astype(BF)
    first = iota(dk_ref.shape, 1) < HD
    d_key = dk_ref[...]
    d_key = (d_key + pltpu.roll(d_key, HD, 1)) * HD ** (-0.5)
    d_key = d_key * cos - swap_halves(d_key) * sin
    d_value = dv_ref[...]
    d_value = d_value + pltpu.roll(d_value, HD, 1)
    out_ref[:, width:] = jnp.where(first, d_key, d_value).astype(BF)


def conv_rows(signal, taps_ref, position):
    total = taps_ref[4:5, :] + taps_ref[3:4, :] * signal
    for lag in range(1, 4):
        moved = jnp.where(position >= lag, pltpu.roll(signal, lag, 0), 0.0)
        total = total + taps_ref[3 - lag : 4 - lag, :] * moved
    return total


def conv_back(signal, d_pre, taps_ref, grad_ref, position):
    rows = signal.shape[0]
    grad_ref[...] = jnp.zeros_like(grad_ref)
    grad_ref[4:5, :] = jnp.sum(d_pre, axis=0, keepdims=True)
    grad_ref[3:4, :] = jnp.sum(d_pre * signal, axis=0, keepdims=True)
    total = taps_ref[3:4, :] * d_pre
    for lag in range(1, 4):
        kept = jnp.where(position >= lag, d_pre, 0.0)
        grad_ref[3 - lag : 4 - lag, :] = jnp.sum(
            kept * pltpu.roll(signal, lag, 0), axis=0, keepdims=True
        )
        total = total + taps_ref[3 - lag : 4 - lag, :] * pltpu.roll(kept, rows - lag, 0)
    return total


def softplus(v):
    return jnp.maximum(v, 0.0) + jnp.log1p(jnp.exp(-jnp.abs(v)))


def spread_matrix(width):
    shape = (2 * LANES, width)
    return ((iota(shape, 0) & (LANES - 1)) == (iota(shape, 1) >> 6)).astype(F32).astype(BF)


def scan_setup(step_ref, heads_ref):
    steps = softplus(step_ref[...] + heads_ref[0:1, :])
    rates = -jnp.exp(heads_ref[1:2, :])
    return steps, rates


def block_decays(steps, rates, segc, lower):
    upper = lower + BLK
    shape = (BLK, BLK)
    lower_ones = (iota(shape, 0) >= iota(shape, 1)).astype(F32)
    low_ones = lower_ones.astype(BF)
    decays = dot_nn(
        jnp.concatenate([low_ones, low_ones], axis=1),
        jnp.concatenate(two_terms(steps[lower:upper] * rates), axis=0),
    )
    seg_part = segc[lower:upper]
    if lower == 0:
        arrive = None
    else:
        carried = seg_part == segc[lower - 1 : lower]
        arrive = jnp.where(carried, jnp.exp(decays), 0.0)
    kept = seg_part == segc[upper - 1 : upper]
    leave = jnp.where(kept, jnp.exp(decays[BLK - 1 : BLK] - decays), 0.0)
    return decays, arrive, leave, lower_ones


def block_mixing(decays, decays_t, head, allowed):
    gap = decays[:, head : head + 1] - decays_t[head : head + 1, :]
    return jnp.exp(jnp.where(allowed, gap, FAR))


def scan_fwd_kernel(
    x_ref, bc_ref, step_ref, tapx_ref, tapbc_ref, heads_ref, skip_ref, segc_ref, segr_ref,
    pos_ref, out_ref, states_ref,
):
    rows, width = x_ref.shape
    position = pos_ref[...]
    segc, segr = segc_ref[...], segr_ref[...]
    conv_x = jax.nn.silu(conv_rows(x_ref[...], tapx_ref, position)).astype(BF)
    conv_bc = jax.nn.silu(conv_rows(bc_ref[...], tapbc_ref, position)).astype(BF)
    steps, rates = scan_setup(step_ref, heads_ref)
    spread = spread_matrix(width)
    scaled = conv_x.astype(F32) * spread_heads(steps, spread)
    state = None
    for lower in range(0, rows, BLK):
        upper = lower + BLK
        b_part = conv_bc[lower:upper, :LANES]
        c_part = conv_bc[lower:upper, LANES:]
        decays, arrive, leave, lower_ones = block_decays(steps, rates, segc, lower)
        decays_t = decays.T
        allowed = (segc[lower:upper] == segr[:, lower:upper]) & (lower_ones > 0.0)
        inner = dot_nt(c_part, b_part)
        scaled_part = scaled[lower:upper]
        scaled_low = scaled_part.astype(BF)
        fresh = dot_tn(b_part, (scaled_part * spread_heads(leave, spread)).astype(BF))
        if state is None:
            recall = None
            states_ref[lower // BLK] = jnp.zeros(fresh.shape, BF)
            state = fresh
        else:
            arrive_wide = spread_heads(arrive, spread)
            recall = dot_nn(c_part, state.astype(BF)) * arrive_wide
            states_ref[lower // BLK] = state.astype(BF)
            state = state * arrive_wide[BLK - 1 : BLK] + fresh
        for pair in range(width // LANES):
            cols = slice(pair * LANES, (pair + 1) * LANES)
            mixes = [
                (block_mixing(decays, decays_t, 2 * pair + side, allowed) * inner).astype(BF)
                for side in range(2)
            ]
            local = dot_nn(jnp.concatenate(mixes, axis=1), split_pair(scaled_low[:, cols]))
            if recall is not None:
                local = local + recall[:, cols]
            out_ref[lower:upper, cols] = local + skip_ref[0:1, cols] * conv_x[
                lower:upper, cols
            ].astype(F32)


def scan_bwd_kernel(
    x_ref, bc_ref, step_ref, tapx_ref, tapbc_ref, heads_ref, skip_ref, segc_ref, segr_ref,
    pos_ref, states_ref, dy_ref, out_ref, gtapx_ref, gtapbc_ref, gheads_ref, dx_ref, dbc_ref,
):
    rows, width = x_ref.shape
    position = pos_ref[...]
    segc, segr = segc_ref[...], segr_ref[...]
    pre_x = conv_rows(x_ref[...], tapx_ref, position)
    pre_bc = conv_rows(bc_ref[...], tapbc_ref, position)
    conv_x = jax.nn.silu(pre_x).astype(BF)
    conv_bc = jax.nn.silu(pre_bc).astype(BF)
    steps, rates = scan_setup(step_ref, heads_ref)
    spread = spread_matrix(width)
    steps_wide = spread_heads(steps, spread)
    lane = iota((BLK, LANES), 1)
    sub = iota((LANES, BLK), 0)
    last_row = iota((BLK, LANES), 0) == BLK - 1
    d_state = None
    g_bias = jnp.zeros((1, LANES), F32)
    g_rate = jnp.zeros((1, LANES), F32)
    g_skip = jnp.zeros((1, width), F32)
    for lower in range(rows - BLK, -1, -BLK):
        upper = lower + BLK
        b_part = conv_bc[lower:upper, :LANES]
        c_part = conv_bc[lower:upper, LANES:]
        decays, arrive, leave, lower_ones = block_decays(steps, rates, segc, lower)
        decays_t = decays.T
        allowed = (segc[lower:upper] == segr[:, lower:upper]) & (lower_ones > 0.0)
        inner = dot_nt(c_part, b_part)
        x_part = conv_x[lower:upper].astype(F32)
        scaled_part = x_part * steps_wide[lower:upper]
        scaled_low = scaled_part.astype(BF)
        grad = dy_ref[lower:upper, :]
        grad_low = grad.astype(BF)
        d_scaled = []
        d_inner = jnp.zeros((BLK, BLK), F32)
        row_sums = jnp.zeros((BLK, LANES), F32)
        col_sums = jnp.zeros((LANES, BLK), F32)
        for pair in range(width // LANES):
            cols = slice(pair * LANES, (pair + 1) * LANES)
            grad_pair = split_pair(grad_low[:, cols])
            d_mix = dot_nt(grad_pair, scaled_low[:, cols])
            mixes = []
            for side in range(2):
                head = 2 * pair + side
                mixing = block_mixing(decays, decays_t, head, allowed)
                mix = mixing * inner
                d_part = d_mix[side * BLK : (side + 1) * BLK]
                d_inner = d_inner + d_part * mixing
                both = d_part * mix
                row_sums = jnp.where(lane == head, jnp.sum(both, axis=1, keepdims=True), row_sums)
                col_sums = jnp.where(sub == head, jnp.sum(both, axis=0, keepdims=True), col_sums)
                mixes.append(mix.astype(BF))
            d_scaled.append(dot_tn(jnp.concatenate(mixes, axis=0), grad_pair))
        d_scaled = jnp.concatenate(d_scaled, axis=1)
        d_decays = row_sums - col_sums.T
        d_inner = d_inner.astype(BF)
        d_c = dot_nn(d_inner, b_part)
        d_b = dot_tn(d_inner, c_part)
        if lower > 0:
            arrive_wide = spread_heads(arrive, spread)
            state_low = states_ref[lower // BLK]
            recall = dot_nn(c_part, state_low) * arrive_wide
            d_decays = d_decays + sum_heads(recall * grad, spread)
            grad_in = (grad * arrive_wide).astype(BF)
            d_c = d_c + dot_nt(grad_in, state_low)
        if d_state is not None:
            state_grad = d_state.astype(BF)
            leave_wide = spread_heads(leave, spread)
            d_kept = dot_nn(b_part, state_grad) * leave_wide
            d_b = d_b + dot_nt((scaled_part * leave_wide).astype(BF), state_grad)
            d_leave = sum_heads(d_kept * scaled_part, spread)
            d_last = jnp.sum(d_leave, axis=0, keepdims=True)
            if lower > 0:
                lingering = jnp.sum(d_state * state_low.astype(F32), axis=0, keepdims=True)
                lingering = lingering * arrive_wide[BLK - 1 : BLK]
                d_last = d_last + sum_heads(jnp.broadcast_to(lingering, (16, width)), spread)[0:1]
            d_decays = d_decays - d_leave + jnp.where(last_row, d_last, 0.0)
            d_scaled = d_scaled + d_kept
        if lower > 0:
            d_new = dot_tn(c_part, grad_in)
            if d_state is None:
                d_state = d_new
            else:
                d_state = d_state * arrive_wide[BLK - 1 : BLK] + d_new
        low_ones = lower_ones.astype(BF)
        d_log = dot_tn(
            jnp.concatenate([low_ones, low_ones], axis=0),
            jnp.concatenate(two_terms(d_decays), axis=0),
        )
        steps_part = steps[lower:upper]
        d_steps = sum_heads(d_scaled * x_part, spread) + d_log * rates
        d_step_in = d_steps * jax.nn.sigmoid(step_ref[lower:upper, :] + heads_ref[0:1, :])
        g_bias = g_bias + jnp.sum(d_step_in, axis=0, keepdims=True)
        g_rate = g_rate + jnp.sum(d_log * steps_part, axis=0, keepdims=True) * rates
        g_skip = g_skip + jnp.sum(grad * x_part, axis=0, keepdims=True)
        out_ref[lower:upper, width + 2 * LANES :] = d_step_in.astype(BF)
        dx_ref[lower:upper, :] = d_scaled * steps_wide[lower:upper] + grad * skip_ref[0:1, :]
        dbc_ref[lower:upper, :LANES] = d_b
        dbc_ref[lower:upper, LANES:] = d_c
    gheads_ref[...] = jnp.zeros_like(gheads_ref)
    gheads_ref[0:1, :] = g_bias
    gheads_ref[1:2, :] = g_rate
    gheads_ref[2:3, :] = sum_heads(jnp.broadcast_to(g_skip, (16, width)), spread)[0:1]
    gate = jax.nn.sigmoid(pre_x)
    d_pre = dx_ref[...] * gate * (1.0 + pre_x * (1.0 - gate))
    out_ref[:, :width] = conv_back(x_ref[...], d_pre, tapx_ref, gtapx_ref, position).astype(BF)
    gate = jax.nn.sigmoid(pre_bc)
    d_pre = dbc_ref[...] * gate * (1.0 + pre_bc * (1.0 - gate))
    out_ref[:, width : width + 2 * LANES] = conv_back(
        bc_ref[...], d_pre, tapbc_ref, gtapbc_ref, position
    ).astype(BF)


def select_parts(spot_ref, part_refs):
    spots = spot_ref[...]
    total, first = None, 0
    for part_ref in part_refs:
        shape = (spots.shape[0], part_ref.shape[0])
        chosen = (spots == iota(shape, 1) + first).astype(F32).astype(BF)
        product = dot_nn(chosen, part_ref[...])
        total = product if total is None else total + product
        first += part_ref.shape[0]
    return total


def pick_kernel(spot_ref, *refs):
    refs[-1][...] = select_parts(spot_ref, refs[:-1]).astype(BF)


def pick_turn_kernel(spot_ref, perm_ref, *refs):
    rows = select_parts(spot_ref, refs[:-1]).astype(BF)
    refs[-1][...] = dot_nn(rows, perm_ref[...]).astype(BF)


def pick_norm_kernel(spot_ref, perm_ref, gain_ref, *refs):
    rows_ref, normed_ref, inverse_ref = refs[-3:]
    rows = select_parts(spot_ref, refs[:-3]).astype(BF)
    rows = dot_nn(rows, perm_ref[...])
    inverse = lax.rsqrt(jnp.mean(rows * rows, axis=1, keepdims=True) + EPSILON)
    rows_ref[...] = rows.astype(BF)
    normed_ref[...] = (rows * inverse * gain_ref[...]).astype(BF)
    inverse_ref[...] = inverse


def join_kernel(*refs):
    start = 0
    for ref in refs[:-1]:
        refs[-1][start : start + ref.shape[0], :] = ref[...]
        start += ref.shape[0]


def join_tail_kernel(piece, near_ref, far_ref, out_ref):
    start = near_ref.shape[0] - piece
    out_ref[:start, :] = near_ref[piece:, :]
    out_ref[start:, :] = far_ref[...]


def grad_kernel(*refs):
    first = 0
    for left_ref, right_ref in zip(refs[:-1:2], refs[1:-1:2]):
        width = right_ref.shape[1]
        refs[-1][:, first : first + width] = dot_tn(left_ref[...], right_ref[...]).astype(BF)
        first += width


def ordered_rows(index_ref, own_ref, other_ref):
    index = index_ref[0]
    core_bit, chip_bit = (index & 1) == 1, (index & 2) == 2
    piece = own_ref.shape[0] // 2
    own, other = own_ref[...].astype(F32), other_ref[...].astype(F32)
    by_gap = (own[:piece], other[:piece], own[piece:], other[piece:])
    rows = []
    for quarter in range(4):
        near = jnp.where(core_bit, by_gap[quarter ^ 1], by_gap[quarter])
        far = jnp.where(core_bit, by_gap[quarter ^ 3], by_gap[quarter ^ 2])
        rows.append(jnp.where(chip_bit, far, near))
    return jnp.concatenate(rows, axis=0)


def finish_late_kernel(index_ref, own_ref, other_ref, up_ref, down_ref):
    rows = ordered_rows(index_ref, own_ref, other_ref)
    width = up_ref.shape[2]
    up_ref[:, 0, :] = rows[:, :width]
    up_ref[:, 1, :] = rows[:, width : 2 * width]
    down_ref[...] = rows[:, 2 * width :].T


def finish_out_kernel(
    index_ref, own_ref, other_ref, attn_ref, mamba_ref, z_ref, query_ref, keyval_ref
):
    rows = ordered_rows(index_ref, own_ref, other_ref)
    first = 0
    for ref in (attn_ref, mamba_ref):
        ref[...] = rows[:, first : first + ref.shape[0]].T
        first += ref.shape[0]
    for ref in (z_ref, query_ref, keyval_ref):
        ref[...] = rows[:, first : first + ref.shape[1]]
        first += ref.shape[1]


def finish_scan_kernel(index_ref, own_ref, other_ref, z_ref, zx_ref, bc_ref, step_ref):
    rows = ordered_rows(index_ref, own_ref, other_ref)
    width = z_ref.shape[1]
    zx_ref[:, 0, :] = z_ref[...]
    zx_ref[:, 1, :] = rows[:, :width]
    bc_ref[...] = rows[:, width : width + bc_ref.shape[1]]
    step_ref[...] = rows[:, width + bc_ref.shape[1] :]


def ffn_kernel(
    normed_ref, cot_ref, near_ref, far_ref, back_near_ref, back_far_ref, act_ref, grad_ref, mid_ref
):
    half = near_ref.shape[0]
    width = act_ref.shape[1]
    tile = 512
    total = [None, None]
    for first in range(0, width, tile):
        gate_cols = slice(first, first + tile)
        up_cols = slice(width + first, width + first + tile)

        def product(left_ref, near, far, cols):
            return dot_nn(left_ref[:, :half], near[:, cols]) + dot_nn(
                left_ref[:, half:], far[:, cols]
            )

        gate = product(normed_ref, near_ref, far_ref, gate_cols)
        up = product(normed_ref, near_ref, far_ref, up_cols)
        d_act = product(cot_ref, back_near_ref, back_far_ref, gate_cols)
        sigma = jax.nn.sigmoid(gate)
        silu = gate * sigma
        act_ref[:, gate_cols] = (silu * up).astype(BF)
        d_gate = (d_act * up * sigma * (1.0 + gate * (1.0 - sigma))).astype(BF)
        d_up = (d_act * silu).astype(BF)
        grad_ref[:, gate_cols] = d_gate
        grad_ref[:, up_cols] = d_up
        for i, ref in enumerate((near_ref, far_ref)):
            part = dot_nt(d_gate, ref[:, gate_cols]) + dot_nt(d_up, ref[:, up_cols])
            total[i] = part if total[i] is None else total[i] + part
    mid_ref[:, :half] = total[0].astype(BF)
    mid_ref[:, half:] = total[1].astype(BF)


def project_kernel(rows_ref, near_ref, far_ref, *outs):
    half = near_ref.shape[0]
    first = 0
    for out_ref in outs:
        cols = slice(first, first + out_ref.shape[1])
        out_ref[...] = dot_nn(rows_ref[:, :half], near_ref[:, cols]) + dot_nn(
            rows_ref[:, half:], far_ref[:, cols]
        )
        first += out_ref.shape[1]


def turn_back_kernel(rows_ref, near_ref, far_ref, out_ref):
    half = near_ref.shape[0]
    out_ref[...] = (
        dot_nn(rows_ref[:, :half], near_ref[...]) + dot_nn(rows_ref[:, half:], far_ref[...])
    ).astype(BF)


def unproject_kernel(count, *refs):
    out_ref = refs[-1]
    half = refs[count].shape[0]
    for side in range(2):
        total = None
        for i in range(count):
            part = dot_nt(refs[i][...], refs[count + 2 * i + side][...])
            total = part if total is None else total + part
        out_ref[:, side * half : (side + 1) * half] = total.astype(BF)


VMEM_BYTES = 48 * 1024 * 1024


def column_block(rows, width, index):
    return pl.BlockSpec((rows, width), lambda i: (0, index))


def whole_block(shape):
    zeros = (0,) * len(shape)
    return pl.BlockSpec(shape, lambda i: zeros)


def single_step(kernel, in_specs, outs, scratch=(), flops=1024):
    return pl.pallas_call(
        kernel,
        grid=(1,),
        in_specs=in_specs,
        out_specs=[whole_block(o.shape) for o in outs],
        out_shape=outs,
        scratch_shapes=list(scratch),
        compiler_params=pltpu.CompilerParams(vmem_limit_bytes=VMEM_BYTES),
        cost_estimate=pl.CostEstimate(flops=flops, bytes_accessed=1024, transcendentals=0),
    )


def attention_specs(rows, width, gate_width):
    return [
        column_block(rows, width, gate_width // width),
        column_block(rows, LANES, (gate_width + width) // LANES),
        whole_block((rows, LANES)),
        whole_block((rows, LANES)),
        whole_block((rows, 1)),
        whole_block((1, rows)),
    ]


def attention_fwd(y_a, width, gate_width, cos, sin, segc, segr):
    rows = y_a.shape[0]
    return single_step(
        attention_fwd_kernel,
        attention_specs(rows, width, gate_width),
        [jax.ShapeDtypeStruct((rows, width), BF)],
    )(y_a, y_a, cos, sin, segc, segr)[0]


def attention_bwd(y_a, width, gate_width, cos, sin, segc, segr, d_attn):
    rows = y_a.shape[0]
    return single_step(
        attention_bwd_kernel,
        attention_specs(rows, width, gate_width) + [whole_block((rows, width))],
        [jax.ShapeDtypeStruct((rows, width + LANES), BF)],
        [pltpu.VMEM((rows, LANES), F32), pltpu.VMEM((rows, LANES), F32)],
    )(y_a, y_a, cos, sin, segc, segr, d_attn)[0]


def scan_specs(rows, width):
    return [
        column_block(rows, width, 0),
        column_block(rows, 2 * LANES, width // (2 * LANES)),
        column_block(rows, LANES, (width + 2 * LANES) // LANES),
        whole_block((8, width)),
        whole_block((8, 2 * LANES)),
        whole_block((8, LANES)),
        whole_block((1, width)),
        whole_block((rows, 1)),
        whole_block((1, rows)),
        whole_block((rows, 1)),
    ]


def scan_fwd(y_b, width, taps_x, taps_bc, heads, skip, segc, segr, position):
    rows = y_b.shape[0]
    return single_step(
        scan_fwd_kernel,
        scan_specs(rows, width),
        [
            jax.ShapeDtypeStruct((rows, width), F32),
            jax.ShapeDtypeStruct((rows // BLK, LANES, width), BF),
        ],
    )(y_b, y_b, y_b, taps_x, taps_bc, heads, skip, segc, segr, position)


def scan_bwd(y_b, width, taps_x, taps_bc, heads, skip, segc, segr, position, states, d_out):
    rows = y_b.shape[0]
    return single_step(
        scan_bwd_kernel,
        scan_specs(rows, width)
        + [whole_block(states.shape), whole_block((rows, width))],
        [
            jax.ShapeDtypeStruct(y_b.shape, BF),
            jax.ShapeDtypeStruct((8, width), F32),
            jax.ShapeDtypeStruct((8, 2 * LANES), F32),
            jax.ShapeDtypeStruct((8, LANES), F32),
        ],
        [pltpu.VMEM((rows, width), F32), pltpu.VMEM((rows, 2 * LANES), F32)],
    )(y_b, y_b, y_b, taps_x, taps_bc, heads, skip, segc, segr, position, states, d_out)


def pick_rows(spots, parts):
    operands = (spots[:, None],) + tuple(parts)
    return single_step(
        pick_kernel,
        [whole_block(v.shape) for v in operands],
        [jax.ShapeDtypeStruct((spots.shape[0], parts[0].shape[1]), BF)],
    )(*operands)[0]


def pick_turned(spots, perm, parts):
    operands = (spots[:, None], perm) + tuple(parts)
    return single_step(
        pick_turn_kernel,
        [whole_block(v.shape) for v in operands],
        [jax.ShapeDtypeStruct((spots.shape[0], perm.shape[1]), BF)],
    )(*operands)[0]


def pick_normed(spots, perm, gain, parts):
    rows = spots.shape[0]
    operands = (spots[:, None], perm, gain) + tuple(parts)
    wide = jax.ShapeDtypeStruct((rows, perm.shape[1]), BF)
    return single_step(
        pick_norm_kernel,
        [whole_block(v.shape) for v in operands],
        [wide, wide, jax.ShapeDtypeStruct((rows, 1), F32)],
    )(*operands)


def join_blocks(operands, specs, width):
    rows = sum(spec.block_shape[0] for spec in specs)
    return single_step(join_kernel, specs, [jax.ShapeDtypeStruct((rows, width), BF)])(*operands)[0]


def ffn_both_ways(normed, cot_rows, near, far, back_near, back_far, width, back_index):
    rows, model_width = normed.shape
    half = near.shape[0]
    return single_step(
        ffn_kernel,
        [whole_block(normed.shape), whole_block(cot_rows.shape)]
        + [whole_block(near.shape), whole_block(far.shape)]
        + [column_block(half, width, back_index), column_block(half, width, back_index)],
        [
            jax.ShapeDtypeStruct((rows, width), BF),
            jax.ShapeDtypeStruct((rows, 2 * width), BF),
            jax.ShapeDtypeStruct((rows, model_width), BF),
        ],
    )(normed, cot_rows, near, far, back_near, back_far)


def project(rows, near, far, width):
    count = near.shape[1] // width
    shape = jax.ShapeDtypeStruct((rows.shape[0], width), F32)
    operands = (rows, near, far)
    return single_step(
        project_kernel, [whole_block(v.shape) for v in operands], [shape] * count
    )(*operands)


def turn_back(rows, near, far, width):
    half = near.shape[0]
    return single_step(
        turn_back_kernel,
        [whole_block(rows.shape), column_block(half, width, 0), column_block(half, width, 0)],
        [jax.ShapeDtypeStruct((rows.shape[0], width), BF)],
    )(rows, near, far)[0]


def unproject(lefts, blocks):
    specs = [whole_block(v.shape) for v in lefts]
    operands = list(lefts)
    for left, (near, far, index) in zip(lefts, blocks):
        specs += [column_block(near.shape[0], left.shape[1], index)] * 2
        operands += [near, far]
    rows, half = lefts[0].shape[0], blocks[0][0].shape[0]
    return single_step(
        functools.partial(unproject_kernel, len(lefts)),
        specs,
        [jax.ShapeDtypeStruct((rows, 2 * half), BF)],
    )(*operands)[0]


def join_tail(near, far, piece):
    rows = near.shape[0] + far.shape[0] - piece
    return single_step(
        functools.partial(join_tail_kernel, piece),
        [whole_block(near.shape), whole_block(far.shape)],
        [jax.ShapeDtypeStruct((rows, near.shape[1]), BF)],
    )(near, far)[0]


def grad_product(pairs, side):
    half = pairs[0][0].shape[1] // 2
    specs, operands = [], []
    for left, right in pairs:
        specs += [column_block(left.shape[0], half, side), whole_block(right.shape)]
        operands += [left, right]
    width = sum(right.shape[1] for left, right in pairs)
    return single_step(grad_kernel, specs, [jax.ShapeDtypeStruct((half, width), BF)])(*operands)[0]


def finish(kernel, index, operands, shapes):
    return single_step(
        kernel,
        [pl.BlockSpec(memory_space=pltpu.SMEM)] + [whole_block(v.shape) for v in operands],
        [jax.ShapeDtypeStruct(shape, F32) for shape in shapes],
    )(index.astype(jnp.int32).reshape(1), *operands)


def finish_late(index, own, other, width):
    rows = 2 * own.shape[0]
    shapes = [(rows, 2, width), (own.shape[1] - 2 * width, rows)]
    return finish(finish_late_kernel, index, (own, other), shapes)


def finish_out(index, own, other, query_width, scan_width):
    rows = 2 * own.shape[0]
    shapes = [(query_width, rows), (scan_width, rows)]
    shapes += [(rows, scan_width), (rows, query_width), (rows, LANES)]
    return finish(finish_out_kernel, index, (own, other), shapes)


def finish_scan(index, own, other, grad_z, bc_width):
    rows, scan_width = grad_z.shape
    shapes = [(rows, 2, scan_width), (rows, bc_width), (rows, LANES)]
    return finish(finish_scan_kernel, index, (own, other, grad_z), shapes)


CORE_SWAP = [(0, 1), (1, 0), (2, 3), (3, 2)]
CHIP_SWAP = [(0, 2), (2, 0), (1, 3), (3, 1)]
PAIR_SWAP = [(0, 1), (1, 0)]
def core_swap(v):
    return lax.ppermute(v, "ctx", CORE_SWAP)


def chip_swap(v):
    return lax.ppermute(v, "ctx", CHIP_SWAP)


def pair_swap(v):
    return lax.ppermute(v, "tp", PAIR_SWAP)


def shard_swap(v, gap):
    size = lax.axis_size("fsdp")
    return lax.ppermute(v, "fsdp", [(i, i ^ gap) for i in range(size)])


def quarter_perm(width):
    size = lax.axis_size("fsdp")
    shard = width // size
    piece = shard // 4
    spots = jnp.arange(width, dtype=jnp.int32)
    slot = spots // (size * piece)
    turn = (spots // piece) % size
    within = spots % piece
    quarter = jnp.where(slot == 1, 2, jnp.where(slot == 2, 1, slot)) ^ lax.axis_index("ctx")
    owner = lax.axis_index("fsdp") ^ turn
    column = owner * shard + quarter * piece + within
    return (spots[:, None] == column[None, :]).astype(BF)


def after(v, *others):
    return lax.optimization_barrier((v,) + others)[0]


def own_quarters(shard, sideways=False):
    index = lax.axis_index("ctx")
    if sideways:
        count = shard.shape[1]
        piece = count // 4
        place = jnp.arange(2 * piece, dtype=jnp.int32)
        column = (index ^ (2 * (place // piece))) * piece + place % piece
        chosen = (jnp.arange(count, dtype=jnp.int32)[None, :] == column[:, None]).astype(BF)
        both = dot_nt(chosen, shard).astype(BF)
        return both[:piece], both[piece:]
    piece = shard.shape[0] // 4
    return tuple(
        lax.dynamic_slice_in_dim(shard, (index ^ gap) * piece, piece, 0) for gap in (0, 2)
    )


def stage(*values):
    return lax.optimization_barrier(values)


def gather_near(own):
    line, gap = own, 1
    while 2 * gap < lax.axis_size("fsdp"):
        line = jnp.concatenate([line, shard_swap(line, gap)], axis=0)
        gap *= 2
    return line


def gather_far(near):
    return shard_swap(near, lax.axis_size("fsdp") // 2)


def swap_line(near, far):
    return chip_swap(join_tail(near, far, near.shape[0] * 2 // lax.axis_size("fsdp")))


def join_half(*parts):
    specs = [whole_block(v.shape) for v in parts]
    return join_blocks(parts, specs, parts[0].shape[1])


def order_shards(rows):
    owner = jnp.arange(rows.shape[0], dtype=jnp.int32)
    turn = lax.axis_index("fsdp") ^ owner
    return dot_nn((turn[:, None] == owner[None, :]).astype(BF), rows)


def add_low(left, right):
    return (left.astype(F32) + right.astype(F32)).astype(BF)


def halves(v):
    half = v.shape[0] // 2
    return v[:half], v[half:]


def direct_near(rows):
    near = [rows, chip_swap(rows), pair_swap(rows)]
    return near + [lax.ppermute(rows, ("ctx", "tp"), [(i, i ^ 5) for i in range(8)])]


def stack_spot(spot, rows):
    member = spot // rows
    gap = (member // 2) ^ lax.axis_index("ctx")
    turn = (member % 2) ^ lax.axis_index("tp")
    return ((gap & 1) * 4 + turn * 2 + (gap >> 1)) * rows + spot % rows


def dealt_order(lengths, dealing):
    numbers = jnp.arange(lengths.shape[0], dtype=jnp.int32)
    given_start = jnp.cumsum(lengths, dtype=jnp.int32) - lengths
    chosen = (dealing[:, None] == numbers[None, :]).astype(jnp.int32)
    dealt_len = jnp.sum(chosen * lengths[None, :], axis=1, dtype=jnp.int32)
    dealt_from = jnp.sum(chosen * given_start[None, :], axis=1, dtype=jnp.int32)
    dealt_start = jnp.cumsum(dealt_len, dtype=jnp.int32) - dealt_len
    return dealt_len, dealt_from, dealt_start


def look_up(spots, starts, counts, *tables):
    inside = (
        (spots[:, None] >= starts[None, :]) & (spots[:, None] < (starts + counts)[None, :])
    ).astype(jnp.int32)
    return [jnp.sum(inside * table[None, :], axis=1, dtype=jnp.int32) for table in tables]


def norm_back(grad_out, unit_rows, inverse, gain):
    scaled = grad_out * gain
    return inverse * (scaled - unit_rows * jnp.mean(scaled * unit_rows, axis=1, keepdims=True))


def inverse_norm(rows):
    return lax.rsqrt(jnp.mean(rows * rows, axis=1, keepdims=True) + EPSILON)


def padded(v, rows, cols):
    return jnp.pad(v, ((0, rows - v.shape[0]), (0, cols - v.shape[1])))


def per_device(
    tokens,
    cotangent,
    lengths,
    dealing,
    norm_in,
    w_query,
    w_keyval,
    w_attn_out,
    w_zx,
    w_bc,
    w_step,
    head_params,
    taps_x,
    taps_bc,
    gain_mamba,
    w_mamba_out,
    norm_mid,
    w_gate_up,
    w_down,
):
    tok_rows, model_width = tokens.shape
    tp_size = lax.axis_size("tp")
    fsdp_size = lax.axis_size("fsdp")
    rank_rows = tok_rows * tp_size
    tp_index = lax.axis_index("tp")
    fsdp_index = lax.axis_index("fsdp")
    ctx_index = lax.axis_index("ctx")
    shard = w_query.shape[0]
    heads = head_params.shape[1]
    scan_width = heads * HD
    query_width = w_query.shape[1]
    bc_width = w_bc.shape[1]
    ffn_width = w_gate_up.shape[2]
    own_start = tp_index * tok_rows
    peer_start = (tp_size - 1) * tok_rows - own_start

    dealt_len, dealt_from, dealt_start = dealt_order(lengths[0], dealing[0])
    numbers = jnp.arange(lengths.shape[1], dtype=jnp.int32)
    spots = ctx_index * rank_rows + jnp.arange(rank_rows, dtype=jnp.int32)
    segment, begins, anchor = look_up(
        spots, dealt_start, dealt_len, numbers, dealt_start, dealt_from
    )
    position = spots - begins
    sources = stack_spot(anchor + position, tok_rows)
    home = (ctx_index * tp_size + tp_index) * tok_rows + jnp.arange(tok_rows, dtype=jnp.int32)
    home_dealt, home_given = look_up(home, dealt_from, dealt_len, dealt_start, dealt_from)
    home_spots = stack_spot(home - home_given + home_dealt, tok_rows)
    segc, segr, posc = segment[:, None], segment[None, :], position[:, None]
    half_width = HD // 2
    freqs = ROPE_BASE ** (-jnp.arange(half_width, dtype=jnp.float32) / half_width)
    angles = position.astype(jnp.float32)[:, None] * freqs[None, :]
    cosine, sine = jnp.cos(angles), jnp.sin(angles)
    cos_table = jnp.concatenate([cosine] * 4, axis=1)
    sin_table = jnp.concatenate([-sine, sine, -sine, sine], axis=1)
    perm = lax.optimization_barrier(quarter_perm(model_width))

    small = (norm_in, norm_mid, taps_x, taps_bc, gain_mamba)
    small_sizes = [v.size for v in small]
    piece = shard // 4
    small = jnp.concatenate([v.reshape(-1) for v in small]).reshape(piece, -1)
    small_width = small.shape[1]
    free = LANES - heads - small_width
    wide = scan_width + 2 * LANES + LANES

    def in_quarter(gap):
        def rows_of(v):
            return lax.dynamic_slice_in_dim(v, (ctx_index ^ gap) * piece, piece, 0)

        zx = rows_of(w_zx)
        parts = [zx[:, 1, :], rows_of(w_bc), rows_of(w_step), small]
        parts += [jnp.zeros((piece, free), BF), zx[:, 0, :], rows_of(w_query)]
        return jnp.concatenate(parts + [rows_of(w_keyval).reshape(piece, -1)], axis=1)

    in_own, in_twin = in_quarter(0), in_quarter(2)
    token_near = direct_near(tokens)
    in_near = gather_near(in_own)
    in_far = gather_far(in_near)
    q_out = own_quarters(jnp.concatenate([w_attn_out, w_mamba_out], axis=0), True)
    q_back = own_quarters(w_down, True)
    q_late = [jnp.concatenate([q_out[i], q_back[i]], axis=1) for i in range(2)]
    late_near = gather_near(q_late[0])
    q_ffn = own_quarters(w_gate_up.reshape(shard, -1))
    places = (sources, home_spots, segc, segr, posc, cos_table, sin_table, perm)
    token_stack = token_near + [core_swap(v) for v in token_near]
    places, token_stack, cotangent, in_near, in_far, in_twin, late_near, q_ffn, late_twin = stage(
        places, token_stack, cotangent, in_near, in_far, in_twin, late_near, q_ffn, q_late[1]
    )
    sources, home_spots, segc, segr, posc, cos_table, sin_table, perm = places

    in_across = swap_line(in_near, in_far)
    ffn_near = gather_near(q_ffn[0])
    cot_pair = jnp.concatenate([cotangent, chip_swap(cotangent)], axis=0)
    late_far = gather_far(late_near)
    small_cols = slice(wide - LANES + heads, wide - free)
    small = jnp.concatenate([in_near[:, small_cols], in_far[:, small_cols]], axis=0)
    small = order_shards(small.reshape(fsdp_size, -1))
    ends = [sum(small_sizes[: i + 1]) for i in range(len(small_sizes))]
    smalls = [small[:, end - size : end] for end, size in zip(ends, small_sizes)]
    gains = jnp.stack([smalls[0].reshape(-1), smalls[1].reshape(-1)], axis=0).astype(BF)
    gains = dot_nn(gains, perm)
    gain_in, gain_mid = gains[0:1], gains[1:2]
    taps_one = smalls[2].reshape((fsdp_size,) + taps_x.shape).transpose(1, 2, 0, 3)
    taps_one = padded(taps_one.reshape(taps_x.shape[0], -1), 8, scan_width)
    taps_two = smalls[3].reshape((fsdp_size,) + taps_bc.shape).transpose(1, 0, 2)
    taps_two = padded(taps_two.reshape(taps_bc.shape[0], -1), 8, bc_width)
    gain_flat = smalls[4].reshape((fsdp_size,) + gain_mamba.shape).transpose(1, 0, 2)
    gain_flat = gain_flat.reshape(1, -1)
    heads_pad = padded(head_params, 8, LANES)
    skip = jnp.repeat(head_params[2], HD)[None, :]

    scan_args = (taps_one, taps_two, heads_pad, skip, segc, segr, posc)
    x_low, normed_in, inverse_in = pick_normed(sources, perm, gain_in, token_stack)
    in_across, normed_in, gain_mid, gain_flat, scan_args, late_far, cot_pair, ffn_near = stage(
        in_across, normed_in, gain_mid, gain_flat, scan_args, late_far, cot_pair, ffn_near
    )

    cot_near = [cot_pair, pair_swap(cot_pair)]
    in_half = join_half(in_near, in_far, in_twin, in_across)
    in_other = core_swap(in_half)
    late_across = swap_line(late_near, late_far)
    ffn_far = gather_far(ffn_near)
    y_scan, y_gate = project(normed_in, in_half, in_other, wide)
    scan_out, states = scan_fwd(y_scan, scan_width, *scan_args)
    attn_args = (query_width, scan_width, cos_table, sin_table, segc, segr)
    attn_rows = attention_fwd(y_gate, *attn_args)
    scan_out, attn_rows, late_across, ffn_far, cot_near = stage(
        scan_out, attn_rows, late_across, ffn_far, cot_near
    )

    ffn_operand = join_tail(ffn_near, ffn_far, 2 * ffn_near.shape[0] // fsdp_size)
    ffn_across = chip_swap(ffn_operand)
    late_half = join_half(late_near, late_far, late_twin, after(late_across, ffn_operand))
    late_rest = core_swap(late_half)
    out_width = query_width + scan_width
    gate_in = y_gate[:, :scan_width]
    sigma_in = jax.nn.sigmoid(gate_in)
    gated = scan_out * gate_in * sigma_in
    square_sum = jnp.sum(gated * gated, axis=1)
    square_sum = (square_sum + pair_swap(square_sum))[:, None]
    channels = scan_width * tp_size
    inverse_gate = lax.rsqrt(square_sum / channels + EPSILON)
    unit_gate = gated * inverse_gate
    mamba_rows = (unit_gate * gain_flat).astype(BF)
    branch_rows = jnp.concatenate([attn_rows, mamba_rows], axis=1)
    mixer = unproject([branch_rows], [(late_half, late_rest, 0)])
    mixer_half, mixer_rest = (pair_swap(v) for v in halves(mixer))
    ffn_half = join_half(ffn_near, ffn_far, q_ffn[1], after(ffn_across, mixer_half))
    ffn_other = core_swap(ffn_half)
    cot_stack = cot_near + [core_swap(v) for v in cot_near]
    cot_rows = pick_turned(sources, perm, after(cot_stack, mixer))
    mixer, mixer_half, mixer_rest, ffn_other, cot_rows = stage(
        mixer, mixer_half, mixer_rest, ffn_other, cot_rows
    )
    mixer_peer = jnp.concatenate([mixer_half, mixer_rest], axis=0)
    hidden = x_low.astype(F32) + (mixer.astype(F32) + mixer_peer.astype(F32))

    inverse_mid = inverse_norm(hidden)
    unit_mid = hidden * inverse_mid
    normed_mid = (unit_mid * gain_mid).astype(BF)
    activated, d_gate_up, d_mid = ffn_both_ways(
        normed_mid, cot_rows, ffn_half, ffn_other, late_half, late_rest, ffn_width, 1
    )

    d_mid_peer = pair_swap(d_mid)
    late_pairs = [(normed_mid, d_gate_up), (cot_rows, activated)]
    late_other = core_swap(grad_product(late_pairs, 1))
    late_grad = grad_product(late_pairs, 0)
    quarter_rows = fsdp_size * piece
    far_sum = add_low(late_grad[quarter_rows:], late_other[quarter_rows:])
    far_recv = chip_swap(far_sum)
    ffn_part = unproject([after(activated, d_mid_peer)], [(late_half, late_rest, 1)])
    d_mid, d_mid_peer, late_grad, late_other, far_sum, ffn_part = stage(
        d_mid, d_mid_peer, late_grad, late_other, far_sum, ffn_part
    )
    near_sum = add_low(late_grad[:quarter_rows], late_other[:quarter_rows])
    d_mid = d_mid.astype(F32) + d_mid_peer.astype(F32)

    ffn_own = lax.dynamic_slice_in_dim(ffn_part, own_start, tok_rows, 0).astype(F32)
    ffn_peer = pair_swap(lax.dynamic_slice_in_dim(ffn_part, peer_start, tok_rows, 0))
    d_hidden = cot_rows.astype(F32) + norm_back(d_mid, unit_mid, inverse_mid, gain_mid)
    g_norm_mid = jnp.sum(d_mid * unit_mid, axis=0, keepdims=True)
    d_mix = d_hidden.astype(BF)
    d_branch = turn_back(d_mix, late_half, late_rest, out_width)
    d_attn = d_branch[:, :query_width]
    d_mamba = d_branch[:, query_width:].astype(F32)
    scaled_gate = d_mamba * gain_flat
    gate_stat = jnp.sum(scaled_gate * unit_gate, axis=1)
    gate_stat = (gate_stat + pair_swap(gate_stat))[:, None]
    d_query = attention_bwd(y_gate, *attn_args, d_attn)
    g_gain = jnp.sum(d_mamba * unit_gate, axis=0, keepdims=True)
    gate_stat, d_query, far_recv = stage(gate_stat, d_query, far_recv)
    d_gated = inverse_gate * (scaled_gate - unit_gate * (gate_stat / channels))
    d_scan = d_gated * gate_in * sigma_in
    d_z = d_gated * scan_out * sigma_in * (1.0 + gate_in * (1.0 - sigma_in))
    dy_gate = jnp.concatenate([d_z.astype(BF), d_query], axis=1)
    out_pairs = [(d_mix, branch_rows), (normed_in, dy_gate)]
    out_other = core_swap(grad_product(out_pairs, 1))
    out_keep, out_far = halves(add_low(grad_product(out_pairs, 0), out_other))
    late_sum, late_send = halves(add_low(near_sum, far_recv))
    d_scan, late_sum, late_send, out_keep, out_far = stage(
        d_scan, late_sum, late_send, out_keep, out_far
    )
    out_far = chip_swap(out_far)
    late_recv = shard_swap(late_send, fsdp_size // 2)
    dy_scan, g_taps_one, g_taps_two, g_heads = scan_bwd(
        y_scan, scan_width, *scan_args, states, d_scan
    )
    hidden_own = lax.dynamic_slice_in_dim(hidden, own_start, tok_rows, 0)
    out_own = (hidden_own + ffn_own + after(ffn_peer, dy_scan).astype(F32)).astype(BF)
    out_own = dot_nt(out_own, perm).astype(BF)
    bc_cols = slice(scan_width, scan_width + bc_width)
    d_bc_peer = pair_swap(dy_scan[:, bc_cols])
    dy_scan, dy_gate, d_bc_peer, out_far, out_keep, out_own, late_recv = stage(
        dy_scan, dy_gate, d_bc_peer, out_far, out_keep, out_own, late_recv
    )

    out_keep, out_far = halves(add_low(out_keep, out_far))
    dy_gate, out_keep, out_far = stage(dy_gate, out_keep, out_far)
    out_far = shard_swap(out_far, fsdp_size // 2)
    d_in = unproject([dy_scan, dy_gate], [(in_half, in_other, 0), (in_half, in_other, 1)])
    d_in_peer = pair_swap(lax.dynamic_slice_in_dim(d_in, peer_start, tok_rows, 0))
    d_bc = add_low(dy_scan[:, bc_cols], d_bc_peer)
    dy_full = jnp.concatenate(
        [dy_scan[:, :scan_width], d_bc, dy_scan[:, scan_width + bc_width :]], axis=1
    )
    out_across = chip_swap(out_own)
    out_pair = jnp.concatenate([out_own, out_across], axis=0)
    late_keep, late_send = halves(add_low(late_sum, late_recv))
    late_recv = shard_swap(late_send, fsdp_size // 4)
    in_pairs = [(normed_in, after(dy_full, d_in_peer, out_far, late_recv, out_across))]
    in_other = core_swap(grad_product(in_pairs, 1))
    in_keep, in_far = halves(add_low(grad_product(in_pairs, 0), in_other))
    in_keep, in_far, d_in, d_in_peer, out_keep, out_far, out_pair, late_keep, late_recv = stage(
        in_keep, in_far, d_in, d_in_peer, out_keep, out_far, out_pair, late_keep, late_recv
    )

    def own_rows(v):
        return lax.dynamic_slice_in_dim(v, own_start, tok_rows, 0)

    d_in_own = own_rows(d_in).astype(F32) + d_in_peer.astype(F32)
    unit_own = own_rows(x_low).astype(F32) * own_rows(inverse_in)
    grad_own = own_rows(d_hidden) + norm_back(d_in_own, unit_own, own_rows(inverse_in), gain_in)
    g_norm_in = jnp.sum(d_in_own * unit_own, axis=0, keepdims=True)
    grad_own = dot_nt(grad_own.astype(BF), perm).astype(BF)
    in_recv = chip_swap(in_far)
    out_near = [out_pair, pair_swap(out_pair)]
    grad_pair = jnp.concatenate([grad_own, chip_swap(grad_own)], axis=0)
    def shards_sum(keep, far, gap):
        total = add_low(keep, far)
        while gap > 1:
            gap //= 2
            keep, far = halves(total)
            total = add_low(keep, shard_swap(far, gap))
        return total

    late_sum = shards_sum(late_keep, late_recv, fsdp_size // 4)
    out_sum = shards_sum(out_keep, out_far, fsdp_size // 2)
    grad_pair, in_keep, in_recv, late_sum, out_sum, out_near, g_norm_in = stage(
        grad_pair, in_keep, in_recv, late_sum, out_sum, out_near, g_norm_in
    )

    in_keep, in_far = halves(add_low(in_keep, in_recv))
    in_recv = shard_swap(in_far, fsdp_size // 2)
    grad_near = [grad_pair, pair_swap(grad_pair)]
    out_twin, late_twin = chip_swap(out_sum), chip_swap(late_sum)
    mixed_home = pick_rows(home_spots, out_near + [core_swap(v) for v in out_near])
    in_keep, in_recv, out_twin, late_twin, mixed_home = stage(
        in_keep, in_recv, out_twin, late_twin, mixed_home
    )

    out_sums = join_half(out_sum, out_twin)
    late_sums = join_half(late_sum, late_twin)
    in_sum = shards_sum(in_keep, in_recv, fsdp_size // 2)
    out_others, late_others = core_swap(out_sums), core_swap(late_sums)
    g_norms = dot_nt(
        jnp.concatenate([g_norm_in, g_norm_mid], axis=0), perm.astype(F32), PRECISE
    )
    g_norms, g_taps_two = g_norms.reshape(-1), g_taps_two[: taps_bc.shape[0]].reshape(-1)
    g_taps_one = g_taps_one[: taps_x.shape[0]].reshape(-1)
    g_heads = g_heads[:3, :heads].reshape(-1)
    g_gain = g_gain.reshape(-1)
    parts = (g_norms[:model_width], g_taps_two, g_norms[model_width:], g_taps_one, g_heads, g_gain)
    paired = model_width + g_taps_two.shape[0]
    sums = jnp.concatenate(parts)
    sums = after(sums, in_recv)
    sums = sums + core_swap(sums)
    sums = sums + chip_swap(sums)
    in_sum, out_others, late_others, sums, grad_near = stage(
        in_sum, out_others, late_others, sums, grad_near
    )

    in_twin = chip_swap(in_sum)
    grad_near += [core_swap(v) for v in grad_near]
    grad_attn_out, grad_mamba_out, grad_z, grad_query, grad_keyval = finish_out(
        ctx_index, out_sums, out_others, query_width, scan_width
    )
    sums = sums + shard_swap(sums, 1)
    in_twin, grad_near, grad_z, sums = stage(in_twin, grad_near, grad_z, sums)
    in_sums = join_half(in_sum, in_twin)
    grad_home = pick_rows(home_spots, grad_near)
    grad_gate_up, grad_down = finish_late(ctx_index, late_sums, late_others, ffn_width)
    gap = 2
    while gap < fsdp_size:
        sums = sums + shard_swap(sums, gap)
        gap *= 2
    sums = jnp.concatenate([sums[:paired] + pair_swap(sums[:paired]), sums[paired:]])
    grad_zx, grad_bc, grad_step = finish_scan(
        ctx_index, in_sums, core_swap(in_sums), grad_z, bc_width
    )
    ends = [sum(v.size for v in parts[: i + 1]) for i in range(len(parts))]
    sum_in, sum_two, sum_mid, sum_one, sum_heads, sum_gain = [
        sums[end - v.size : end] for end, v in zip(ends, parts)
    ]

    def shard_of(array, dim_index):
        piece = array.shape[dim_index] // fsdp_size
        return lax.dynamic_slice_in_dim(array, fsdp_index * piece, piece, dim_index)

    return (
        mixed_home,
        grad_home,
        shard_of(sum_in, 0),
        grad_query,
        grad_keyval.reshape(w_keyval.shape),
        grad_attn_out,
        grad_zx,
        grad_bc,
        grad_step[:, : w_step.shape[1]],
        sum_heads.reshape(head_params.shape),
        shard_of(sum_one.reshape(taps_x.shape[0], heads, HD), 2),
        shard_of(sum_two.reshape(taps_bc.shape[0], -1), 1),
        shard_of(sum_gain.reshape(heads, HD), 1),
        grad_mamba_out,
        shard_of(sum_mid, 0),
        grad_gate_up,
        grad_down,
    )


def solution(mesh):
    rows = P(("fsdp", "ctx", "tp"), None)
    in_specs = (
        rows,
        rows,
        P("fsdp", None),
        P("fsdp", None),
        P("fsdp"),
        P("fsdp", "tp"),
        P("fsdp", "tp", None),
        P("tp", "fsdp"),
        P("fsdp", None, "tp"),
        P("fsdp", None),
        P("fsdp", "tp"),
        P(None, "tp"),
        P(None, "tp", "fsdp"),
        P(None, "fsdp"),
        P("tp", "fsdp"),
        P("tp", "fsdp"),
        P("fsdp"),
        P("fsdp", None, "tp"),
        P("tp", "fsdp"),
    )
    out_specs = (
        rows,
        rows,
        P("fsdp"),
        P("fsdp", "tp"),
        P("fsdp", "tp", None),
        P("tp", "fsdp"),
        P("fsdp", None, "tp"),
        P("fsdp", None),
        P("fsdp", "tp"),
        P(None, "tp"),
        P(None, "tp", "fsdp"),
        P(None, "fsdp"),
        P("tp", "fsdp"),
        P("tp", "fsdp"),
        P("fsdp"),
        P("fsdp", None, "tp"),
        P("tp", "fsdp"),
    )
    return jax.shard_map(
        per_device, mesh=mesh, in_specs=in_specs, out_specs=out_specs, check_vma=False
    )
```
